32 devices in a mesh: tm: 16 (over z, y, core), pb: 2 (over x).
Axes of the slice: x: 2, y: 2, z: 4, core: 2. Of those that a mesh axis runs over, the one named last changes fastest.
Arguments:
- queries: bfloat16 [4096, 768], P(('tm', 'pb')), may hold values from -64 to 64
- corpus: bfloat16 [262144, 768], P(('tm', 'pb')), may hold values from -40 to 40
- window_start: int32 [4096, 2], P(('tm', 'pb')), may hold values from 0 to 262142, as said below
- window_end: int32 [4096, 2], P(('tm', 'pb')), may hold values from 2 to 262144, as said below
Outputs:
- pooled: bfloat16 [4096, 2, 768], P(('tm', 'pb'))
- log_mass: float32 [4096, 2], P(('tm', 'pb'))
- mean_score: float32 [4096, 2], P(('tm', 'pb'))
The draws below stay inside these ranges and needn't reach their ends.
Inputs may be any that keep to these rules, and one draw needn't show every extreme that they name: `window_start`: for query q both windows are nonempty and lie within documents (q // 128 - 1) * 8192 to (q // 128 + 2) * 8192 - 1, that is the time block of q and the blocks just before and after it. window_end[q, w] > window_start[q, w], and window_end[q, w] <= (q // 128 + 2) * 8192.
All inputs are finite; a program needn't handle non-finite values.
Results may differ from the reference program's by a relative error of at most 0.0051.
Values may be sent and summed in bfloat16 or wider, within the bound.
No kernel may reach another device: no remote copies, remote signals or barrier semaphores. Data moves between devices by JAX's collectives and lax.ppermute only.
A program may use at most 128 MiB of HBM per device.

```python
import math
from functools import reduce
import jax
import jax.numpy as jnp
from jax import lax

D = 768
Q_DEV = 128
DOC_DEV = 8192
NQ = 4096
NDOC = 262144
N_TM = 16
N_PB = 2


def window_bounds(key):
    key_anchor, key_back, key_ahead = jax.random.split(jax.random.fold_in(key, 101), 3)
    owner_block = jnp.arange(NQ, dtype=jnp.int32) // Q_DEV
    anchor = owner_block * DOC_DEV + 2 * jax.random.randint(key_anchor, (NQ,), 0, DOC_DEV // 2) + 1
    behind = jax.random.randint(key_back, (NQ, 2), 1, DOC_DEV + 1)
    forward = jax.random.randint(key_ahead, (NQ, 2), 0, DOC_DEV + 1)
    first_doc = jnp.maximum(anchor[:, None] - behind, 0)
    stop_doc = jnp.minimum(anchor[:, None] + forward + 1, NDOC)
    return (first_doc.astype(jnp.int32), stop_doc.astype(jnp.int32))


def corpus_rows(key):
    key_base = jax.random.fold_in(jax.random.fold_in(key, 202), 0)
    values = jax.random.normal(key_base, (NDOC, D), jnp.float32)
    return jnp.clip(values, -40.0, 40.0)


def draw_corpus(key, part):
    return corpus_rows(key).astype(jnp.bfloat16)


def draw_queries(key, part):
    drawn = jax.random.normal(jax.random.fold_in(key, 303), (NQ, D), jnp.float32)
    return jnp.clip(drawn, -64.0, 64.0).astype(jnp.bfloat16)


def draw_window_start(key, part):
    first_doc, stop_doc = window_bounds(key)
    return first_doc


def draw_window_end(key, part):
    first_doc, stop_doc = window_bounds(key)
    return stop_doc


def setup_inputs(seed: int = 0) -> dict:
    keys = jax.random.split(jax.random.key(seed), 5)
    return {
        "queries": draw_queries(jax.random.fold_in(keys[4], 71), 0),
        "corpus": draw_corpus(jax.random.fold_in(keys[4], 71), 0),
        "window_start": draw_window_start(jax.random.fold_in(keys[4], 71), 0),
        "window_end": draw_window_end(jax.random.fold_in(keys[4], 71), 0),
    }


NEG_FILL = -1e+30
SCORE_SCALE = 3.0

def block_state(query_rows, first_doc, stop_doc, block, start_doc):
    scores = lax.dot_general(query_rows, block, (((1,), (1,)), ((), ())), preferred_element_type=jnp.float32)
    scores = scores * (SCORE_SCALE / math.sqrt(block.shape[1]))
    doc_index = start_doc + jnp.arange(block.shape[0], dtype=jnp.int32)
    maxima, totals, parts, score_sums, counts = ([], [], [], [], [])
    for window in range(2):
        inside = (doc_index[None, :] >= first_doc[:, window:window + 1]) & (doc_index[None, :] < stop_doc[:, window:window + 1])
        window_max = lax.optimization_barrier(jnp.max(jnp.where(inside, scores, NEG_FILL), axis=1))
        weights = jnp.where(inside, jnp.exp(scores - window_max[:, None]), 0.0)
        maxima.append(window_max)
        totals.append(lax.optimization_barrier(jnp.sum(weights, axis=1)))
        parts.append(jnp.dot(weights.astype(jnp.bfloat16), block, preferred_element_type=jnp.float32).astype(jnp.bfloat16))
        score_sums.append(lax.optimization_barrier(jnp.sum(jnp.where(inside, scores, 0.0), axis=1)))
        counts.append(lax.optimization_barrier(jnp.sum(inside.astype(jnp.float32), axis=1)))
    return (jnp.stack(maxima, 1), jnp.stack(totals, 1), jnp.stack(parts, 1), jnp.stack(score_sums, 1), jnp.stack(counts, 1))

def combine(states):
    tops = [jnp.where(member[4] > 0, member[0], NEG_FILL) for member in states]
    overall = reduce(jnp.maximum, tops)
    rescale = [jnp.exp(value - overall) for value in tops]
    denominator = reduce(jnp.add, [factor * member[1] for factor, member in zip(rescale, states)])
    weighted = reduce(jnp.add, [factor[..., None] * member[2].astype(jnp.float32) for factor, member in zip(rescale, states)])
    pooled = (weighted / denominator[..., None]).astype(jnp.bfloat16)
    log_mass = overall + jnp.log(denominator)
    mean_score = reduce(jnp.add, [member[3] for member in states]) / reduce(jnp.add, [member[4] for member in states])
    return (pooled, log_mass, mean_score)

def reference(queries, corpus, window_start, window_end):
    blocks = N_TM * N_PB
    feature_width = corpus.shape[1]
    padding = jnp.zeros((DOC_DEV, feature_width), corpus.dtype)
    padded = jnp.concatenate([padding, corpus, padding], axis=0)

    def per_owner(owner_block):
        query_rows = lax.dynamic_slice_in_dim(queries, owner_block * Q_DEV, Q_DEV, 0)
        first_doc = lax.dynamic_slice_in_dim(window_start, owner_block * Q_DEV, Q_DEV, 0)
        stop_doc = lax.dynamic_slice_in_dim(window_end, owner_block * Q_DEV, Q_DEV, 0)
        states = []
        for offset in (-1, 0, 1):
            block = lax.dynamic_slice_in_dim(padded, (owner_block + offset + 1) * DOC_DEV, DOC_DEV, 0)
            start_doc = ((owner_block + offset) * DOC_DEV).astype(jnp.int32)
            states.append(block_state(query_rows, first_doc, stop_doc, block, start_doc))
        return combine(states)
    pooled, log_mass, mean_score = lax.map(per_owner, jnp.arange(blocks, dtype=jnp.int32))
    return (pooled.reshape(blocks * Q_DEV, 2, feature_width), log_mass.reshape(blocks * Q_DEV, 2), mean_score.reshape(blocks * Q_DEV, 2))
```

```python
import functools
import math

import jax
import jax.numpy as jnp
from jax import lax
from jax.experimental import pallas as pl
from jax.experimental.pallas import tpu as pltpu
from jax.sharding import PartitionSpec as P

SCORE_SCALE = 3.0
NEG = -1e30
LOG2E = math.log2(math.e)
AXES = ("tm", "pb")
BF16 = jnp.bfloat16
F32 = jnp.float32
NT = (((1,), (1,)), ((), ()))
TN = (((0,), (0,)), ((), ()))
META = 16
LANES = 128
DOC_TILE = 1024
DOT_TILE = 256
ROW_TILE = 16

VMEM = pl.BlockSpec(memory_space=pltpu.VMEM)
SMEM = pl.BlockSpec(memory_space=pltpu.SMEM)


def params(mebibytes):
    return pltpu.CompilerParams(vmem_limit_bytes=mebibytes * 2**20)


def identity(n):
    rows = lax.broadcasted_iota(jnp.int32, (n, n), 0)
    return (rows == lax.broadcasted_iota(jnp.int32, (n, n), 1)).astype(BF16)


def split_int(value):
    return (value >> 8).astype(F32), (value & 255).astype(F32)


def split_float(value):
    high = value.astype(BF16).astype(F32)
    rest = value - high
    middle = rest.astype(BF16).astype(F32)
    return high, middle, rest - middle


def row_scratch(rows, docs, width, tile):
    return [
        pltpu.VMEM((rows, width), BF16),
        pltpu.VMEM((2, rows, LANES), jnp.int32),
        pltpu.VMEM((rows, LANES), F32),
        pltpu.VMEM((rows, LANES), F32),
        pltpu.VMEM((rows, LANES), F32),
        pltpu.VMEM((rows, tile), F32),
        pltpu.VMEM((rows, tile), F32),
        pltpu.VMEM((docs // tile, rows, tile), F32),
        pltpu.VMEM((rows, tile), BF16),
        pltpu.VMEM((rows, tile), BF16),
        pltpu.VMEM((rows, width), F32),
    ]


def attend_rows(docs, scratch):
    rows_q, bounds, peak, score_sum, mass, s_a, s_b, masked, p_a, p_b, acc = scratch
    n_docs, width = docs.shape
    rows, tile = s_a.shape
    tiles = n_docs // tile
    scale = SCORE_SCALE / math.sqrt(width)
    starts = range(0, rows, ROW_TILE)

    def share(part, parts):
        each = -(-len(starts) // parts)
        return starts[part * each : (part + 1) * each]

    def score(t, out, part):
        first = pl.multiple_of(t * tile + part * DOT_TILE, DOT_TILE)
        out[:, part * DOT_TILE : (part + 1) * DOT_TILE] = lax.dot_general(
            rows_q[...], docs[pl.ds(first, DOT_TILE), :], NT, preferred_element_type=F32
        )

    def scan(t, scores, some):
        for r in some:
            at = slice(r, r + ROW_TILE)
            offset = t * tile - bounds[0, at, :]
            length = bounds[1, at, :].astype(jnp.uint32)
            top, total = peak[at, :], score_sum[at, :]
            for c in range(0, tile, LANES):
                value = scores[at, c : c + LANES]
                inside = (offset + c).astype(jnp.uint32) < length
                kept = jnp.where(inside, value, NEG)
                top = jnp.maximum(top, kept)
                total = total + jnp.where(inside, value, 0.0)
                masked[t, at, c : c + LANES] = kept
            peak[at, :] = top
            score_sum[at, :] = total

    def score_and_scan(t_score, out, t_scan, scores):
        parts = tile // DOT_TILE
        for part in range(parts):
            score(t_score, out, part)
            scan(t_scan, scores, share(part, parts))

    peak[...] = jnp.full(peak.shape, NEG, F32)
    score_sum[...] = jnp.zeros(score_sum.shape, F32)
    mass[...] = jnp.zeros(mass.shape, F32)
    for part in range(tile // DOT_TILE):
        score(0, s_a, part)

    def first_step(i, carry):
        t = 2 * i
        score_and_scan(t + 1, s_b, t, s_a)
        score_and_scan(jnp.minimum(t + 2, tiles - 1), s_a, t + 1, s_b)
        return carry

    lax.fori_loop(0, tiles // 2, first_step, 0)
    top = jnp.max(peak[...], axis=1, keepdims=True)
    peak[...] = jnp.broadcast_to(jnp.maximum(top, 0.5 * NEG), peak.shape)
    acc[...] = jnp.zeros(acc.shape, F32)

    def weigh(t, out, some):
        for r in some:
            at = slice(r, r + ROW_TILE)
            shift, total = peak[at, :], mass[at, :]
            for c in range(0, tile, LANES):
                p = jnp.exp2((masked[t, at, c : c + LANES] - shift) * (scale * LOG2E))
                total = total + p
                out[at, c : c + LANES] = p.astype(BF16)
            mass[at, :] = total

    def pool(t, weights, part):
        at = slice(part * DOT_TILE, (part + 1) * DOT_TILE)
        block = docs[pl.ds(pl.multiple_of(t * tile, tile), tile), at]
        acc[:, at] += jnp.dot(weights[...], block, preferred_element_type=F32)

    def pool_and_weigh(t, weights, t_weigh, out):
        parts = width // DOT_TILE
        for part in range(parts):
            pool(t, weights, part)
            weigh(t_weigh, out, share(part, parts))

    weigh(0, p_a, starts)

    def second_step(i, carry):
        t = 2 * i + 1
        pool_and_weigh(t - 1, p_a, t, p_b)
        pool_and_weigh(t, p_b, t + 1, p_a)
        return carry

    lax.fori_loop(0, tiles // 2 - 1, second_step, 0)
    pool_and_weigh(tiles - 2, p_a, tiles - 1, p_b)
    for part in range(width // DOT_TILE):
        pool(tiles - 1, p_b, part)
    return (
        top * scale,
        jnp.sum(mass[...], axis=1, keepdims=True),
        jnp.sum(score_sum[...], axis=1, keepdims=True) * scale,
    )


def stats_matrix(stats):
    rows = stats[0].shape[0]
    lane = lax.broadcasted_iota(jnp.int32, (rows, META), 1)
    matrix = jnp.zeros((rows, META), F32)
    for k, value in enumerate(stats):
        for j, part in enumerate(split_float(value)):
            matrix = jnp.where(lane == 3 * k + j, part, matrix)
    return matrix.astype(BF16)


def set_bounds(bounds, at, low, length):
    shape = (low.shape[0], LANES)
    bounds[0, at, :] = low - lax.broadcasted_iota(jnp.int32, shape, 1)
    bounds[1, at, :] = jnp.broadcast_to(length, shape)


def own_kernel(shift, message, docs, out, *scratch):
    queries = message.shape[0] - META
    rows_q, bounds = scratch[:2]
    unit = identity(queries)
    columns = lax.dot_general(
        unit, message[queries:, 0:queries], NT, preferred_element_type=F32
    )

    def bound(k):
        value = columns[:, 2 * k : 2 * k + 1] * 256.0 + columns[:, 2 * k + 1 : 2 * k + 2]
        return jnp.clip(value.astype(jnp.int32) - shift[0], 0, docs.shape[0])

    for w in range(2):
        at = slice(w * queries, (w + 1) * queries)
        low = bound(w)
        set_bounds(bounds, at, low, jnp.maximum(bound(2 + w) - low, 0))
        rows_q[at, :] = message[0:queries, :]
    stats = stats_matrix(attend_rows(docs, scratch))
    out[0 : 2 * queries, :] = scratch[-1][...].astype(BF16)
    out[2 * queries :, :] = jnp.zeros((META, out.shape[1]), BF16)
    for w in range(2):
        at = slice(w * queries, (w + 1) * queries)
        out[2 * queries :, at] = lax.dot_general(
            stats[at, :], unit, TN, preferred_element_type=F32
        ).astype(BF16)


def own(shift, message, corpus):
    docs, width = corpus.shape
    queries = message.shape[0] - META
    tile = min(DOC_TILE, docs // 2)
    return pl.pallas_call(
        own_kernel,
        out_shape=jax.ShapeDtypeStruct((2 * queries + META, width), BF16),
        in_specs=[SMEM, VMEM, VMEM],
        out_specs=VMEM,
        scratch_shapes=row_scratch(2 * queries, docs, width, tile),
        compiler_params=params(20),
        cost_estimate=pl.CostEstimate(
            flops=8 * queries * docs * width,
            bytes_accessed=docs * width * 2,
            transcendentals=2 * queries * docs,
        ),
        name="own_block",
    )(shift, message, corpus)


def neighbour_kernel(shifts, near, far_a, far_b, docs, near_out, far_out, both_q, *scratch):
    queries = near.shape[0] - META
    rows_q, bounds = scratch[:2]
    group = rows_q.shape[0]
    both_q[0:queries, :] = near[0:queries, :]
    both_q[queries:, :] = far_a[0:queries, :] + far_b[0:queries, :]

    lows, lengths = [], []
    for side, meta in enumerate((near[queries:, 0:queries], far_a[queries:, 0:queries] + far_b[queries:, 0:queries])):
        meta = meta.astype(F32)

        def bound(k):
            value = meta[2 * k : 2 * k + 1, :] * 256.0 + meta[2 * k + 1 : 2 * k + 2, :]
            return jnp.clip(value.astype(jnp.int32) - shifts[side], 0, docs.shape[0])

        for w in range(2):
            low = bound(w)
            lows.append(low)
            lengths.append(jnp.maximum(bound(2 + w) - low, 0))
    blocks = len(lows)
    parts = []
    for low, length in zip(lows, lengths):
        rows = [*split_int(low), *split_int(length)]
        parts.append(jnp.concatenate(rows + [jnp.zeros((META - 4, queries), F32)], axis=0).astype(BF16))
    flags = [(length > 0).astype(F32) for length in lengths]
    stacked = jnp.concatenate(flags + [jnp.zeros((META - blocks, queries), F32)], axis=0).astype(BF16)
    before = lax.broadcasted_iota(jnp.int32, (queries, queries), 0) < lax.broadcasted_iota(
        jnp.int32, (queries, queries), 1
    )
    ranks = jnp.dot(stacked, before.astype(BF16), preferred_element_type=F32)
    places, first = [], jnp.zeros((1, 1), F32)
    for b in range(blocks):
        places.append(jnp.where(flags[b] > 0, ranks[b : b + 1, :] + first, -1.0).astype(jnp.int32))
        first = first + jnp.sum(flags[b], axis=1, keepdims=True)
    active = jnp.max(first).astype(jnp.int32)

    near_out[...] = jnp.zeros(near_out.shape, BF16)
    far_out[...] = jnp.zeros(far_out.shape, BF16)

    def work(g, carry):
        row = lax.broadcasted_iota(jnp.int32, (group, queries), 0) + g * group
        pick = [(row == place).astype(F32).astype(BF16) for place in places]
        of_query = jnp.concatenate([pick[0] + pick[1], pick[2] + pick[3]], axis=1)
        rows_q[...] = jnp.dot(of_query, both_q[...], preferred_element_type=F32).astype(BF16)
        columns = jnp.zeros((group, META), F32)
        for chosen, part in zip(pick, parts):
            columns = columns + lax.dot_general(chosen, part, NT, preferred_element_type=F32)
        low = (columns[:, 0:1] * 256.0 + columns[:, 1:2]).astype(jnp.int32)
        length = (columns[:, 2:3] * 256.0 + columns[:, 3:4]).astype(jnp.int32)
        set_bounds(bounds, slice(0, group), low, length)
        stats = stats_matrix(attend_rows(docs, scratch))
        pooled = scratch[-1][...].astype(BF16)
        for b, chosen in enumerate(pick):
            out = (near_out, far_out)[b // 2]
            at = slice((b % 2) * queries, (b % 2 + 1) * queries)
            out[at, :] += lax.dot_general(chosen, pooled, TN, preferred_element_type=F32).astype(BF16)
            out[2 * queries :, at] += lax.dot_general(
                stats, chosen, TN, preferred_element_type=F32
            ).astype(BF16)
        return carry

    lax.fori_loop(0, (active + group - 1) // group, work, 0)


def neighbours(shifts, near, far_a, far_b, corpus):
    docs, width = corpus.shape
    queries = near.shape[0] - META
    tile = min(DOC_TILE, docs // 2)
    group = min(4 * queries, (2 * queries + 3 * queries // 8) // ROW_TILE * ROW_TILE)
    result = jax.ShapeDtypeStruct((2 * queries + META, width), BF16)
    return pl.pallas_call(
        neighbour_kernel,
        out_shape=(result, result),
        in_specs=[SMEM, VMEM, VMEM, VMEM, VMEM],
        out_specs=(VMEM, VMEM),
        scratch_shapes=[pltpu.VMEM((2 * queries, width), BF16)] + row_scratch(group, docs, width, tile),
        compiler_params=params(24),
        cost_estimate=pl.CostEstimate(
            flops=8 * queries * docs * width,
            bytes_accessed=docs * width * 2,
            transcendentals=2 * queries * docs,
        ),
        name="neighbour_blocks",
    )(shifts, near, far_a, far_b, corpus)


def pack_kernel(queries, relative, out):
    rows, width = queries.shape
    out[0:rows, :] = queries[...]
    out[rows:, :] = jnp.zeros((META, width), BF16)
    high, low = split_int(relative[...])
    lines = [part[k : k + 1, :] for k in range(4) for part in (high, low)]
    lines.append(jnp.zeros((META - 8, rows), F32))
    out[rows:, 0:rows] = jnp.concatenate(lines, axis=0).astype(BF16)


def pack(queries, relative):
    rows, width = queries.shape
    return pl.pallas_call(
        pack_kernel,
        out_shape=jax.ShapeDtypeStruct((rows + META, width), BF16),
        in_specs=[VMEM, VMEM],
        out_specs=VMEM,
        name="pack",
    )(queries, relative)


def columns_of(state, unit, w):
    queries = unit.shape[0]
    lines = state[2 * queries :, w * queries : (w + 1) * queries]
    columns = lax.dot_general(unit, lines, NT, preferred_element_type=F32)
    top, total, score_sum = (
        columns[:, 3 * k : 3 * k + 1] + columns[:, 3 * k + 1 : 3 * k + 2] + columns[:, 3 * k + 2 : 3 * k + 3]
        for k in range(3)
    )
    return jnp.where(total > 0, top, NEG), total, score_sum


def weigh_states(tops):
    best = functools.reduce(jnp.maximum, tops)
    return best, [jnp.exp(top - best) for top in tops]


def merge_kernel(first, second, out):
    queries = (first.shape[0] - META) // 2
    unit = identity(queries)
    out[2 * queries :, :] = jnp.zeros((META, out.shape[1]), BF16)
    for w in range(2):
        at = slice(w * queries, (w + 1) * queries)
        states = [columns_of(state, unit, w) for state in (first, second)]
        best, factors = weigh_states([state[0] for state in states])
        total = functools.reduce(jnp.add, [f * state[1] for f, state in zip(factors, states)])
        score_sum = states[0][2] + states[1][2]
        out[at, :] = (
            factors[0] * first[at, :].astype(F32) + factors[1] * second[at, :].astype(F32)
        ).astype(BF16)
        stats = stats_matrix((best, total, score_sum))
        out[2 * queries :, at] = lax.dot_general(
            stats, unit, TN, preferred_element_type=F32
        ).astype(BF16)


def merge(first, second):
    return pl.pallas_call(
        merge_kernel,
        out_shape=jax.ShapeDtypeStruct(first.shape, BF16),
        in_specs=[VMEM, VMEM],
        out_specs=VMEM,
        name="merge",
    )(first, second)


def finish_kernel(window_start, window_end, first, second, third, pooled, log_mass, mean_score):
    queries = window_start.shape[1]
    unit = identity(queries)
    members = (first, second, third)
    for w in range(2):
        at = slice(w * queries, (w + 1) * queries)
        states = [columns_of(member, unit, w) for member in members]
        _, factors = weigh_states([state[0] for state in states])
        total = functools.reduce(jnp.add, [f * state[1] for f, state in zip(factors, states)])
        weighted = functools.reduce(
            jnp.add, [f * member[at, :].astype(F32) for f, member in zip(factors, members)]
        )
        pooled[at, :] = (weighted / total).astype(BF16)

        lines = [member[2 * queries :, at].astype(F32) for member in members]
        tops, totals, sums = (
            [line[3 * k : 3 * k + 1, :] + line[3 * k + 1 : 3 * k + 2, :] + line[3 * k + 2 : 3 * k + 3, :] for line in lines]
            for k in range(3)
        )
        best, factors = weigh_states([jnp.where(t > 0, top, NEG) for top, t in zip(tops, totals)])
        total = functools.reduce(jnp.add, [f * t for f, t in zip(factors, totals)])
        log_mass[w : w + 1, :] = best + jnp.log(total)
        count = (window_end[w : w + 1, :] - window_start[w : w + 1, :]).astype(F32)
        mean_score[w : w + 1, :] = functools.reduce(jnp.add, sums) / count


def finish(window_start, window_end, *members):
    queries = window_start.shape[1]
    width = members[0].shape[1]
    line = jax.ShapeDtypeStruct((2, queries), F32)
    return pl.pallas_call(
        finish_kernel,
        out_shape=(jax.ShapeDtypeStruct((2 * queries, width), BF16), line, line),
        in_specs=[VMEM] * 5,
        out_specs=(VMEM, VMEM, VMEM),
        name="finish",
    )(window_start, window_end, *members)


def local(queries, corpus, window_start, window_end):
    rows, width = queries.shape
    docs = corpus.shape[0]
    size = lax.axis_size(AXES)
    position = lax.axis_index(AXES)
    across = [(i, i ^ 1) for i in range(size)]
    between = [(i, i + 1) for i in range(3, size - 1, 4)] + [(i + 1, i) for i in range(3, size - 1, 4)]
    relay = [(i, i + 2) for i in range(0, size, 4)] + [(i + 3, i + 1) for i in range(0, size, 4)]
    relay_back = [(target, source) for source, target in relay]
    odd = position % 2

    starts, ends = window_start.T, window_end.T
    relative = jnp.concatenate([starts, ends], axis=0) - (position - 1) * docs
    message = pack(queries, relative)
    near = lax.ppermute(message, AXES, across)
    far_a = lax.ppermute(message, AXES, between)
    far_b = lax.ppermute(near, AXES, relay)
    shifts = jnp.stack([2 * docs * odd, 2 * docs * (1 - odd)]).astype(jnp.int32)
    near_part, far_part = neighbours(shifts, near, far_a, far_b, corpus)
    far_back = lax.ppermute(far_part, AXES, between)
    relayed = lax.ppermute(far_part, AXES, relay_back)
    near_back = lax.ppermute(merge(near_part, relayed), AXES, across)
    message, _ = lax.optimization_barrier((message, far_part))
    own_part = own(jnp.full((1,), docs, jnp.int32), message, corpus)
    pooled, log_mass, mean_score = finish(starts, ends, own_part, near_back, far_back)
    pooled = pooled.reshape(2, rows, width).transpose(1, 0, 2)
    return pooled, log_mass.T, mean_score.T


def solution(mesh):
    placed = P(AXES, None)
    return jax.shard_map(
        local,
        mesh=mesh,
        in_specs=(placed,) * 4,
        out_specs=(P(AXES, None, None), placed, placed),
        check_vma=False,
    )
```

```python
import functools
import math

import jax
import jax.numpy as jnp
from jax import lax
from jax.experimental import pallas as pl
from jax.experimental.pallas import tpu as pltpu
from jax.sharding import PartitionSpec as P

SCORE_SCALE = 3.0
NEG = -1e30
LOG2E = math.log2(math.e)
AXES = ("tm", "pb")
BF16 = jnp.bfloat16
F32 = jnp.float32
NT = (((1,), (1,)), ((), ()))
TN = (((0,), (0,)), ((), ()))
META = 16
LANES = 128
DOC_TILE = 1024
DOT_TILE = 256
ROW_TILE = 16
LOADS = 8

VMEM = pl.BlockSpec(memory_space=pltpu.VMEM)
SMEM = pl.BlockSpec(memory_space=pltpu.SMEM)


def params(mebibytes):
    return pltpu.CompilerParams(vmem_limit_bytes=mebibytes * 2**20)


def identity(n):
    rows = lax.broadcasted_iota(jnp.int32, (n, n), 0)
    return (rows == lax.broadcasted_iota(jnp.int32, (n, n), 1)).astype(BF16)


def split_int(value):
    return (value >> 8).astype(F32), (value & 255).astype(F32)


def split_float(value):
    high = value.astype(BF16).astype(F32)
    rest = value - high
    middle = rest.astype(BF16).astype(F32)
    return high, middle, rest - middle


def row_scratch(rows, docs, width, tile):
    return [
        pltpu.VMEM((rows, width), BF16),
        pltpu.VMEM((2, rows, LANES), jnp.int32),
        pltpu.VMEM((rows, LANES), F32),
        pltpu.VMEM((rows, LANES), F32),
        pltpu.VMEM((rows, LANES), F32),
        pltpu.VMEM((rows, tile), F32),
        pltpu.VMEM((rows, tile), F32),
        pltpu.VMEM((docs // tile, rows, tile), F32),
        pltpu.VMEM((rows, tile), BF16),
        pltpu.VMEM((rows, tile), BF16),
        pltpu.VMEM((rows, width), F32),
    ]


def attend_rows(docs, scratch):
    rows_q, bounds, peak, score_sum, mass, s_a, s_b, masked, p_a, p_b, acc = scratch
    n_docs, width = docs.shape
    rows, tile = s_a.shape
    tiles = n_docs // tile
    scale = SCORE_SCALE / math.sqrt(width)
    starts = range(0, rows, ROW_TILE)

    def share(part, parts):
        each = -(-len(starts) // parts)
        return starts[part * each : (part + 1) * each]

    def score(t, out, part):
        first = pl.multiple_of(t * tile + part * DOT_TILE, DOT_TILE)
        out[:, part * DOT_TILE : (part + 1) * DOT_TILE] = lax.dot_general(
            rows_q[...], docs[pl.ds(first, DOT_TILE), :], NT, preferred_element_type=F32
        )

    def scan(t, scores, some):
        for r in some:
            at = slice(r, r + ROW_TILE)
            offset = t * tile - bounds[0, at, :]
            length = bounds[1, at, :].astype(jnp.uint32)
            top, total = peak[at, :], score_sum[at, :]
            for c in range(0, tile, LANES):
                value = scores[at, c : c + LANES]
                inside = (offset + c).astype(jnp.uint32) < length
                kept = jnp.where(inside, value, NEG)
                top = jnp.maximum(top, kept)
                total = total + jnp.where(inside, value, 0.0)
                masked[t, at, c : c + LANES] = kept
            peak[at, :] = top
            score_sum[at, :] = total

    def score_and_scan(t_score, out, t_scan, scores):
        parts = tile // DOT_TILE
        for part in range(parts):
            score(t_score, out, part)
            scan(t_scan, scores, share(part, parts))

    peak[...] = jnp.full(peak.shape, NEG, F32)
    score_sum[...] = jnp.zeros(score_sum.shape, F32)
    mass[...] = jnp.zeros(mass.shape, F32)
    for part in range(tile // DOT_TILE):
        score(0, s_a, part)

    def first_step(i, carry):
        t = 2 * i
        score_and_scan(t + 1, s_b, t, s_a)
        score_and_scan(jnp.minimum(t + 2, tiles - 1), s_a, t + 1, s_b)
        return carry

    lax.fori_loop(0, tiles // 2, first_step, 0)
    top = jnp.max(peak[...], axis=1, keepdims=True)
    peak[...] = jnp.broadcast_to(jnp.maximum(top, 0.5 * NEG), peak.shape)
    acc[...] = jnp.zeros(acc.shape, F32)

    def weigh(t, out, some):
        for r in some:
            at = slice(r, r + ROW_TILE)
            shift, total = peak[at, :], mass[at, :]
            for c in range(0, tile, LANES):
                p = jnp.exp2((masked[t, at, c : c + LANES] - shift) * (scale * LOG2E))
                total = total + p
                out[at, c : c + LANES] = p.astype(BF16)
            mass[at, :] = total

    def pool(t, weights, part):
        at = slice(part * DOT_TILE, (part + 1) * DOT_TILE)
        block = docs[pl.ds(pl.multiple_of(t * tile, tile), tile), at]
        acc[:, at] += jnp.dot(weights[...], block, preferred_element_type=F32)

    def pool_and_weigh(t, weights, t_weigh, out):
        parts = width // DOT_TILE
        for part in range(parts):
            pool(t, weights, part)
            weigh(t_weigh, out, share(part, parts))

    weigh(0, p_a, starts)

    def second_step(i, carry):
        t = 2 * i + 1
        pool_and_weigh(t - 1, p_a, t, p_b)
        pool_and_weigh(t, p_b, t + 1, p_a)
        return carry

    lax.fori_loop(0, tiles // 2 - 1, second_step, 0)
    pool_and_weigh(tiles - 2, p_a, tiles - 1, p_b)
    for part in range(width // DOT_TILE):
        pool(tiles - 1, p_b, part)
    return (
        top * scale,
        jnp.sum(mass[...], axis=1, keepdims=True),
        jnp.sum(score_sum[...], axis=1, keepdims=True) * scale,
    )


def stats_matrix(stats):
    rows = stats[0].shape[0]
    lane = lax.broadcasted_iota(jnp.int32, (rows, META), 1)
    matrix = jnp.zeros((rows, META), F32)
    for k, value in enumerate(stats):
        for j, part in enumerate(split_float(value)):
            matrix = jnp.where(lane == 3 * k + j, part, matrix)
    return matrix.astype(BF16)


def set_bounds(bounds, at, low, length):
    shape = (low.shape[0], LANES)
    bounds[0, at, :] = low - lax.broadcasted_iota(jnp.int32, shape, 1)
    bounds[1, at, :] = jnp.broadcast_to(length, shape)


def own_kernel(shift, message, docs, out, *scratch):
    queries = message.shape[0] - META
    rows_q, bounds = scratch[:2]
    unit = identity(queries)
    columns = lax.dot_general(
        unit, message[queries:, 0:queries], NT, preferred_element_type=F32
    )

    def bound(k):
        value = columns[:, 2 * k : 2 * k + 1] * 256.0 + columns[:, 2 * k + 1 : 2 * k + 2]
        return jnp.clip(value.astype(jnp.int32) - shift[0], 0, docs.shape[0])

    for w in range(2):
        at = slice(w * queries, (w + 1) * queries)
        low = bound(w)
        set_bounds(bounds, at, low, jnp.maximum(bound(2 + w) - low, 0))
        rows_q[at, :] = message[0:queries, :]
    stats = stats_matrix(attend_rows(docs, scratch))
    out[0 : 2 * queries, :] = scratch[-1][...].astype(BF16)
    out[2 * queries :, :] = jnp.zeros((META, out.shape[1]), BF16)
    for w in range(2):
        at = slice(w * queries, (w + 1) * queries)
        out[2 * queries :, at] = lax.dot_general(
            stats[at, :], unit, TN, preferred_element_type=F32
        ).astype(BF16)


def own(shift, message, corpus):
    docs, width = corpus.shape
    queries = message.shape[0] - META
    tile = min(DOC_TILE, docs // 2)
    return pl.pallas_call(
        own_kernel,
        out_shape=jax.ShapeDtypeStruct((2 * queries + META, width), BF16),
        in_specs=[SMEM, VMEM, VMEM],
        out_specs=VMEM,
        scratch_shapes=row_scratch(2 * queries, docs, width, tile),
        compiler_params=params(20),
        cost_estimate=pl.CostEstimate(
            flops=8 * queries * docs * width,
            bytes_accessed=docs * width * 2,
            transcendentals=2 * queries * docs,
        ),
        name="own_block",
    )(shift, message, corpus)


def neighbour_kernel(shifts, near, far_a, far_b, docs, near_out, far_out, both_q, *scratch):
    queries = near.shape[0] - META
    rows_q, bounds = scratch[:2]
    group = rows_q.shape[0]
    both_q[0:queries, :] = near[0:queries, :]
    both_q[queries:, :] = far_a[0:queries, :] + far_b[0:queries, :]

    lows, lengths = [], []
    for side, meta in enumerate((near[queries:, 0:queries], far_a[queries:, 0:queries] + far_b[queries:, 0:queries])):
        meta = meta.astype(F32)

        def bound(k):
            value = meta[2 * k : 2 * k + 1, :] * 256.0 + meta[2 * k + 1 : 2 * k + 2, :]
            return jnp.clip(value.astype(jnp.int32) - shifts[side], 0, docs.shape[0])

        for w in range(2):
            low = bound(w)
            lows.append(low)
            lengths.append(jnp.maximum(bound(2 + w) - low, 0))
    blocks = len(lows)
    parts = []
    for low, length in zip(lows, lengths):
        rows = [*split_int(low), *split_int(length)]
        parts.append(jnp.concatenate(rows + [jnp.zeros((META - 4, queries), F32)], axis=0).astype(BF16))
    flags = [(length > 0).astype(F32) for length in lengths]
    stacked = jnp.concatenate(flags + [jnp.zeros((META - blocks, queries), F32)], axis=0).astype(BF16)
    before = lax.broadcasted_iota(jnp.int32, (queries, queries), 0) < lax.broadcasted_iota(
        jnp.int32, (queries, queries), 1
    )
    ranks = jnp.dot(stacked, before.astype(BF16), preferred_element_type=F32)
    places, first = [], jnp.zeros((1, 1), F32)
    for b in range(blocks):
        places.append(jnp.where(flags[b] > 0, ranks[b : b + 1, :] + first, -1.0).astype(jnp.int32))
        first = first + jnp.sum(flags[b], axis=1, keepdims=True)
    active = jnp.max(first).astype(jnp.int32)

    near_out[...] = jnp.zeros(near_out.shape, BF16)
    far_out[...] = jnp.zeros(far_out.shape, BF16)

    def work(g, carry):
        row = lax.broadcasted_iota(jnp.int32, (group, queries), 0) + g * group
        pick = [(row == place).astype(F32).astype(BF16) for place in places]
        of_query = jnp.concatenate([pick[0] + pick[1], pick[2] + pick[3]], axis=1)
        rows_q[...] = jnp.dot(of_query, both_q[...], preferred_element_type=F32).astype(BF16)
        columns = jnp.zeros((group, META), F32)
        for chosen, part in zip(pick, parts):
            columns = columns + lax.dot_general(chosen, part, NT, preferred_element_type=F32)
        low = (columns[:, 0:1] * 256.0 + columns[:, 1:2]).astype(jnp.int32)
        length = (columns[:, 2:3] * 256.0 + columns[:, 3:4]).astype(jnp.int32)
        set_bounds(bounds, slice(0, group), low, length)
        stats = stats_matrix(attend_rows(docs, scratch))
        pooled = scratch[-1][...].astype(BF16)
        for b, chosen in enumerate(pick):
            out = (near_out, far_out)[b // 2]
            at = slice((b % 2) * queries, (b % 2 + 1) * queries)
            out[at, :] += lax.dot_general(chosen, pooled, TN, preferred_element_type=F32).astype(BF16)
            out[2 * queries :, at] += lax.dot_general(
                stats, chosen, TN, preferred_element_type=F32
            ).astype(BF16)
        return carry

    lax.fori_loop(0, (active + group - 1) // group, work, 0)


def neighbours(shifts, near, far_a, far_b, corpus):
    docs, width = corpus.shape
    queries = near.shape[0] - META
    tile = min(DOC_TILE, docs // 2)
    group = min(4 * queries, (2 * queries + 3 * queries // 8) // ROW_TILE * ROW_TILE)
    result = jax.ShapeDtypeStruct((2 * queries + META, width), BF16)
    return pl.pallas_call(
        neighbour_kernel,
        out_shape=(result, result),
        in_specs=[SMEM, VMEM, VMEM, VMEM, VMEM],
        out_specs=(VMEM, VMEM),
        scratch_shapes=[pltpu.VMEM((2 * queries, width), BF16)] + row_scratch(group, docs, width, tile),
        compiler_params=params(24),
        cost_estimate=pl.CostEstimate(
            flops=8 * queries * docs * width,
            bytes_accessed=docs * width * 2,
            transcendentals=2 * queries * docs,
        ),
        name="neighbour_blocks",
    )(shifts, near, far_a, far_b, corpus)


def load_kernel(corpus, out, arrived):
    step = corpus.shape[0] // LOADS
    copies = [
        pltpu.make_async_copy(corpus.at[pl.ds(k * step, step)], out.at[pl.ds(k * step, step)], arrived.at[k])
        for k in range(LOADS)
    ]
    for copy in copies:
        copy.start()
    for copy in copies:
        copy.wait()


def load(corpus):
    return pl.pallas_call(
        load_kernel,
        out_shape=jax.ShapeDtypeStruct(corpus.shape, corpus.dtype),
        in_specs=[pl.BlockSpec(memory_space=pltpu.HBM)],
        out_specs=VMEM,
        scratch_shapes=[pltpu.SemaphoreType.DMA((LOADS,))],
        compiler_params=params(44),
        cost_estimate=pl.CostEstimate(flops=0, bytes_accessed=2 * corpus.size * 2, transcendentals=0),
        name="load",
    )(corpus)


def pack_kernel(base, queries, starts, ends, out):
    rows, width = queries.shape
    out[0:rows, :] = queries[...]
    out[rows:, :] = jnp.zeros((META, width), BF16)
    parts = [split_int(lines[...] - base[0]) for lines in (starts, ends)]
    lines = [part[w : w + 1, :] for pair in parts for w in range(2) for part in pair]
    lines.append(jnp.zeros((META - 8, rows), F32))
    out[rows:, 0:rows] = jnp.concatenate(lines, axis=0).astype(BF16)


def pack(base, queries, starts, ends):
    rows, width = queries.shape
    return pl.pallas_call(
        pack_kernel,
        out_shape=jax.ShapeDtypeStruct((rows + META, width), BF16),
        in_specs=[SMEM, VMEM, VMEM, VMEM],
        out_specs=VMEM,
        compiler_params=params(4),
        name="pack",
    )(base, queries, starts, ends)


def columns_of(state, unit, w):
    queries = unit.shape[0]
    lines = state[2 * queries :, w * queries : (w + 1) * queries]
    columns = lax.dot_general(unit, lines, NT, preferred_element_type=F32)
    top, total, score_sum = (
        columns[:, 3 * k : 3 * k + 1] + columns[:, 3 * k + 1 : 3 * k + 2] + columns[:, 3 * k + 2 : 3 * k + 3]
        for k in range(3)
    )
    return jnp.where(total > 0, top, NEG), total, score_sum


def weigh_states(tops):
    best = functools.reduce(jnp.maximum, tops)
    return best, [jnp.exp(top - best) for top in tops]


def merge_kernel(first, second, out):
    queries = (first.shape[0] - META) // 2
    unit = identity(queries)
    out[2 * queries :, :] = jnp.zeros((META, out.shape[1]), BF16)
    for w in range(2):
        at = slice(w * queries, (w + 1) * queries)
        states = [columns_of(state, unit, w) for state in (first, second)]
        best, factors = weigh_states([state[0] for state in states])
        total = functools.reduce(jnp.add, [f * state[1] for f, state in zip(factors, states)])
        score_sum = states[0][2] + states[1][2]
        out[at, :] = (
            factors[0] * first[at, :].astype(F32) + factors[1] * second[at, :].astype(F32)
        ).astype(BF16)
        stats = stats_matrix((best, total, score_sum))
        out[2 * queries :, at] = lax.dot_general(
            stats, unit, TN, preferred_element_type=F32
        ).astype(BF16)


def merge(first, second):
    return pl.pallas_call(
        merge_kernel,
        out_shape=jax.ShapeDtypeStruct(first.shape, BF16),
        in_specs=[VMEM, VMEM],
        out_specs=VMEM,
        compiler_params=params(8),
        name="merge",
    )(first, second)


def finish_kernel(window_start, window_end, first, second, third, pooled, log_mass, mean_score):
    queries = window_start.shape[1]
    unit = identity(queries)
    members = (first, second, third)
    for w in range(2):
        at = slice(w * queries, (w + 1) * queries)
        states = [columns_of(member, unit, w) for member in members]
        _, factors = weigh_states([state[0] for state in states])
        total = functools.reduce(jnp.add, [f * state[1] for f, state in zip(factors, states)])
        weighted = functools.reduce(
            jnp.add, [f * member[at, :].astype(F32) for f, member in zip(factors, members)]
        )
        pooled[:, w, :] = (weighted / total).astype(BF16)

        lines = [member[2 * queries :, at].astype(F32) for member in members]
        tops, totals, sums = (
            [line[3 * k : 3 * k + 1, :] + line[3 * k + 1 : 3 * k + 2, :] + line[3 * k + 2 : 3 * k + 3, :] for line in lines]
            for k in range(3)
        )
        best, factors = weigh_states([jnp.where(t > 0, top, NEG) for top, t in zip(tops, totals)])
        total = functools.reduce(jnp.add, [f * t for f, t in zip(factors, totals)])
        log_mass[w : w + 1, :] = best + jnp.log(total)
        count = (window_end[w : w + 1, :] - window_start[w : w + 1, :]).astype(F32)
        mean_score[w : w + 1, :] = functools.reduce(jnp.add, sums) / count


def finish(window_start, window_end, *members):
    queries = window_start.shape[1]
    width = members[0].shape[1]
    line = jax.ShapeDtypeStruct((2, queries), F32)
    return pl.pallas_call(
        finish_kernel,
        out_shape=(jax.ShapeDtypeStruct((queries, 2, width), BF16), line, line),
        in_specs=[VMEM] * 5,
        out_specs=(VMEM, VMEM, VMEM),
        compiler_params=params(8),
        name="finish",
    )(window_start, window_end, *members)


def local(queries, corpus, window_start, window_end):
    docs = corpus.shape[0]
    size = lax.axis_size(AXES)
    position = lax.axis_index(AXES)
    across = [(i, i ^ 1) for i in range(size)]
    between = [(i, i + 1) for i in range(3, size - 1, 4)] + [(i + 1, i) for i in range(3, size - 1, 4)]
    relay = [(i, i + 2) for i in range(0, size, 4)] + [(i + 3, i + 1) for i in range(0, size, 4)]
    relay_back = [(target, source) for source, target in relay]
    odd = position % 2

    starts, ends = window_start.T, window_end.T
    base = jnp.full((1,), (position - 1) * docs, jnp.int32)
    message = pack(base, queries, starts, ends)
    near = lax.ppermute(message, AXES, across)
    far_a = lax.ppermute(message, AXES, between)
    near, corpus = lax.optimization_barrier((near, load(corpus)))
    far_b = lax.ppermute(near, AXES, relay)
    shifts = jnp.stack([2 * docs * odd, 2 * docs * (1 - odd)]).astype(jnp.int32)
    near_part, far_part = neighbours(shifts, near, far_a, far_b, corpus)
    far_back = lax.ppermute(far_part, AXES, between)
    relayed = lax.ppermute(far_part, AXES, relay_back)
    near_back = lax.ppermute(merge(near_part, relayed), AXES, across)
    message, _ = lax.optimization_barrier((message, far_part))
    own_part = own(jnp.full((1,), docs, jnp.int32), message, corpus)
    pooled, log_mass, mean_score = finish(starts, ends, own_part, near_back, far_back)
    return pooled, log_mass.T, mean_score.T


def solution(mesh):
    placed = P(AXES, None)
    return jax.shard_map(
        local,
        mesh=mesh,
        in_specs=(placed,) * 4,
        out_specs=(P(AXES, None, None), placed, placed),
        check_vma=False,
    )
```

```python
import functools
import math

import jax
import jax.numpy as jnp
from jax import lax
from jax.experimental import pallas as pl
from jax.experimental.pallas import tpu as pltpu
from jax.sharding import PartitionSpec as P

SCORE_SCALE = 3.0
NEG = -1e30
LOG2E = math.log2(math.e)
AXES = ("tm", "pb")
BF16 = jnp.bfloat16
F32 = jnp.float32
NT = (((1,), (1,)), ((), ()))
TN = (((0,), (0,)), ((), ()))
META = 16
LANES = 128
DOC_TILE = 1024
DOT_TILE = 256
ROW_TILE = 16
LOADS = 8

VMEM = pl.BlockSpec(memory_space=pltpu.VMEM)
SMEM = pl.BlockSpec(memory_space=pltpu.SMEM)


def params(mebibytes):
    return pltpu.CompilerParams(vmem_limit_bytes=mebibytes * 2**20)


def identity(n):
    rows = lax.broadcasted_iota(jnp.int32, (n, n), 0)
    return (rows == lax.broadcasted_iota(jnp.int32, (n, n), 1)).astype(BF16)


def split_int(value):
    return (value >> 8).astype(F32), (value & 255).astype(F32)


def split_float(value):
    high = value.astype(BF16).astype(F32)
    rest = value - high
    middle = rest.astype(BF16).astype(F32)
    return high, middle, rest - middle


def row_scratch(rows, docs, width, tile):
    return [
        pltpu.VMEM((rows, width), BF16),
        pltpu.VMEM((2, rows, LANES), jnp.int32),
        pltpu.VMEM((rows, LANES), F32),
        pltpu.VMEM((rows, LANES), F32),
        pltpu.VMEM((rows, LANES), F32),
        pltpu.VMEM((rows, tile), F32),
        pltpu.VMEM((rows, tile), F32),
        pltpu.VMEM((docs // tile, rows, tile), F32),
        pltpu.VMEM((rows, tile), BF16),
        pltpu.VMEM((rows, tile), BF16),
        pltpu.VMEM((rows, width), F32),
    ]


def attend_rows(docs, scratch):
    rows_q, bounds, peak, score_sum, mass, s_a, s_b, masked, p_a, p_b, acc = scratch
    n_docs, width = docs.shape
    rows, tile = s_a.shape
    tiles = n_docs // tile
    scale = SCORE_SCALE / math.sqrt(width)
    starts = range(0, rows, ROW_TILE)

    def share(part, parts):
        each = -(-len(starts) // parts)
        return starts[part * each : (part + 1) * each]

    def score(t, out, part):
        first = pl.multiple_of(t * tile + part * DOT_TILE, DOT_TILE)
        out[:, part * DOT_TILE : (part + 1) * DOT_TILE] = lax.dot_general(
            rows_q[...], docs[pl.ds(first, DOT_TILE), :], NT, preferred_element_type=F32
        )

    def scan(t, scores, some):
        for r in some:
            at = slice(r, r + ROW_TILE)
            offset = t * tile - bounds[0, at, :]
            length = bounds[1, at, :].astype(jnp.uint32)
            top, total = peak[at, :], score_sum[at, :]
            for c in range(0, tile, LANES):
                value = scores[at, c : c + LANES]
                inside = (offset + c).astype(jnp.uint32) < length
                kept = jnp.where(inside, value, NEG)
                top = jnp.maximum(top, kept)
                total = total + jnp.where(inside, value, 0.0)
                masked[t, at, c : c + LANES] = kept
            peak[at, :] = top
            score_sum[at, :] = total

    def score_and_scan(t_score, out, t_scan, scores):
        parts = tile // DOT_TILE
        for part in range(parts):
            score(t_score, out, part)
            scan(t_scan, scores, share(part, parts))

    peak[...] = jnp.full(peak.shape, NEG, F32)
    score_sum[...] = jnp.zeros(score_sum.shape, F32)
    mass[...] = jnp.zeros(mass.shape, F32)
    for part in range(tile // DOT_TILE):
        score(0, s_a, part)

    def first_step(i, carry):
        t = 2 * i
        score_and_scan(t + 1, s_b, t, s_a)
        score_and_scan(jnp.minimum(t + 2, tiles - 1), s_a, t + 1, s_b)
        return carry

    lax.fori_loop(0, tiles // 2, first_step, 0)
    top = jnp.max(peak[...], axis=1, keepdims=True)
    peak[...] = jnp.broadcast_to(jnp.maximum(top, 0.5 * NEG), peak.shape)
    acc[...] = jnp.zeros(acc.shape, F32)

    def weigh(t, out, some):
        for r in some:
            at = slice(r, r + ROW_TILE)
            shift, total = peak[at, :], mass[at, :]
            for c in range(0, tile, LANES):
                p = jnp.exp2((masked[t, at, c : c + LANES] - shift) * (scale * LOG2E))
                total = total + p
                out[at, c : c + LANES] = p.astype(BF16)
            mass[at, :] = total

    def pool(t, weights, part):
        at = slice(part * DOT_TILE, (part + 1) * DOT_TILE)
        block = docs[pl.ds(pl.multiple_of(t * tile, tile), tile), at]
        acc[:, at] += jnp.dot(weights[...], block, preferred_element_type=F32)

    def pool_and_weigh(t, weights, t_weigh, out):
        parts = width // DOT_TILE
        for part in range(parts):
            pool(t, weights, part)
            weigh(t_weigh, out, share(part, parts))

    weigh(0, p_a, starts)

    def second_step(i, carry):
        t = 2 * i + 1
        pool_and_weigh(t - 1, p_a, t, p_b)
        pool_and_weigh(t, p_b, t + 1, p_a)
        return carry

    lax.fori_loop(0, tiles // 2 - 1, second_step, 0)
    pool_and_weigh(tiles - 2, p_a, tiles - 1, p_b)
    for part in range(width // DOT_TILE):
        pool(tiles - 1, p_b, part)
    return (
        top * scale,
        jnp.sum(mass[...], axis=1, keepdims=True),
        jnp.sum(score_sum[...], axis=1, keepdims=True) * scale,
    )


def stats_matrix(stats):
    rows = stats[0].shape[0]
    lane = lax.broadcasted_iota(jnp.int32, (rows, META), 1)
    matrix = jnp.zeros((rows, META), F32)
    for k, value in enumerate(stats):
        for j, part in enumerate(split_float(value)):
            matrix = jnp.where(lane == 3 * k + j, part, matrix)
    return matrix.astype(BF16)


def set_bounds(bounds, at, low, length):
    shape = (low.shape[0], LANES)
    bounds[0, at, :] = low - lax.broadcasted_iota(jnp.int32, shape, 1)
    bounds[1, at, :] = jnp.broadcast_to(length, shape)


def own_kernel(shift, message, docs, out, *scratch):
    queries = message.shape[0] - META
    rows_q, bounds = scratch[:2]
    unit = identity(queries)
    columns = lax.dot_general(
        unit, message[queries:, 0:queries], NT, preferred_element_type=F32
    )

    def bound(k):
        value = columns[:, 2 * k : 2 * k + 1] * 256.0 + columns[:, 2 * k + 1 : 2 * k + 2]
        return jnp.clip(value.astype(jnp.int32) - shift[0], 0, docs.shape[0])

    for w in range(2):
        at = slice(w * queries, (w + 1) * queries)
        low = bound(w)
        set_bounds(bounds, at, low, jnp.maximum(bound(2 + w) - low, 0))
        rows_q[at, :] = message[0:queries, :]
    stats = stats_matrix(attend_rows(docs, scratch))
    out[0 : 2 * queries, :] = scratch[-1][...].astype(BF16)
    out[2 * queries :, :] = jnp.zeros((META, out.shape[1]), BF16)
    for w in range(2):
        at = slice(w * queries, (w + 1) * queries)
        out[2 * queries :, at] = lax.dot_general(
            stats[at, :], unit, TN, preferred_element_type=F32
        ).astype(BF16)


def own(shift, message, corpus):
    docs, width = corpus.shape
    queries = message.shape[0] - META
    tile = min(DOC_TILE, docs // 2)
    return pl.pallas_call(
        own_kernel,
        out_shape=jax.ShapeDtypeStruct((2 * queries + META, width), BF16),
        in_specs=[SMEM, VMEM, VMEM],
        out_specs=VMEM,
        scratch_shapes=row_scratch(2 * queries, docs, width, tile),
        compiler_params=params(20),
        cost_estimate=pl.CostEstimate(
            flops=8 * queries * docs * width,
            bytes_accessed=docs * width * 2,
            transcendentals=2 * queries * docs,
        ),
        name="own_block",
    )(shift, message, corpus)


def neighbour_kernel(shifts, near, far_a, far_b, docs, near_out, far_out, both_q, *scratch):
    queries = near.shape[0] - META
    rows_q, bounds = scratch[:2]
    group = rows_q.shape[0]
    both_q[0:queries, :] = near[0:queries, :]
    both_q[queries:, :] = far_a[0:queries, :] + far_b[0:queries, :]

    lows, lengths = [], []
    for side, meta in enumerate((near[queries:, 0:queries], far_a[queries:, 0:queries] + far_b[queries:, 0:queries])):
        meta = meta.astype(F32)

        def bound(k):
            value = meta[2 * k : 2 * k + 1, :] * 256.0 + meta[2 * k + 1 : 2 * k + 2, :]
            return jnp.clip(value.astype(jnp.int32) - shifts[side], 0, docs.shape[0])

        for w in range(2):
            low = bound(w)
            lows.append(low)
            lengths.append(jnp.maximum(bound(2 + w) - low, 0))
    blocks = len(lows)
    parts = []
    for low, length in zip(lows, lengths):
        rows = [*split_int(low), *split_int(length)]
        parts.append(jnp.concatenate(rows + [jnp.zeros((META - 4, queries), F32)], axis=0).astype(BF16))
    flags = [(length > 0).astype(F32) for length in lengths]
    stacked = jnp.concatenate(flags + [jnp.zeros((META - blocks, queries), F32)], axis=0).astype(BF16)
    before = lax.broadcasted_iota(jnp.int32, (queries, queries), 0) < lax.broadcasted_iota(
        jnp.int32, (queries, queries), 1
    )
    ranks = jnp.dot(stacked, before.astype(BF16), preferred_element_type=F32)
    places, first = [], jnp.zeros((1, 1), F32)
    for b in range(blocks):
        places.append(jnp.where(flags[b] > 0, ranks[b : b + 1, :] + first, -1.0).astype(jnp.int32))
        first = first + jnp.sum(flags[b], axis=1, keepdims=True)
    active = jnp.max(first).astype(jnp.int32)

    near_out[...] = jnp.zeros(near_out.shape, BF16)
    far_out[...] = jnp.zeros(far_out.shape, BF16)

    def work(g, carry):
        row = lax.broadcasted_iota(jnp.int32, (group, queries), 0) + g * group
        pick = [(row == place).astype(F32).astype(BF16) for place in places]
        of_query = jnp.concatenate([pick[0] + pick[1], pick[2] + pick[3]], axis=1)
        rows_q[...] = jnp.dot(of_query, both_q[...], preferred_element_type=F32).astype(BF16)
        columns = jnp.zeros((group, META), F32)
        for chosen, part in zip(pick, parts):
            columns = columns + lax.dot_general(chosen, part, NT, preferred_element_type=F32)
        low = (columns[:, 0:1] * 256.0 + columns[:, 1:2]).astype(jnp.int32)
        length = (columns[:, 2:3] * 256.0 + columns[:, 3:4]).astype(jnp.int32)
        set_bounds(bounds, slice(0, group), low, length)
        stats = stats_matrix(attend_rows(docs, scratch))
        pooled = scratch[-1][...].astype(BF16)
        for b, chosen in enumerate(pick):
            out = (near_out, far_out)[b // 2]
            at = slice((b % 2) * queries, (b % 2 + 1) * queries)
            out[at, :] += lax.dot_general(chosen, pooled, TN, preferred_element_type=F32).astype(BF16)
            out[2 * queries :, at] += lax.dot_general(
                stats, chosen, TN, preferred_element_type=F32
            ).astype(BF16)
        return carry

    lax.fori_loop(0, (active + group - 1) // group, work, 0)


def neighbours(shifts, near, far_a, far_b, corpus):
    docs, width = corpus.shape
    queries = near.shape[0] - META
    tile = min(DOC_TILE, docs // 2)
    group = min(4 * queries, (2 * queries + 3 * queries // 8) // ROW_TILE * ROW_TILE)
    result = jax.ShapeDtypeStruct((2 * queries + META, width), BF16)
    return pl.pallas_call(
        neighbour_kernel,
        out_shape=(result, result),
        in_specs=[SMEM, VMEM, VMEM, VMEM, VMEM],
        out_specs=(VMEM, VMEM),
        scratch_shapes=[pltpu.VMEM((2 * queries, width), BF16)] + row_scratch(group, docs, width, tile),
        compiler_params=params(24),
        cost_estimate=pl.CostEstimate(
            flops=8 * queries * docs * width,
            bytes_accessed=docs * width * 2,
            transcendentals=2 * queries * docs,
        ),
        name="neighbour_blocks",
    )(shifts, near, far_a, far_b, corpus)


def load_kernel(corpus, out, arrived):
    step = corpus.shape[0] // LOADS
    copies = [
        pltpu.make_async_copy(corpus.at[pl.ds(k * step, step)], out.at[pl.ds(k * step, step)], arrived.at[k])
        for k in range(LOADS)
    ]
    for copy in copies:
        copy.start()
    for copy in copies:
        copy.wait()


def load(corpus):
    return pl.pallas_call(
        load_kernel,
        out_shape=jax.ShapeDtypeStruct(corpus.shape, corpus.dtype),
        in_specs=[pl.BlockSpec(memory_space=pltpu.HBM)],
        out_specs=VMEM,
        scratch_shapes=[pltpu.SemaphoreType.DMA((LOADS,))],
        compiler_params=params(36),
        cost_estimate=pl.CostEstimate(flops=0, bytes_accessed=2 * corpus.size * 2, transcendentals=0),
        name="load",
    )(corpus)


def pack_kernel(base, queries, starts, ends, out):
    rows, width = queries.shape
    out[0:rows, :] = queries[...]
    out[rows:, :] = jnp.zeros((META, width), BF16)
    parts = [split_int(lines[...] - base[0]) for lines in (starts, ends)]
    lines = [part[w : w + 1, :] for pair in parts for w in range(2) for part in pair]
    lines.append(jnp.zeros((META - 8, rows), F32))
    out[rows:, 0:rows] = jnp.concatenate(lines, axis=0).astype(BF16)


def pack(base, queries, starts, ends):
    rows, width = queries.shape
    return pl.pallas_call(
        pack_kernel,
        out_shape=jax.ShapeDtypeStruct((rows + META, width), BF16),
        in_specs=[SMEM, VMEM, VMEM, VMEM],
        out_specs=VMEM,
        compiler_params=params(4),
        name="pack",
    )(base, queries, starts, ends)


def columns_of(state, unit, w):
    queries = unit.shape[0]
    lines = state[2 * queries :, w * queries : (w + 1) * queries]
    columns = lax.dot_general(unit, lines, NT, preferred_element_type=F32)
    top, total, score_sum = (
        columns[:, 3 * k : 3 * k + 1] + columns[:, 3 * k + 1 : 3 * k + 2] + columns[:, 3 * k + 2 : 3 * k + 3]
        for k in range(3)
    )
    return jnp.where(total > 0, top, NEG), total, score_sum


def weigh_states(tops):
    best = functools.reduce(jnp.maximum, tops)
    return best, [jnp.exp(top - best) for top in tops]


def merge_kernel(first, second, out):
    queries = (first.shape[0] - META) // 2
    unit = identity(queries)
    out[2 * queries :, :] = jnp.zeros((META, out.shape[1]), BF16)
    for w in range(2):
        at = slice(w * queries, (w + 1) * queries)
        states = [columns_of(state, unit, w) for state in (first, second)]
        best, factors = weigh_states([state[0] for state in states])
        total = functools.reduce(jnp.add, [f * state[1] for f, state in zip(factors, states)])
        score_sum = states[0][2] + states[1][2]
        out[at, :] = (
            factors[0] * first[at, :].astype(F32) + factors[1] * second[at, :].astype(F32)
        ).astype(BF16)
        stats = stats_matrix((best, total, score_sum))
        out[2 * queries :, at] = lax.dot_general(
            stats, unit, TN, preferred_element_type=F32
        ).astype(BF16)


def merge(first, second):
    return pl.pallas_call(
        merge_kernel,
        out_shape=jax.ShapeDtypeStruct(first.shape, BF16),
        in_specs=[VMEM, VMEM],
        out_specs=VMEM,
        compiler_params=params(8),
        name="merge",
    )(first, second)


def finish_kernel(window_start, window_end, first, second, third, pooled, log_mass, mean_score):
    queries = window_start.shape[1]
    unit = identity(queries)
    members = (first, second, third)
    for w in range(2):
        at = slice(w * queries, (w + 1) * queries)
        states = [columns_of(member, unit, w) for member in members]
        _, factors = weigh_states([state[0] for state in states])
        total = functools.reduce(jnp.add, [f * state[1] for f, state in zip(factors, states)])
        weighted = functools.reduce(
            jnp.add, [f * member[at, :].astype(F32) for f, member in zip(factors, members)]
        )
        pooled[:, w, :] = (weighted / total).astype(BF16)

        lines = [member[2 * queries :, at].astype(F32) for member in members]
        tops, totals, sums = (
            [line[3 * k : 3 * k + 1, :] + line[3 * k + 1 : 3 * k + 2, :] + line[3 * k + 2 : 3 * k + 3, :] for line in lines]
            for k in range(3)
        )
        best, factors = weigh_states([jnp.where(t > 0, top, NEG) for top, t in zip(tops, totals)])
        total = functools.reduce(jnp.add, [f * t for f, t in zip(factors, totals)])
        log_mass[w : w + 1, :] = best + jnp.log(total)
        count = (window_end[w : w + 1, :] - window_start[w : w + 1, :]).astype(F32)
        mean_score[w : w + 1, :] = functools.reduce(jnp.add, sums) / count


def finish(window_start, window_end, *members):
    queries = window_start.shape[1]
    width = members[0].shape[1]
    line = jax.ShapeDtypeStruct((2, queries), F32)
    return pl.pallas_call(
        finish_kernel,
        out_shape=(jax.ShapeDtypeStruct((queries, 2, width), BF16), line, line),
        in_specs=[VMEM] * 5,
        out_specs=(VMEM, VMEM, VMEM),
        compiler_params=params(8),
        name="finish",
    )(window_start, window_end, *members)


def local(queries, corpus, window_start, window_end):
    docs = corpus.shape[0]
    size = lax.axis_size(AXES)
    position = lax.axis_index(AXES)
    across = [(i, i ^ 1) for i in range(size)]
    between = [(i, i + 1) for i in range(3, size - 1, 4)] + [(i + 1, i) for i in range(3, size - 1, 4)]
    relay = [(i, i + 2) for i in range(0, size, 4)] + [(i + 3, i + 1) for i in range(0, size, 4)]
    relay_back = [(target, source) for source, target in relay]
    odd = position % 2

    starts, ends = window_start.T, window_end.T
    base = jnp.full((1,), (position - 1) * docs, jnp.int32)
    message = pack(base, queries, starts, ends)
    near = lax.ppermute(message, AXES, across)
    far_a = lax.ppermute(message, AXES, between)
    near, corpus = lax.optimization_barrier((near, load(corpus)))
    far_b = lax.ppermute(near, AXES, relay)
    shifts = jnp.stack([2 * docs * odd, 2 * docs * (1 - odd)]).astype(jnp.int32)
    near_part, far_part = neighbours(shifts, near, far_a, far_b, corpus)
    far_back = lax.ppermute(far_part, AXES, between)
    relayed = lax.ppermute(far_part, AXES, relay_back)
    near_back = lax.ppermute(merge(near_part, relayed), AXES, across)
    message, _ = lax.optimization_barrier((message, far_part))
    own_part = own(jnp.full((1,), docs, jnp.int32), message, corpus)
    pooled, log_mass, mean_score = finish(starts, ends, own_part, near_back, far_back)
    return pooled, log_mass.T, mean_score.T


def solution(mesh):
    placed = P(AXES, None)
    return jax.shard_map(
        local,
        mesh=mesh,
        in_specs=(placed,) * 4,
        out_specs=(P(AXES, None, None), placed, placed),
        check_vma=False,
    )
```

```python
import functools
import math

import jax
import jax.numpy as jnp
from jax import lax
from jax.experimental import pallas as pl
from jax.experimental.pallas import tpu as pltpu
from jax.sharding import PartitionSpec as P

SCORE_SCALE = 3.0
NEG = -1e30
LOG2E = math.log2(math.e)
AXES = ("tm", "pb")
BF16 = jnp.bfloat16
F32 = jnp.float32
NT = (((1,), (1,)), ((), ()))
TN = (((0,), (0,)), ((), ()))
META = 16
LANES = 128
DOC_TILE = 1024
DOT_TILE = 256
ROW_TILE = 16

VMEM = pl.BlockSpec(memory_space=pltpu.VMEM)
SMEM = pl.BlockSpec(memory_space=pltpu.SMEM)
HBM = pl.BlockSpec(memory_space=pltpu.HBM)


def params(mebibytes):
    return pltpu.CompilerParams(vmem_limit_bytes=mebibytes * 2**20)


def identity(n):
    rows = lax.broadcasted_iota(jnp.int32, (n, n), 0)
    return (rows == lax.broadcasted_iota(jnp.int32, (n, n), 1)).astype(BF16)


def split_int(value):
    return (value >> 8).astype(F32), (value & 255).astype(F32)


def split_float(value):
    high = value.astype(BF16).astype(F32)
    rest = value - high
    middle = rest.astype(BF16).astype(F32)
    return high, middle, rest - middle


def row_scratch(rows, window, items, docs, width, tile):
    return [
        pltpu.VMEM((docs, width), BF16),
        pltpu.SemaphoreType.DMA((docs // tile,)),
        pltpu.VMEM((rows, width), BF16),
        pltpu.VMEM((2, rows, LANES), jnp.int32),
        pltpu.VMEM((rows, LANES), F32),
        pltpu.VMEM((rows, LANES), F32),
        pltpu.VMEM((rows, LANES), F32),
        pltpu.VMEM((window, tile), F32),
        pltpu.VMEM((window, tile), F32),
        pltpu.VMEM((items, window, tile), F32),
        pltpu.VMEM((window, tile), BF16),
        pltpu.VMEM((window, tile), BF16),
        pltpu.VMEM((rows, width), F32),
    ]


def tile_copy(corpus, docs, arrived, t):
    tile = docs.shape[0] // arrived.shape[0]
    at = pl.ds(pl.multiple_of(t * tile, tile), tile)
    return pltpu.make_async_copy(corpus.at[at], docs.at[at], arrived.at[t])


def start_copies(corpus, docs, arrived):
    for t in range(arrived.shape[0]):
        tile_copy(corpus, docs, arrived, t).start()


def attend_rows(scratch, count, item, ready):
    docs, _, rows_q, bounds, peak, score_sum, mass, s_a, s_b, masked, p_a, p_b, acc = scratch
    width = docs.shape[1]
    window, tile = s_a.shape
    scale = SCORE_SCALE / math.sqrt(width)
    starts = range(0, window, ROW_TILE)

    def rows_from(first, n):
        if isinstance(first, int):
            return slice(first, first + n)
        return pl.ds(pl.multiple_of(first, ROW_TILE), n)

    def share(part, parts):
        each = -(-len(starts) // parts)
        return starts[part * each : (part + 1) * each]

    def score(i, out, part):
        t, first_row = item(i)
        first = pl.multiple_of(t * tile + part * DOT_TILE, DOT_TILE)
        out[:, part * DOT_TILE : (part + 1) * DOT_TILE] = lax.dot_general(
            rows_q[rows_from(first_row, window), :],
            docs[pl.ds(first, DOT_TILE), :],
            NT,
            preferred_element_type=F32,
        )

    def scan(i, scores, some):
        t, first_row = item(i)
        for r in some:
            at = rows_from(first_row + r, ROW_TILE)
            offset = t * tile - bounds[0, at, :]
            length = bounds[1, at, :].astype(jnp.uint32)
            top, total = peak[at, :], score_sum[at, :]
            for c in range(0, tile, LANES):
                value = scores[r : r + ROW_TILE, c : c + LANES]
                inside = (offset + c).astype(jnp.uint32) < length
                kept = jnp.where(inside, value, NEG)
                top = jnp.maximum(top, kept)
                total = total + jnp.where(inside, value, 0.0)
                masked[i, r : r + ROW_TILE, c : c + LANES] = kept
            peak[at, :] = top
            score_sum[at, :] = total

    def score_and_scan(i_score, out, i_scan, scores):
        parts = tile // DOT_TILE
        for part in range(parts):
            score(i_score, out, part)
            scan(i_scan, scores, share(part, parts))

    peak[...] = jnp.full(peak.shape, NEG, F32)
    score_sum[...] = jnp.zeros(score_sum.shape, F32)
    mass[...] = jnp.zeros(mass.shape, F32)
    ready(0)
    for part in range(tile // DOT_TILE):
        score(0, s_a, part)

    def first_step(k, carry):
        i = 2 * k
        ready(i + 1)

        @pl.when(i + 2 < count)
        def _():
            ready(i + 2)

        score_and_scan(i + 1, s_b, i, s_a)
        score_and_scan(jnp.minimum(i + 2, count - 1), s_a, i + 1, s_b)
        return carry

    lax.fori_loop(0, count // 2, first_step, 0)
    top = jnp.max(peak[...], axis=1, keepdims=True)
    peak[...] = jnp.broadcast_to(jnp.maximum(top, 0.5 * NEG), peak.shape)
    acc[...] = jnp.zeros(acc.shape, F32)

    def weigh(i, out, some):
        _, first_row = item(i)
        for r in some:
            at = rows_from(first_row + r, ROW_TILE)
            shift, total = peak[at, :], mass[at, :]
            for c in range(0, tile, LANES):
                p = jnp.exp2((masked[i, r : r + ROW_TILE, c : c + LANES] - shift) * (scale * LOG2E))
                total = total + p
                out[r : r + ROW_TILE, c : c + LANES] = p.astype(BF16)
            mass[at, :] = total

    def pool(i, weights, part):
        t, first_row = item(i)
        at = slice(part * DOT_TILE, (part + 1) * DOT_TILE)
        block = docs[pl.ds(pl.multiple_of(t * tile, tile), tile), at]
        acc[rows_from(first_row, window), at] += jnp.dot(weights[...], block, preferred_element_type=F32)

    def pool_and_weigh(i, weights, i_weigh, out):
        parts = width // DOT_TILE
        for part in range(parts):
            pool(i, weights, part)
            weigh(i_weigh, out, share(part, parts))

    weigh(0, p_a, starts)

    def second_step(k, carry):
        i = 2 * k + 1
        pool_and_weigh(i - 1, p_a, i, p_b)
        pool_and_weigh(i, p_b, i + 1, p_a)
        return carry

    lax.fori_loop(0, count // 2 - 1, second_step, 0)
    pool_and_weigh(count - 2, p_a, count - 1, p_b)
    for part in range(width // DOT_TILE):
        pool(count - 1, p_b, part)
    return (
        top * scale,
        jnp.sum(mass[...], axis=1, keepdims=True),
        jnp.sum(score_sum[...], axis=1, keepdims=True) * scale,
    )


def stats_matrix(stats):
    rows = stats[0].shape[0]
    lane = lax.broadcasted_iota(jnp.int32, (rows, META), 1)
    matrix = jnp.zeros((rows, META), F32)
    for k, value in enumerate(stats):
        for j, part in enumerate(split_float(value)):
            matrix = jnp.where(lane == 3 * k + j, part, matrix)
    return matrix.astype(BF16)


def set_bounds(bounds, at, low, length):
    shape = (low.shape[0], LANES)
    bounds[0, at, :] = low - lax.broadcasted_iota(jnp.int32, shape, 1)
    bounds[1, at, :] = jnp.broadcast_to(length, shape)


def own_kernel(shift, message, corpus, out, *scratch):
    docs, arrived, rows_q, bounds = scratch[:4]
    start_copies(corpus, docs, arrived)
    queries = message.shape[0] - META
    unit = identity(queries)
    columns = lax.dot_general(
        unit, message[queries:, 0:queries], NT, preferred_element_type=F32
    )

    def bound(k):
        value = columns[:, 2 * k : 2 * k + 1] * 256.0 + columns[:, 2 * k + 1 : 2 * k + 2]
        return jnp.clip(value.astype(jnp.int32) - shift[0], 0, docs.shape[0])

    for w in range(2):
        at = slice(w * queries, (w + 1) * queries)
        low = bound(w)
        set_bounds(bounds, at, low, jnp.maximum(bound(2 + w) - low, 0))
        rows_q[at, :] = message[0:queries, :]
    stats = stats_matrix(
        attend_rows(
            scratch,
            arrived.shape[0],
            lambda i: (i, 0),
            lambda i: tile_copy(corpus, docs, arrived, i).wait(),
        )
    )
    out[0 : 2 * queries, :] = scratch[-1][...].astype(BF16)
    out[2 * queries :, :] = jnp.zeros((META, out.shape[1]), BF16)
    for w in range(2):
        at = slice(w * queries, (w + 1) * queries)
        out[2 * queries :, at] = lax.dot_general(
            stats[at, :], unit, TN, preferred_element_type=F32
        ).astype(BF16)


def own(shift, message, corpus):
    docs, width = corpus.shape
    queries = message.shape[0] - META
    tile = min(DOC_TILE, docs // 2)
    return pl.pallas_call(
        own_kernel,
        out_shape=jax.ShapeDtypeStruct((2 * queries + META, width), BF16),
        in_specs=[SMEM, VMEM, HBM],
        out_specs=VMEM,
        scratch_shapes=row_scratch(2 * queries, 2 * queries, docs // tile, docs, width, tile),
        compiler_params=params(44),
        cost_estimate=pl.CostEstimate(
            flops=8 * queries * docs * width,
            bytes_accessed=docs * width * 2,
            transcendentals=2 * queries * docs,
        ),
        name="own_block",
    )(shift, message, corpus)


def neighbour_kernel(
    shifts, near, far_a, far_b, corpus, near_out, far_out, both_q, pooled, spans, item_spans, items, span_done, *scratch
):
    docs, arrived, rows_q, bounds = scratch[:4]
    start_copies(corpus, docs, arrived)
    queries = near.shape[0] - META
    n_docs = docs.shape[0]
    tiles = arrived.shape[0]
    tile = n_docs // tiles
    window = scratch[7].shape[0]
    both_q[0:queries, :] = near[0:queries, :]
    both_q[queries:, :] = far_a[0:queries, :] + far_b[0:queries, :]
    metas = (near[queries:, 0:queries], far_a[queries:, 0:queries] + far_b[queries:, 0:queries])

    lows, highs = [], []
    for side, meta in enumerate(metas):
        meta = meta.astype(F32)

        def bound(k):
            value = meta[2 * k : 2 * k + 1, :] * 256.0 + meta[2 * k + 1 : 2 * k + 2, :]
            return jnp.clip(value.astype(jnp.int32) - shifts[side], 0, n_docs)

        for w in range(2):
            lows.append(bound(w))
            highs.append(jnp.maximum(bound(2 + w), lows[-1]))
    blocks = len(lows)
    rows = blocks * queries

    keys = [
        jnp.where(high > low, jnp.where(low == 0, high, n_docs + low), 2 * n_docs)
        for low, high in zip(lows, highs)
    ]
    parts = []
    for low, high, key in zip(lows, highs, keys):
        lines = [*split_int(low), *split_int(high - low), *split_int(key)]
        parts.append(jnp.concatenate(lines + [jnp.zeros((META - 6, queries), F32)], axis=0).astype(BF16))
    unit = identity(queries)
    lane = lax.broadcasted_iota(jnp.int32, (1, queries), 1)
    line = lax.broadcasted_iota(jnp.int32, (queries, 1), 0)
    places = [jnp.zeros((1, queries), F32)] * blocks
    ordered = [keys[b] * rows + (lane + b * queries) for b in range(blocks)]
    for a in range(blocks):
        columns = lax.dot_general(unit, parts[a], NT, preferred_element_type=F32)
        key = (columns[:, 4:5] * 256.0 + columns[:, 5:6]).astype(jnp.int32)
        key = jnp.broadcast_to(key * rows + (line + a * queries), (queries, queries))
        for b in range(blocks):
            places[b] = places[b] + jnp.sum((key < ordered[b]).astype(F32), axis=0, keepdims=True)
    places = [place.astype(jnp.int32) for place in places]

    begin = lax.broadcasted_iota(jnp.int32, (tiles, queries), 0) * tile
    first = jnp.full((tiles, 1), rows, jnp.int32)
    last = jnp.zeros((tiles, 1), jnp.int32)
    for low, high, place in zip(lows, highs, places):
        met = (high > low) & (low < begin + tile) & (high > begin)
        first = jnp.minimum(first, jnp.min(jnp.where(met, place, rows), axis=1, keepdims=True))
        last = jnp.maximum(last, jnp.max(jnp.where(met, place + 1, 0), axis=1, keepdims=True))
    column = lax.broadcasted_iota(jnp.int32, (tiles, LANES), 1)
    spans[...] = jnp.where(column == 0, first, last)
    copy = pltpu.make_async_copy(spans, item_spans, span_done)
    copy.start()

    pick = []
    for b in range(blocks):
        row = lax.broadcasted_iota(jnp.int32, (rows, queries), 0)
        pick.append((row == places[b]).astype(F32).astype(BF16))
    of_query = jnp.concatenate([pick[0] + pick[1], pick[2] + pick[3]], axis=1)
    rows_q[0:rows, :] = jnp.dot(of_query, both_q[...], preferred_element_type=F32).astype(BF16)
    rows_q[rows:, :] = jnp.zeros((rows_q.shape[0] - rows, rows_q.shape[1]), BF16)
    columns = jnp.zeros((rows, META), F32)
    for chosen, part in zip(pick, parts):
        columns = columns + lax.dot_general(chosen, part, NT, preferred_element_type=F32)
    low = (columns[:, 0:1] * 256.0 + columns[:, 1:2]).astype(jnp.int32)
    length = (columns[:, 2:3] * 256.0 + columns[:, 3:4]).astype(jnp.int32)
    set_bounds(bounds, slice(0, rows), low, length)
    none = jnp.zeros((bounds.shape[1] - rows, 1), jnp.int32)
    set_bounds(bounds, slice(rows, bounds.shape[1]), none, none)

    copy.wait()
    count = jnp.int32(0)
    for t in range(tiles):
        head = jnp.minimum(item_spans[t, 0] // ROW_TILE * ROW_TILE, rows - ROW_TILE)
        for k in range(-(-rows // window)):
            items[0, count] = t
            items[1, count] = head + k * window
            items[2, count] = 1 if k == 0 else 0
            more = True if k == 0 else head + k * window < item_spans[t, 1]
            count = count + jnp.where(more, 1, 0)
    items[0, count] = tiles - 1
    items[1, count] = rows
    items[2, count] = 0
    count = (count + 1) // 2 * 2

    def ready(i):
        @pl.when(items[2, i] == 1)
        def _():
            tile_copy(corpus, docs, arrived, items[0, i]).wait()

    stats = stats_matrix(attend_rows(scratch, count, lambda i: (items[0, i], items[1, i]), ready))[0:rows, :]
    pooled[...] = scratch[-1][0:rows, :].astype(BF16)
    for out in (near_out, far_out):
        out[2 * queries :, :] = jnp.zeros((META, out.shape[1]), BF16)
    for b, chosen in enumerate(pick):
        out = (near_out, far_out)[b // 2]
        at = slice((b % 2) * queries, (b % 2 + 1) * queries)
        out[at, :] = lax.dot_general(chosen, pooled[...], TN, preferred_element_type=F32).astype(BF16)
        out[2 * queries :, at] = lax.dot_general(
            stats, chosen, TN, preferred_element_type=F32
        ).astype(BF16)


def neighbours(shifts, near, far_a, far_b, corpus):
    docs, width = corpus.shape
    queries = near.shape[0] - META
    rows = 4 * queries
    tile = min(DOC_TILE, docs // 2)
    window = min(rows, (queries + 3 * queries // 8) // ROW_TILE * ROW_TILE)
    most = docs // tile * -(-rows // window) + 2
    result = jax.ShapeDtypeStruct((2 * queries + META, width), BF16)
    return pl.pallas_call(
        neighbour_kernel,
        out_shape=(result, result),
        in_specs=[SMEM, VMEM, VMEM, VMEM, HBM],
        out_specs=(VMEM, VMEM),
        scratch_shapes=[
            pltpu.VMEM((2 * queries, width), BF16),
            pltpu.VMEM((rows, width), BF16),
            pltpu.VMEM((docs // tile, LANES), jnp.int32),
            pltpu.SMEM((docs // tile, LANES), jnp.int32),
            pltpu.SMEM((3, most), jnp.int32),
            pltpu.SemaphoreType.DMA,
        ]
        + row_scratch(rows + window, window, most, docs, width, tile),
        compiler_params=params(44),
        cost_estimate=pl.CostEstimate(
            flops=8 * queries * docs * width,
            bytes_accessed=docs * width * 2,
            transcendentals=2 * queries * docs,
        ),
        name="neighbour_blocks",
    )(shifts, near, far_a, far_b, corpus)


def pack_kernel(base, queries, starts, ends, out):
    rows, width = queries.shape
    out[0:rows, :] = queries[...]
    out[rows:, :] = jnp.zeros((META, width), BF16)
    parts = [split_int(lines[...] - base[0]) for lines in (starts, ends)]
    lines = [part[w : w + 1, :] for pair in parts for w in range(2) for part in pair]
    lines.append(jnp.zeros((META - 8, rows), F32))
    out[rows:, 0:rows] = jnp.concatenate(lines, axis=0).astype(BF16)


def pack(base, queries, starts, ends):
    rows, width = queries.shape
    return pl.pallas_call(
        pack_kernel,
        out_shape=jax.ShapeDtypeStruct((rows + META, width), BF16),
        in_specs=[SMEM, VMEM, VMEM, VMEM],
        out_specs=VMEM,
        compiler_params=params(4),
        name="pack",
    )(base, queries, starts, ends)


def columns_of(state, unit, w):
    queries = unit.shape[0]
    lines = state[2 * queries :, w * queries : (w + 1) * queries]
    columns = lax.dot_general(unit, lines, NT, preferred_element_type=F32)
    top, total, score_sum = (
        columns[:, 3 * k : 3 * k + 1] + columns[:, 3 * k + 1 : 3 * k + 2] + columns[:, 3 * k + 2 : 3 * k + 3]
        for k in range(3)
    )
    return jnp.where(total > 0, top, NEG), total, score_sum


def weigh_states(tops):
    best = functools.reduce(jnp.maximum, tops)
    return best, [jnp.exp(top - best) for top in tops]


def merge_kernel(first, second, out):
    queries = (first.shape[0] - META) // 2
    unit = identity(queries)
    out[2 * queries :, :] = jnp.zeros((META, out.shape[1]), BF16)
    for w in range(2):
        at = slice(w * queries, (w + 1) * queries)
        states = [columns_of(state, unit, w) for state in (first, second)]
        best, factors = weigh_states([state[0] for state in states])
        total = functools.reduce(jnp.add, [f * state[1] for f, state in zip(factors, states)])
        score_sum = states[0][2] + states[1][2]
        out[at, :] = (
            factors[0] * first[at, :].astype(F32) + factors[1] * second[at, :].astype(F32)
        ).astype(BF16)
        stats = stats_matrix((best, total, score_sum))
        out[2 * queries :, at] = lax.dot_general(
            stats, unit, TN, preferred_element_type=F32
        ).astype(BF16)


def merge(first, second):
    return pl.pallas_call(
        merge_kernel,
        out_shape=jax.ShapeDtypeStruct(first.shape, BF16),
        in_specs=[VMEM, VMEM],
        out_specs=VMEM,
        compiler_params=params(8),
        name="merge",
    )(first, second)


def finish_kernel(window_start, window_end, first, second, third, pooled, log_mass, mean_score):
    queries = window_start.shape[1]
    unit = identity(queries)
    members = (first, second, third)
    for w in range(2):
        at = slice(w * queries, (w + 1) * queries)
        states = [columns_of(member, unit, w) for member in members]
        _, factors = weigh_states([state[0] for state in states])
        total = functools.reduce(jnp.add, [f * state[1] for f, state in zip(factors, states)])
        weighted = functools.reduce(
            jnp.add, [f * member[at, :].astype(F32) for f, member in zip(factors, members)]
        )
        pooled[:, w, :] = (weighted / total).astype(BF16)

        lines = [member[2 * queries :, at].astype(F32) for member in members]
        tops, totals, sums = (
            [line[3 * k : 3 * k + 1, :] + line[3 * k + 1 : 3 * k + 2, :] + line[3 * k + 2 : 3 * k + 3, :] for line in lines]
            for k in range(3)
        )
        best, factors = weigh_states([jnp.where(t > 0, top, NEG) for top, t in zip(tops, totals)])
        total = functools.reduce(jnp.add, [f * t for f, t in zip(factors, totals)])
        log_mass[w : w + 1, :] = best + jnp.log(total)
        count = (window_end[w : w + 1, :] - window_start[w : w + 1, :]).astype(F32)
        mean_score[w : w + 1, :] = functools.reduce(jnp.add, sums) / count


def finish(window_start, window_end, *members):
    queries = window_start.shape[1]
    width = members[0].shape[1]
    line = jax.ShapeDtypeStruct((2, queries), F32)
    return pl.pallas_call(
        finish_kernel,
        out_shape=(jax.ShapeDtypeStruct((queries, 2, width), BF16), line, line),
        in_specs=[VMEM] * 5,
        out_specs=(VMEM, VMEM, VMEM),
        compiler_params=params(8),
        name="finish",
    )(window_start, window_end, *members)


def local(queries, corpus, window_start, window_end):
    docs = corpus.shape[0]
    size = lax.axis_size(AXES)
    position = lax.axis_index(AXES)
    across = [(i, i ^ 1) for i in range(size)]
    between = [(i, i + 1) for i in range(3, size - 1, 4)] + [(i + 1, i) for i in range(3, size - 1, 4)]
    relay = [(i, i + 2) for i in range(0, size, 4)] + [(i + 3, i + 1) for i in range(0, size, 4)]
    relay_back = [(target, source) for source, target in relay]
    odd = position % 2

    starts, ends = window_start.T, window_end.T
    base = jnp.full((1,), (position - 1) * docs, jnp.int32)
    message = pack(base, queries, starts, ends)
    near = lax.ppermute(message, AXES, across)
    far_a = lax.ppermute(message, AXES, between)
    far_b = lax.ppermute(near, AXES, relay)
    shifts = jnp.stack([2 * docs * odd, 2 * docs * (1 - odd)]).astype(jnp.int32)
    near_part, far_part = neighbours(shifts, near, far_a, far_b, corpus)
    far_back = lax.ppermute(far_part, AXES, between)
    relayed = lax.ppermute(far_part, AXES, relay_back)
    near_back = lax.ppermute(merge(near_part, relayed), AXES, across)
    message, _ = lax.optimization_barrier((message, far_part))
    own_part = own(jnp.full((1,), docs, jnp.int32), message, corpus)
    pooled, log_mass, mean_score = finish(starts, ends, own_part, near_back, far_back)
    return pooled, log_mass.T, mean_score.T


def solution(mesh):
    placed = P(AXES, None)
    return jax.shard_map(
        local,
        mesh=mesh,
        in_specs=(placed,) * 4,
        out_specs=(P(AXES, None, None), placed, placed),
        check_vma=False,
    )
```

```python
import functools
import math

import jax
import jax.numpy as jnp
from jax import lax
from jax.experimental import pallas as pl
from jax.experimental.pallas import tpu as pltpu
from jax.sharding import PartitionSpec as P

SCORE_SCALE = 3.0
NEG = -1e30
LOG2E = math.log2(math.e)
AXES = ("tm", "pb")
BF16 = jnp.bfloat16
F32 = jnp.float32
NT = (((1,), (1,)), ((), ()))
TN = (((0,), (0,)), ((), ()))
META = 16
LANES = 128
DOC_TILE = 1024
DOT_TILE = 256
ROW_TILE = 16

VMEM = pl.BlockSpec(memory_space=pltpu.VMEM)
SMEM = pl.BlockSpec(memory_space=pltpu.SMEM)
HBM = pl.BlockSpec(memory_space=pltpu.HBM)


def params(mebibytes):
    return pltpu.CompilerParams(vmem_limit_bytes=mebibytes * 2**20)


def identity(n):
    rows = lax.broadcasted_iota(jnp.int32, (n, n), 0)
    return (rows == lax.broadcasted_iota(jnp.int32, (n, n), 1)).astype(BF16)


def split_int(value):
    return (value >> 8).astype(F32), (value & 255).astype(F32)


def split_float(value):
    high = value.astype(BF16).astype(F32)
    rest = value - high
    middle = rest.astype(BF16).astype(F32)
    return high, middle, rest - middle


def row_scratch(rows, window, items, docs, width, tile):
    return [
        pltpu.VMEM((docs, width), BF16),
        pltpu.SemaphoreType.DMA((docs // tile,)),
        pltpu.VMEM((rows, width), BF16),
        pltpu.VMEM((2, rows, LANES), jnp.int32),
        pltpu.VMEM((rows, LANES), F32),
        pltpu.VMEM((rows, LANES), F32),
        pltpu.VMEM((rows, LANES), F32),
        pltpu.VMEM((window, tile), F32),
        pltpu.VMEM((window, tile), F32),
        pltpu.VMEM((items, window, tile), F32),
        pltpu.VMEM((window, tile), BF16),
        pltpu.VMEM((window, tile), BF16),
        pltpu.VMEM((rows, width), F32),
    ]


def tile_copy(corpus, docs, arrived, t):
    tile = docs.shape[0] // arrived.shape[0]
    at = pl.ds(pl.multiple_of(t * tile, tile), tile)
    return pltpu.make_async_copy(corpus.at[at], docs.at[at], arrived.at[t])


def start_copies(corpus, docs, arrived):
    for t in range(arrived.shape[0]):
        tile_copy(corpus, docs, arrived, t).start()


def attend_rows(scratch, count, item, ready):
    docs, _, rows_q, bounds, peak, score_sum, mass, s_a, s_b, masked, p_a, p_b, acc = scratch
    width = docs.shape[1]
    window, tile = s_a.shape
    scale = SCORE_SCALE / math.sqrt(width)
    starts = range(0, window, ROW_TILE)

    def rows_from(first, n):
        if isinstance(first, int):
            return slice(first, first + n)
        return pl.ds(pl.multiple_of(first, ROW_TILE), n)

    def share(part, parts):
        each = -(-len(starts) // parts)
        return starts[part * each : (part + 1) * each]

    def score(i, out, part):
        t, first_row = item(i)
        first = pl.multiple_of(t * tile + part * DOT_TILE, DOT_TILE)
        out[:, part * DOT_TILE : (part + 1) * DOT_TILE] = lax.dot_general(
            rows_q[rows_from(first_row, window), :],
            docs[pl.ds(first, DOT_TILE), :],
            NT,
            preferred_element_type=F32,
        )

    def scan(i, scores, some):
        t, first_row = item(i)
        for r in some:
            at = rows_from(first_row + r, ROW_TILE)
            offset = t * tile - bounds[0, at, :]
            length = bounds[1, at, :].astype(jnp.uint32)
            top, total = peak[at, :], score_sum[at, :]
            for c in range(0, tile, LANES):
                value = scores[r : r + ROW_TILE, c : c + LANES]
                inside = (offset + c).astype(jnp.uint32) < length
                kept = jnp.where(inside, value, NEG)
                top = jnp.maximum(top, kept)
                total = total + jnp.where(inside, value, 0.0)
                masked[i, r : r + ROW_TILE, c : c + LANES] = kept
            peak[at, :] = top
            score_sum[at, :] = total

    def score_and_scan(i_score, out, i_scan, scores):
        parts = tile // DOT_TILE
        for part in range(parts):
            score(i_score, out, part)
            scan(i_scan, scores, share(part, parts))

    peak[...] = jnp.full(peak.shape, NEG, F32)
    score_sum[...] = jnp.zeros(score_sum.shape, F32)
    mass[...] = jnp.zeros(mass.shape, F32)
    ready(0)
    for part in range(tile // DOT_TILE):
        score(0, s_a, part)

    def first_step(k, carry):
        i = 2 * k
        ready(i + 1)

        @pl.when(i + 2 < count)
        def _():
            ready(i + 2)

        score_and_scan(i + 1, s_b, i, s_a)
        score_and_scan(jnp.minimum(i + 2, count - 1), s_a, i + 1, s_b)
        return carry

    lax.fori_loop(0, count // 2, first_step, 0)
    top = jnp.max(peak[...], axis=1, keepdims=True)
    peak[...] = jnp.broadcast_to(jnp.maximum(top, 0.5 * NEG), peak.shape)
    acc[...] = jnp.zeros(acc.shape, F32)

    def weigh(i, out, some):
        _, first_row = item(i)
        for r in some:
            at = rows_from(first_row + r, ROW_TILE)
            shift, total = peak[at, :], mass[at, :]
            for c in range(0, tile, LANES):
                p = jnp.exp2((masked[i, r : r + ROW_TILE, c : c + LANES] - shift) * (scale * LOG2E))
                total = total + p
                out[r : r + ROW_TILE, c : c + LANES] = p.astype(BF16)
            mass[at, :] = total

    def pool(i, weights, part):
        t, first_row = item(i)
        at = slice(part * DOT_TILE, (part + 1) * DOT_TILE)
        block = docs[pl.ds(pl.multiple_of(t * tile, tile), tile), at]
        acc[rows_from(first_row, window), at] += jnp.dot(weights[...], block, preferred_element_type=F32)

    def pool_and_weigh(i, weights, i_weigh, out):
        parts = width // DOT_TILE
        for part in range(parts):
            pool(i, weights, part)
            weigh(i_weigh, out, share(part, parts))

    weigh(0, p_a, starts)

    def second_step(k, carry):
        i = 2 * k + 1
        pool_and_weigh(i - 1, p_a, i, p_b)
        pool_and_weigh(i, p_b, i + 1, p_a)
        return carry

    lax.fori_loop(0, count // 2 - 1, second_step, 0)
    pool_and_weigh(count - 2, p_a, count - 1, p_b)
    for part in range(width // DOT_TILE):
        pool(count - 1, p_b, part)
    return (
        top * scale,
        jnp.sum(mass[...], axis=1, keepdims=True),
        jnp.sum(score_sum[...], axis=1, keepdims=True) * scale,
    )


def stats_matrix(stats):
    rows = stats[0].shape[0]
    lane = lax.broadcasted_iota(jnp.int32, (rows, META), 1)
    matrix = jnp.zeros((rows, META), F32)
    for k, value in enumerate(stats):
        for j, part in enumerate(split_float(value)):
            matrix = jnp.where(lane == 3 * k + j, part, matrix)
    return matrix.astype(BF16)


def set_bounds(bounds, at, low, length):
    shape = (low.shape[0], LANES)
    bounds[0, at, :] = low - lax.broadcasted_iota(jnp.int32, shape, 1)
    bounds[1, at, :] = jnp.broadcast_to(length, shape)


def own_kernel(first_doc, shift, message, corpus, out, *scratch):
    docs, arrived, rows_q, bounds = scratch[:4]
    corpus = corpus.at[pl.ds(first_doc, docs.shape[0])]
    start_copies(corpus, docs, arrived)
    queries = message.shape[0] - META
    unit = identity(queries)
    columns = lax.dot_general(
        unit, message[queries:, 0:queries], NT, preferred_element_type=F32
    )

    def bound(k):
        value = columns[:, 2 * k : 2 * k + 1] * 256.0 + columns[:, 2 * k + 1 : 2 * k + 2]
        return jnp.clip(value.astype(jnp.int32) - (shift[0] + first_doc), 0, docs.shape[0])

    for w in range(2):
        at = slice(w * queries, (w + 1) * queries)
        low = bound(w)
        set_bounds(bounds, at, low, jnp.maximum(bound(2 + w) - low, 0))
        rows_q[at, :] = message[0:queries, :]
    stats = stats_matrix(
        attend_rows(
            scratch,
            arrived.shape[0],
            lambda i: (i, 0),
            lambda i: tile_copy(corpus, docs, arrived, i).wait(),
        )
    )
    out[0 : 2 * queries, :] = scratch[-1][...].astype(BF16)
    out[2 * queries :, :] = jnp.zeros((META, out.shape[1]), BF16)
    for w in range(2):
        at = slice(w * queries, (w + 1) * queries)
        out[2 * queries :, at] = lax.dot_general(
            stats[at, :], unit, TN, preferred_element_type=F32
        ).astype(BF16)


def own(shift, message, corpus, first_doc, docs):
    width = corpus.shape[1]
    queries = message.shape[0] - META
    tile = min(DOC_TILE, docs // 2)
    return pl.pallas_call(
        functools.partial(own_kernel, first_doc),
        out_shape=jax.ShapeDtypeStruct((2 * queries + META, width), BF16),
        in_specs=[SMEM, VMEM, HBM],
        out_specs=VMEM,
        scratch_shapes=row_scratch(2 * queries, 2 * queries, docs // tile, docs, width, tile),
        compiler_params=params(44),
        cost_estimate=pl.CostEstimate(
            flops=8 * queries * docs * width if first_doc == 0 else 0,
            bytes_accessed=docs * width * 2 if first_doc == 0 else 0,
            transcendentals=0,
        ),
        name="own_block",
    )(shift, message, corpus)


def side_kernel(shift, message, corpus, out, pooled, *scratch):
    docs, arrived, rows_q, bounds = scratch[:4]
    start_copies(corpus, docs, arrived)
    queries = message.shape[0] - META
    group = rows_q.shape[0]
    meta = message[queries:, 0:queries].astype(F32)

    def bound(k):
        value = meta[2 * k : 2 * k + 1, :] * 256.0 + meta[2 * k + 1 : 2 * k + 2, :]
        return jnp.clip(value.astype(jnp.int32) - shift[0], 0, docs.shape[0])

    lows = [bound(w) for w in range(2)]
    lengths = [jnp.maximum(bound(2 + w) - low, 0) for w, low in enumerate(lows)]
    parts = []
    for low, length in zip(lows, lengths):
        lines = [*split_int(low), *split_int(length), jnp.zeros((META - 4, queries), F32)]
        parts.append(jnp.concatenate(lines, axis=0).astype(BF16))
    flags = [(length > 0).astype(F32) for length in lengths]
    stacked = jnp.concatenate(flags + [jnp.zeros((META - 2, queries), F32)], axis=0).astype(BF16)
    before = lax.broadcasted_iota(jnp.int32, (queries, queries), 0) < lax.broadcasted_iota(
        jnp.int32, (queries, queries), 1
    )
    ranks = jnp.dot(stacked, before.astype(F32).astype(BF16), preferred_element_type=F32)
    held = jnp.sum(flags[0], axis=1, keepdims=True)
    places = [
        jnp.where(flag > 0, ranks[w : w + 1, :] + w * held, -1.0).astype(jnp.int32)
        for w, flag in enumerate(flags)
    ]
    active = jnp.sum(flags[0] + flags[1]).astype(jnp.int32)
    out[...] = jnp.zeros(out.shape, BF16)

    def work(g, carry):
        row = lax.broadcasted_iota(jnp.int32, (group, queries), 0) + g * group
        pick = [(row == place).astype(F32).astype(BF16) for place in places]
        rows_q[...] = jnp.dot(
            pick[0] + pick[1], message[0:queries, :], preferred_element_type=F32
        ).astype(BF16)
        columns = sum(
            lax.dot_general(chosen, part, NT, preferred_element_type=F32) for chosen, part in zip(pick, parts)
        )
        low = (columns[:, 0:1] * 256.0 + columns[:, 1:2]).astype(jnp.int32)
        length = (columns[:, 2:3] * 256.0 + columns[:, 3:4]).astype(jnp.int32)
        set_bounds(bounds, slice(0, group), low, length)

        def ready(i):
            @pl.when(g == 0)
            def _():
                tile_copy(corpus, docs, arrived, i).wait()

        stats = stats_matrix(attend_rows(scratch, arrived.shape[0], lambda i: (i, 0), ready))
        pooled[...] = scratch[-1][...].astype(BF16)
        for w, chosen in enumerate(pick):
            at = slice(w * queries, (w + 1) * queries)
            out[at, :] += lax.dot_general(chosen, pooled[...], TN, preferred_element_type=F32).astype(BF16)
            out[2 * queries :, at] += lax.dot_general(
                stats, chosen, TN, preferred_element_type=F32
            ).astype(BF16)
        return carry

    lax.fori_loop(0, jnp.maximum((active + group - 1) // group, 1), work, 0)


def side(shift, message, corpus):
    docs, width = corpus.shape
    queries = message.shape[0] - META
    tile = min(DOC_TILE, docs // 2)
    group = min(2 * queries, (queries + queries // 4) // ROW_TILE * ROW_TILE)
    return pl.pallas_call(
        side_kernel,
        out_shape=jax.ShapeDtypeStruct((2 * queries + META, width), BF16),
        in_specs=[SMEM, VMEM, HBM],
        out_specs=VMEM,
        scratch_shapes=[pltpu.VMEM((group, width), BF16)]
        + row_scratch(group, group, docs // tile, docs, width, tile),
        compiler_params=params(44),
        cost_estimate=pl.CostEstimate(
            flops=5 * queries * docs * width,
            bytes_accessed=docs * width * 2,
            transcendentals=queries * docs,
        ),
        name="side_block",
    )(shift, message, corpus)


def pack_kernel(base, queries, starts, ends, out):
    rows, width = queries.shape
    out[0:rows, :] = queries[...]
    out[rows:, :] = jnp.zeros((META, width), BF16)
    parts = [split_int(lines[...] - base[0]) for lines in (starts, ends)]
    lines = [part[w : w + 1, :] for pair in parts for w in range(2) for part in pair]
    lines.append(jnp.zeros((META - 8, rows), F32))
    out[rows:, 0:rows] = jnp.concatenate(lines, axis=0).astype(BF16)


def pack(base, queries, starts, ends):
    rows, width = queries.shape
    return pl.pallas_call(
        pack_kernel,
        out_shape=jax.ShapeDtypeStruct((rows + META, width), BF16),
        in_specs=[SMEM, VMEM, VMEM, VMEM],
        out_specs=VMEM,
        compiler_params=params(4),
        name="pack",
    )(base, queries, starts, ends)


def columns_of(state, unit, w):
    queries = unit.shape[0]
    lines = state[2 * queries :, w * queries : (w + 1) * queries]
    columns = lax.dot_general(unit, lines, NT, preferred_element_type=F32)
    top, total, score_sum = (
        columns[:, 3 * k : 3 * k + 1] + columns[:, 3 * k + 1 : 3 * k + 2] + columns[:, 3 * k + 2 : 3 * k + 3]
        for k in range(3)
    )
    return jnp.where(total > 0, top, NEG), total, score_sum


def weigh_states(tops):
    best = functools.reduce(jnp.maximum, tops)
    return best, [jnp.exp(top - best) for top in tops]


def merge_kernel(first, second, out):
    queries = (first.shape[0] - META) // 2
    unit = identity(queries)
    out[2 * queries :, :] = jnp.zeros((META, out.shape[1]), BF16)
    for w in range(2):
        at = slice(w * queries, (w + 1) * queries)
        states = [columns_of(state, unit, w) for state in (first, second)]
        best, factors = weigh_states([state[0] for state in states])
        total = functools.reduce(jnp.add, [f * state[1] for f, state in zip(factors, states)])
        score_sum = states[0][2] + states[1][2]
        out[at, :] = (
            factors[0] * first[at, :].astype(F32) + factors[1] * second[at, :].astype(F32)
        ).astype(BF16)
        stats = stats_matrix((best, total, score_sum))
        out[2 * queries :, at] = lax.dot_general(
            stats, unit, TN, preferred_element_type=F32
        ).astype(BF16)


def merge(first, second):
    return pl.pallas_call(
        merge_kernel,
        out_shape=jax.ShapeDtypeStruct(first.shape, BF16),
        in_specs=[VMEM, VMEM],
        out_specs=VMEM,
        compiler_params=params(8),
        name="merge",
    )(first, second)


def finish_kernel(window_start, window_end, first, second, third, fourth_a, fourth_b, pooled, log_mass, mean_score):
    queries = window_start.shape[1]
    unit = identity(queries)
    members = (first[...], second[...], third[...], fourth_a[...] + fourth_b[...])
    for w in range(2):
        at = slice(w * queries, (w + 1) * queries)
        states = [columns_of(member, unit, w) for member in members]
        _, factors = weigh_states([state[0] for state in states])
        total = functools.reduce(jnp.add, [f * state[1] for f, state in zip(factors, states)])
        weighted = functools.reduce(
            jnp.add, [f * member[at, :].astype(F32) for f, member in zip(factors, members)]
        )
        pooled[:, w, :] = (weighted / total).astype(BF16)

        lines = [member[2 * queries :, at].astype(F32) for member in members]
        tops, totals, sums = (
            [line[3 * k : 3 * k + 1, :] + line[3 * k + 1 : 3 * k + 2, :] + line[3 * k + 2 : 3 * k + 3, :] for line in lines]
            for k in range(3)
        )
        best, factors = weigh_states([jnp.where(t > 0, top, NEG) for top, t in zip(tops, totals)])
        total = functools.reduce(jnp.add, [f * t for f, t in zip(factors, totals)])
        log_mass[w : w + 1, :] = best + jnp.log(total)
        count = (window_end[w : w + 1, :] - window_start[w : w + 1, :]).astype(F32)
        mean_score[w : w + 1, :] = functools.reduce(jnp.add, sums) / count


def finish(window_start, window_end, *members):
    queries = window_start.shape[1]
    width = members[0].shape[1]
    line = jax.ShapeDtypeStruct((2, queries), F32)
    return pl.pallas_call(
        finish_kernel,
        out_shape=(jax.ShapeDtypeStruct((queries, 2, width), BF16), line, line),
        in_specs=[VMEM] * 7,
        out_specs=(VMEM, VMEM, VMEM),
        compiler_params=params(8),
        name="finish",
    )(window_start, window_end, *members)


def local(queries, corpus, window_start, window_end):
    docs = corpus.shape[0]
    size = lax.axis_size(AXES)
    position = lax.axis_index(AXES)
    across = [(i, i ^ 1) for i in range(size)]
    past = [(i, i + 1) for i in range(1, size - 1, 2)] + [(i + 1, i) for i in range(1, size - 1, 2)]
    between = [(i, i + 1) for i in range(3, size - 1, 4)] + [(i + 1, i) for i in range(3, size - 1, 4)]
    relay = [(i + 2, i) for i in range(0, size, 4)] + [(i + 1, i + 3) for i in range(0, size, 4)]
    outward = [(i + 1, i) for i in range(0, size, 4)] + [(i + 2, i + 3) for i in range(0, size, 4)]
    inward = [(target, source) for source, target in outward]
    odd = position % 2

    starts, ends = window_start.T, window_end.T
    base = jnp.full((1,), (position - 1) * docs, jnp.int32)
    message = pack(base, queries, starts, ends)
    near = lax.ppermute(message, AXES, across)
    far = lax.ppermute(message, AXES, past)
    shift = jnp.full((1,), docs, jnp.int32)
    early = docs // 2
    own_early = own(shift, message, corpus, 0, early)
    near, _ = lax.optimization_barrier((near, own_early))
    near_part = side(jnp.full((1,), 2 * docs * odd, jnp.int32), near, corpus)
    near_back_a = lax.ppermute(near_part, AXES, outward)
    far, _ = lax.optimization_barrier((far, near_part))
    far_part = side(jnp.full((1,), 2 * docs * (1 - odd), jnp.int32), far, corpus)
    far_back = lax.ppermute(far_part, AXES, between)
    merged = merge(near_part, lax.ppermute(far_part, AXES, relay))
    near_back_b = lax.ppermute(merged, AXES, inward)
    message, _ = lax.optimization_barrier((message, merged))
    own_late = own(shift, message, corpus, early, docs - early)
    pooled, log_mass, mean_score = finish(starts, ends, own_early, own_late, far_back, near_back_a, near_back_b)
    return pooled, log_mass.T, mean_score.T


def solution(mesh):
    placed = P(AXES, None)
    return jax.shard_map(
        local,
        mesh=mesh,
        in_specs=(placed,) * 4,
        out_specs=(P(AXES, None, None), placed, placed),
        check_vma=False,
    )
```

```python
import functools
import math

import jax
import jax.numpy as jnp
from jax import lax
from jax.experimental import pallas as pl
from jax.experimental.pallas import tpu as pltpu
from jax.sharding import PartitionSpec as P

SCORE_SCALE = 3.0
NEG = -1e30
LOG2E = math.log2(math.e)
AXES = ("tm", "pb")
BF16 = jnp.bfloat16
F32 = jnp.float32
NT = (((1,), (1,)), ((), ()))
TN = (((0,), (0,)), ((), ()))
META = 16
LANES = 128
DOC_TILE = 1024
SUBLANES = 8
CHUNK = 32

VMEM = pl.BlockSpec(memory_space=pltpu.VMEM)
SMEM = pl.BlockSpec(memory_space=pltpu.SMEM)
HBM = pl.BlockSpec(memory_space=pltpu.HBM)


def params(mebibytes):
    return pltpu.CompilerParams(vmem_limit_bytes=mebibytes * 2**20)


def identity(n):
    rows = lax.broadcasted_iota(jnp.int32, (n, n), 0)
    return (rows == lax.broadcasted_iota(jnp.int32, (n, n), 1)).astype(BF16)


def split_int(value):
    return (value >> 8).astype(F32), (value & 255).astype(F32)


def split_float(value):
    high = value.astype(BF16).astype(F32)
    rest = value - high
    middle = rest.astype(BF16).astype(F32)
    return high, middle, rest - middle


def row_scratch(rows, docs, width, tile):
    groups = rows // LANES
    return [
        pltpu.VMEM((docs, width), BF16),
        pltpu.SemaphoreType.DMA((docs // tile,)),
        pltpu.VMEM((rows, width), BF16),
        pltpu.VMEM((groups, SUBLANES, LANES), jnp.int32),
        pltpu.VMEM((groups, SUBLANES, LANES), jnp.int32),
        pltpu.VMEM((groups, SUBLANES, LANES), F32),
        pltpu.VMEM((groups, SUBLANES, LANES), F32),
        pltpu.VMEM((groups, SUBLANES, LANES), F32),
        pltpu.VMEM((tile, 2 * LANES), F32),
        pltpu.VMEM((tile, 2 * LANES), F32),
        pltpu.VMEM((docs, 2 * LANES), F32),
        pltpu.VMEM((tile, 2 * LANES), BF16),
        pltpu.VMEM((tile, 2 * LANES), BF16),
        pltpu.VMEM((rows, width), F32),
    ]


def tile_copy(corpus, docs, arrived, t):
    tile = docs.shape[0] // arrived.shape[0]
    at = pl.ds(t * tile, tile)
    return pltpu.make_async_copy(corpus.at[at], docs.at[at], arrived.at[t])


def start_copies(corpus, docs, arrived):
    for t in range(arrived.shape[0]):
        tile_copy(corpus, docs, arrived, t).start()


def fold(values, op):
    return op(values.reshape(values.shape[0] // SUBLANES, SUBLANES, values.shape[1]), axis=0)


def set_bounds(scratch, low, length):
    lows, lengths = scratch[3:5]
    for g in range(lows.shape[0]):
        at = slice(g * LANES, (g + 1) * LANES)
        lows[g] = jnp.broadcast_to(low[:, at], (SUBLANES, LANES))
        lengths[g] = jnp.broadcast_to(length[:, at], (SUBLANES, LANES))


def attend_rows(scratch, corpus, step):
    docs, arrived, rows_q, lows, lengths, peak, score_sum, mass, s_a, s_b, masked, p_a, p_b, acc = scratch
    n_docs, width = docs.shape
    tile = s_a.shape[0]
    tiles = n_docs // tile
    scale = SCORE_SCALE / math.sqrt(width)

    def first_group(t):
        if isinstance(t, int):
            return step if t >= tiles // 2 else 0
        return jnp.where(t >= tiles // 2, step, 0)

    def met_rows(t):
        first = first_group(t)
        if isinstance(first, int):
            return slice(first * LANES, (first + 2) * LANES)
        return pl.ds(pl.multiple_of(first * LANES, LANES), 2 * LANES)

    def wide(ref, g):
        return jnp.broadcast_to(ref[g][0:1, :], (CHUNK, LANES))

    def score(t):
        tile_copy(corpus, docs, arrived, t).wait()
        (s_a, s_b)[t % 2][...] = lax.dot_general(
            docs[t * tile : (t + 1) * tile, :], rows_q[met_rows(t), :], NT, preferred_element_type=F32
        )

    def scan(t):
        scores = (s_a, s_b)[t % 2]
        down = lax.broadcasted_iota(jnp.int32, (CHUNK, LANES), 0)
        for side in range(2):
            g = first_group(t) + side
            at = slice(side * LANES, (side + 1) * LANES)
            offset = down - wide(lows, g)
            length = wide(lengths, g).astype(jnp.uint32)
            top, total = peak[g], score_sum[g]
            for c in range(0, tile, CHUNK):
                value = scores[c : c + CHUNK, at]
                inside = (offset + (t * tile + c)).astype(jnp.uint32) < length
                kept = jnp.where(inside, value, NEG)
                top = jnp.maximum(top, fold(kept, jnp.max))
                total = total + fold(jnp.where(inside, value, 0.0), jnp.sum)
                masked[t * tile + c : t * tile + c + CHUNK, at] = kept
            peak[g] = top
            score_sum[g] = total

    peak[...] = jnp.full(peak.shape, NEG, F32)
    score_sum[...] = jnp.zeros(score_sum.shape, F32)
    mass[...] = jnp.zeros(mass.shape, F32)
    acc[...] = jnp.zeros(acc.shape, F32)
    score(0)
    for t in range(tiles):
        if t + 1 < tiles:
            score(t + 1)
        scan(t)
    groups = range(peak.shape[0])
    tops = [jnp.max(peak[g], axis=0, keepdims=True) for g in groups]
    for g in groups:
        peak[g] = jnp.broadcast_to(jnp.maximum(tops[g], 0.5 * NEG), (SUBLANES, LANES))

    def weigh(t, out):
        for side in range(2):
            g = first_group(t) + side
            at = slice(side * LANES, (side + 1) * LANES)
            shift, total = wide(peak, g), mass[g]
            for c in range(0, tile, CHUNK):
                value = masked[pl.ds(pl.multiple_of(t * tile + c, CHUNK), CHUNK), at]
                p = jnp.exp2((value - shift) * (scale * LOG2E))
                total = total + fold(p, jnp.sum)
                out[c : c + CHUNK, at] = p.astype(BF16)
            mass[g] = total

    def pool(t, weights):
        block = docs[pl.ds(pl.multiple_of(t * tile, tile), tile), :]
        acc[met_rows(t), :] += lax.dot_general(weights[...], block, TN, preferred_element_type=F32)

    weigh(0, p_a)

    def second_step(k, carry):
        t = 2 * k + 1
        pool(t - 1, p_a)
        weigh(t, p_b)
        pool(t, p_b)
        weigh(t + 1, p_a)
        return carry

    lax.fori_loop(0, tiles // 2 - 1, second_step, 0)
    pool(tiles - 2, p_a)
    weigh(tiles - 1, p_b)
    pool(tiles - 1, p_b)

    def line(parts):
        return jnp.concatenate(parts, axis=1)

    return (
        line(tops) * scale,
        line([jnp.sum(mass[g], axis=0, keepdims=True) for g in groups]),
        line([jnp.sum(score_sum[g], axis=0, keepdims=True) for g in groups]) * scale,
    )


def stats_lines(stats):
    lines = [part for value in stats for part in split_float(value)]
    lines.append(jnp.zeros((META - len(lines), stats[0].shape[1]), F32))
    return jnp.concatenate(lines, axis=0).astype(BF16)


def bound_lines(meta, shift, n_docs):
    meta = meta.astype(F32)

    def bound(k):
        value = meta[2 * k : 2 * k + 1, :] * 256.0 + meta[2 * k + 1 : 2 * k + 2, :]
        return jnp.clip(value.astype(jnp.int32) - shift, 0, n_docs)

    lows = [bound(w) for w in range(2)]
    return lows, [jnp.maximum(bound(2 + w) - low, 0) for w, low in enumerate(lows)]


def own_kernel(shift, message, corpus, out, *scratch):
    docs, arrived, rows_q = scratch[:3]
    start_copies(corpus, docs, arrived)
    queries = message.shape[0] - META
    lows, lengths = bound_lines(message[queries:, 0:queries], shift[0], docs.shape[0])
    set_bounds(scratch, jnp.concatenate(lows, axis=1), jnp.concatenate(lengths, axis=1))
    for w in range(2):
        rows_q[w * queries : (w + 1) * queries, :] = message[0:queries, :]
    stats = attend_rows(scratch, corpus, 0)
    out[0 : 2 * queries, :] = scratch[-1][...].astype(BF16)
    out[2 * queries :, :] = jnp.zeros((META, out.shape[1]), BF16)
    out[2 * queries :, 0 : 2 * queries] = stats_lines(stats)


def own(shift, message, corpus):
    docs, width = corpus.shape
    queries = message.shape[0] - META
    tile = min(DOC_TILE, docs // 2)
    return pl.pallas_call(
        own_kernel,
        out_shape=jax.ShapeDtypeStruct((2 * queries + META, width), BF16),
        in_specs=[SMEM, VMEM, HBM],
        out_specs=VMEM,
        scratch_shapes=row_scratch(2 * queries, docs, width, tile),
        compiler_params=params(44),
        cost_estimate=pl.CostEstimate(
            flops=8 * queries * docs * width,
            bytes_accessed=docs * width * 2,
            transcendentals=2 * queries * docs,
        ),
        name="own_block",
    )(shift, message, corpus)


def neighbour_kernel(shifts, near, far_a, far_b, corpus, near_out, far_out, both_q, pooled, *scratch):
    docs, arrived, rows_q = scratch[:3]
    start_copies(corpus, docs, arrived)
    queries = near.shape[0] - META
    n_docs = docs.shape[0]
    held = rows_q.shape[0]
    centre = held // 2
    both_q[0:queries, :] = near[0:queries, :]
    both_q[queries:, :] = far_a[0:queries, :] + far_b[0:queries, :]
    metas = (near[queries:, 0:queries], far_a[queries:, 0:queries] + far_b[queries:, 0:queries])
    lows, lengths = [], []
    for side, meta in enumerate(metas):
        low, length = bound_lines(meta, shifts[side], n_docs)
        lows += low
        lengths += length
    blocks = len(lows)
    rows = blocks * queries

    keys = [
        jnp.where(length > 0, jnp.where(low == 0, length, n_docs + low), 2 * n_docs)
        for low, length in zip(lows, lengths)
    ]
    parts = []
    for low, length, key in zip(lows, lengths, keys):
        lines = [*split_int(low), *split_int(length), *split_int(key), jnp.zeros((META - 6, queries), F32)]
        parts.append(jnp.concatenate(lines, axis=0).astype(BF16))
    unit = identity(queries)
    lane = lax.broadcasted_iota(jnp.int32, (1, queries), 1)
    line = lax.broadcasted_iota(jnp.int32, (queries, 1), 0)
    ordered = [keys[b] * rows + (lane + b * queries) for b in range(blocks)]
    ranks = [jnp.zeros((1, queries), F32)] * blocks
    for a in range(blocks):
        columns = lax.dot_general(unit, parts[a], NT, preferred_element_type=F32)
        key = (columns[:, 4:5] * 256.0 + columns[:, 5:6]).astype(jnp.int32)
        key = jnp.broadcast_to(key * rows + (line + a * queries), (queries, queries))
        for b in range(blocks):
            ranks[b] = ranks[b] + jnp.sum((key < ordered[b]).astype(F32), axis=0, keepdims=True)
    opened = jnp.zeros((1, 1), F32)
    for low, length in zip(lows, lengths):
        opened = opened + jnp.sum(((length > 0) & (low == 0)).astype(F32), axis=1, keepdims=True)
    places, misfits = [], jnp.zeros((1, 1), F32)
    half = n_docs // 2
    for low, length, rank in zip(lows, lengths, ranks):
        place = (rank + (centre - opened)).astype(jnp.int32)
        bad = (place < 0) | (place >= held)
        bad = bad | ((place < LANES) & (low + length > half)) | ((place >= 2 * LANES) & (low < half))
        misfits = misfits + jnp.sum(((length > 0) & bad).astype(F32), axis=1, keepdims=True)
        places.append(jnp.where(length > 0, place, -1))
    fits = jnp.max(misfits) == 0.0
    passes = jnp.where(fits, 1, 2)
    step = jnp.where(fits, held // LANES - 2, 0)

    near_out[...] = jnp.zeros(near_out.shape, BF16)
    far_out[...] = jnp.zeros(far_out.shape, BF16)

    def work(turn, carry):
        row = lax.broadcasted_iota(jnp.int32, (held, queries), 0)
        pick = []
        for b in range(blocks):
            plain = jnp.where(turn == b // 2, lane + (b % 2) * queries, -1)
            place = jnp.where(fits, places[b], plain)
            pick.append((row == place).astype(F32).astype(BF16))
        of_query = jnp.concatenate([pick[0] + pick[1], pick[2] + pick[3]], axis=1)
        rows_q[...] = jnp.dot(of_query, both_q[...], preferred_element_type=F32).astype(BF16)
        lines = sum(
            lax.dot_general(part, chosen, NT, preferred_element_type=F32) for part, chosen in zip(parts, pick)
        )
        set_bounds(
            scratch,
            (lines[0:1, :] * 256.0 + lines[1:2, :]).astype(jnp.int32),
            (lines[2:3, :] * 256.0 + lines[3:4, :]).astype(jnp.int32),
        )
        stats = stats_lines(attend_rows(scratch, corpus, step))
        pooled[...] = scratch[-1][...].astype(BF16)
        for b, chosen in enumerate(pick):
            out = (near_out, far_out)[b // 2]
            at = slice((b % 2) * queries, (b % 2 + 1) * queries)
            out[at, :] += lax.dot_general(chosen, pooled[...], TN, preferred_element_type=F32).astype(BF16)
            out[2 * queries :, at] += jnp.dot(stats, chosen, preferred_element_type=F32).astype(BF16)

        @pl.when(turn + 1 < passes)
        def _():
            start_copies(corpus, docs, arrived)

        return carry

    lax.fori_loop(0, passes, work, 0)


def neighbours(shifts, near, far_a, far_b, corpus):
    docs, width = corpus.shape
    queries = near.shape[0] - META
    held = 3 * LANES
    tile = min(DOC_TILE, docs // 2)
    result = jax.ShapeDtypeStruct((2 * queries + META, width), BF16)
    return pl.pallas_call(
        neighbour_kernel,
        out_shape=(result, result),
        in_specs=[SMEM, VMEM, VMEM, VMEM, HBM],
        out_specs=(VMEM, VMEM),
        scratch_shapes=[pltpu.VMEM((2 * queries, width), BF16), pltpu.VMEM((held, width), BF16)]
        + row_scratch(held, docs, width, tile),
        compiler_params=params(44),
        cost_estimate=pl.CostEstimate(
            flops=8 * queries * docs * width,
            bytes_accessed=docs * width * 2,
            transcendentals=2 * queries * docs,
        ),
        name="neighbour_blocks",
    )(shifts, near, far_a, far_b, corpus)


def pack_kernel(base, queries, starts, ends, out):
    rows, width = queries.shape
    out[0:rows, :] = queries[...]
    out[rows:, :] = jnp.zeros((META, width), BF16)
    parts = [split_int(lines[...] - base[0]) for lines in (starts, ends)]
    lines = [part[w : w + 1, :] for pair in parts for w in range(2) for part in pair]
    lines.append(jnp.zeros((META - 8, rows), F32))
    out[rows:, 0:rows] = jnp.concatenate(lines, axis=0).astype(BF16)


def pack(base, queries, starts, ends):
    rows, width = queries.shape
    return pl.pallas_call(
        pack_kernel,
        out_shape=jax.ShapeDtypeStruct((rows + META, width), BF16),
        in_specs=[SMEM, VMEM, VMEM, VMEM],
        out_specs=VMEM,
        compiler_params=params(4),
        name="pack",
    )(base, queries, starts, ends)


def columns_of(state, unit, w):
    queries = unit.shape[0]
    lines = state[2 * queries :, w * queries : (w + 1) * queries]
    columns = lax.dot_general(unit, lines, NT, preferred_element_type=F32)
    top, total, score_sum = (
        columns[:, 3 * k : 3 * k + 1] + columns[:, 3 * k + 1 : 3 * k + 2] + columns[:, 3 * k + 2 : 3 * k + 3]
        for k in range(3)
    )
    return jnp.where(total > 0, top, NEG), total, score_sum


def weigh_states(tops):
    best = functools.reduce(jnp.maximum, tops)
    return best, [jnp.exp(top - best) for top in tops]


def stats_matrix(stats):
    rows = stats[0].shape[0]
    lane = lax.broadcasted_iota(jnp.int32, (rows, META), 1)
    matrix = jnp.zeros((rows, META), F32)
    for k, value in enumerate(stats):
        for j, part in enumerate(split_float(value)):
            matrix = jnp.where(lane == 3 * k + j, part, matrix)
    return matrix.astype(BF16)


def merge_kernel(first, second, out):
    queries = (first.shape[0] - META) // 2
    unit = identity(queries)
    out[2 * queries :, :] = jnp.zeros((META, out.shape[1]), BF16)
    for w in range(2):
        at = slice(w * queries, (w + 1) * queries)
        states = [columns_of(state, unit, w) for state in (first, second)]
        best, factors = weigh_states([state[0] for state in states])
        total = functools.reduce(jnp.add, [f * state[1] for f, state in zip(factors, states)])
        score_sum = states[0][2] + states[1][2]
        out[at, :] = (
            factors[0] * first[at, :].astype(F32) + factors[1] * second[at, :].astype(F32)
        ).astype(BF16)
        stats = stats_matrix((best, total, score_sum))
        out[2 * queries :, at] = lax.dot_general(
            stats, unit, TN, preferred_element_type=F32
        ).astype(BF16)


def merge(first, second):
    return pl.pallas_call(
        merge_kernel,
        out_shape=jax.ShapeDtypeStruct(first.shape, BF16),
        in_specs=[VMEM, VMEM],
        out_specs=VMEM,
        compiler_params=params(8),
        name="merge",
    )(first, second)


def finish_kernel(window_start, window_end, first, second, third, pooled, log_mass, mean_score):
    queries = window_start.shape[1]
    unit = identity(queries)
    members = (first, second, third)
    for w in range(2):
        at = slice(w * queries, (w + 1) * queries)
        states = [columns_of(member, unit, w) for member in members]
        _, factors = weigh_states([state[0] for state in states])
        total = functools.reduce(jnp.add, [f * state[1] for f, state in zip(factors, states)])
        weighted = functools.reduce(
            jnp.add, [f * member[at, :].astype(F32) for f, member in zip(factors, members)]
        )
        pooled[:, w, :] = (weighted / total).astype(BF16)

        lines = [member[2 * queries :, at].astype(F32) for member in members]
        tops, totals, sums = (
            [line[3 * k : 3 * k + 1, :] + line[3 * k + 1 : 3 * k + 2, :] + line[3 * k + 2 : 3 * k + 3, :] for line in lines]
            for k in range(3)
        )
        best, factors = weigh_states([jnp.where(t > 0, top, NEG) for top, t in zip(tops, totals)])
        total = functools.reduce(jnp.add, [f * t for f, t in zip(factors, totals)])
        log_mass[w : w + 1, :] = best + jnp.log(total)
        count = (window_end[w : w + 1, :] - window_start[w : w + 1, :]).astype(F32)
        mean_score[w : w + 1, :] = functools.reduce(jnp.add, sums) / count


def finish(window_start, window_end, *members):
    queries = window_start.shape[1]
    width = members[0].shape[1]
    line = jax.ShapeDtypeStruct((2, queries), F32)
    return pl.pallas_call(
        finish_kernel,
        out_shape=(jax.ShapeDtypeStruct((queries, 2, width), BF16), line, line),
        in_specs=[VMEM] * 5,
        out_specs=(VMEM, VMEM, VMEM),
        compiler_params=params(8),
        name="finish",
    )(window_start, window_end, *members)


def local(queries, corpus, window_start, window_end):
    docs = corpus.shape[0]
    size = lax.axis_size(AXES)
    position = lax.axis_index(AXES)
    across = [(i, i ^ 1) for i in range(size)]
    between = [(i, i + 1) for i in range(3, size - 1, 4)] + [(i + 1, i) for i in range(3, size - 1, 4)]
    relay = [(i, i + 2) for i in range(0, size, 4)] + [(i + 3, i + 1) for i in range(0, size, 4)]
    relay_back = [(target, source) for source, target in relay]
    odd = position % 2

    starts, ends = window_start.T, window_end.T
    base = jnp.full((1,), (position - 1) * docs, jnp.int32)
    message = pack(base, queries, starts, ends)
    near = lax.ppermute(message, AXES, across)
    far_a = lax.ppermute(message, AXES, between)
    far_b = lax.ppermute(near, AXES, relay)
    shifts = jnp.stack([2 * docs * odd, 2 * docs * (1 - odd)]).astype(jnp.int32)
    near_part, far_part = neighbours(shifts, near, far_a, far_b, corpus)
    far_back = lax.ppermute(far_part, AXES, between)
    relayed = lax.ppermute(far_part, AXES, relay_back)
    near_back = lax.ppermute(merge(near_part, relayed), AXES, across)
    message, _ = lax.optimization_barrier((message, far_part))
    own_part = own(jnp.full((1,), docs, jnp.int32), message, corpus)
    pooled, log_mass, mean_score = finish(starts, ends, own_part, near_back, far_back)
    return pooled, log_mass.T, mean_score.T


def solution(mesh):
    placed = P(AXES, None)
    return jax.shard_map(
        local,
        mesh=mesh,
        in_specs=(placed,) * 4,
        out_specs=(P(AXES, None, None), placed, placed),
        check_vma=False,
    )
```

```python
import functools
import math

import jax
import jax.numpy as jnp
from jax import lax
from jax.experimental import pallas as pl
from jax.experimental.pallas import tpu as pltpu
from jax.sharding import PartitionSpec as P

SCORE_SCALE = 3.0
NEG = -1e30
LOG2E = math.log2(math.e)
AXES = ("tm", "pb")
BF16 = jnp.bfloat16
F32 = jnp.float32
NT = (((1,), (1,)), ((), ()))
TN = (((0,), (0,)), ((), ()))
META = 16
LANES = 128
DOC_TILE = 1024
SUBLANES = 8
CHUNK = 32

VMEM = pl.BlockSpec(memory_space=pltpu.VMEM)
SMEM = pl.BlockSpec(memory_space=pltpu.SMEM)
HBM = pl.BlockSpec(memory_space=pltpu.HBM)


def params(mebibytes):
    return pltpu.CompilerParams(vmem_limit_bytes=mebibytes * 2**20)


def identity(n):
    rows = lax.broadcasted_iota(jnp.int32, (n, n), 0)
    return (rows == lax.broadcasted_iota(jnp.int32, (n, n), 1)).astype(BF16)


def split_int(value):
    return (value >> 8).astype(F32), (value & 255).astype(F32)


def split_float(value):
    high = value.astype(BF16).astype(F32)
    rest = value - high
    middle = rest.astype(BF16).astype(F32)
    return high, middle, rest - middle


def row_scratch(rows, docs, width, tile):
    groups = rows // LANES
    return [
        pltpu.VMEM((rows, width), BF16),
        pltpu.VMEM((groups, SUBLANES, LANES), jnp.int32),
        pltpu.VMEM((groups, SUBLANES, LANES), jnp.int32),
        pltpu.VMEM((groups, SUBLANES, LANES), F32),
        pltpu.VMEM((groups, SUBLANES, LANES), F32),
        pltpu.VMEM((groups, SUBLANES, LANES), F32),
        pltpu.VMEM((tile, 2 * LANES), F32),
        pltpu.VMEM((tile, 2 * LANES), F32),
        pltpu.VMEM((docs, 2 * LANES), F32),
        pltpu.VMEM((tile, 2 * LANES), BF16),
        pltpu.VMEM((tile, 2 * LANES), BF16),
        pltpu.VMEM((rows, width), F32),
    ]


def tile_copy(corpus, docs, arrived, t):
    tile = docs.shape[0] // arrived.shape[0]
    at = pl.ds(t * tile, tile)
    return pltpu.make_async_copy(corpus.at[at], docs.at[at], arrived.at[t])


def start_copies(corpus, docs, arrived):
    for t in range(arrived.shape[0]):
        tile_copy(corpus, docs, arrived, t).start()


def fold(values, op):
    return op(values.reshape(values.shape[0] // SUBLANES, SUBLANES, values.shape[1]), axis=0)


def set_bounds(scratch, low, length):
    lows, lengths = scratch[1:3]
    for g in range(lows.shape[0]):
        at = slice(g * LANES, (g + 1) * LANES)
        lows[g] = jnp.broadcast_to(low[:, at], (SUBLANES, LANES))
        lengths[g] = jnp.broadcast_to(length[:, at], (SUBLANES, LANES))


def attend_rows(docs, scratch, step, corpus=None, arrived=None):
    rows_q, lows, lengths, peak, score_sum, mass, s_a, s_b, masked, p_a, p_b, acc = scratch
    n_docs, width = docs.shape
    tile = s_a.shape[0]
    tiles = n_docs // tile
    scale = SCORE_SCALE / math.sqrt(width)

    def first_group(t):
        if isinstance(t, int):
            return step if t >= tiles // 2 else 0
        return jnp.where(t >= tiles // 2, step, 0)

    def met_rows(t):
        first = first_group(t)
        if isinstance(first, int):
            return slice(first * LANES, (first + 2) * LANES)
        return pl.ds(pl.multiple_of(first * LANES, LANES), 2 * LANES)

    def wide(ref, g):
        return jnp.broadcast_to(ref[g][0:1, :], (CHUNK, LANES))

    def score(t):
        if corpus is not None and t % (tiles // 2) == 0:
            for k in range(t, t + tiles // 2):
                tile_copy(corpus, docs, arrived, k).wait()
        (s_a, s_b)[t % 2][...] = lax.dot_general(
            docs[t * tile : (t + 1) * tile, :], rows_q[met_rows(t), :], NT, preferred_element_type=F32
        )

    def scan(t):
        scores = (s_a, s_b)[t % 2]
        down = lax.broadcasted_iota(jnp.int32, (CHUNK, LANES), 0)
        for side in range(2):
            g = first_group(t) + side
            at = slice(side * LANES, (side + 1) * LANES)
            offset = down - wide(lows, g)
            length = wide(lengths, g).astype(jnp.uint32)
            top, total = peak[g], score_sum[g]
            for c in range(0, tile, CHUNK):
                value = scores[c : c + CHUNK, at]
                inside = (offset + (t * tile + c)).astype(jnp.uint32) < length
                kept = jnp.where(inside, value, NEG)
                top = jnp.maximum(top, fold(kept, jnp.max))
                total = total + fold(jnp.where(inside, value, 0.0), jnp.sum)
                masked[t * tile + c : t * tile + c + CHUNK, at] = kept
            peak[g] = top
            score_sum[g] = total

    peak[...] = jnp.full(peak.shape, NEG, F32)
    score_sum[...] = jnp.zeros(score_sum.shape, F32)
    mass[...] = jnp.zeros(mass.shape, F32)
    acc[...] = jnp.zeros(acc.shape, F32)
    score(0)
    for t in range(tiles):
        if t + 1 < tiles:
            score(t + 1)
        scan(t)
    groups = range(peak.shape[0])
    tops = [jnp.max(peak[g], axis=0, keepdims=True) for g in groups]
    for g in groups:
        peak[g] = jnp.broadcast_to(jnp.maximum(tops[g], 0.5 * NEG), (SUBLANES, LANES))

    def weigh(t, out):
        for side in range(2):
            g = first_group(t) + side
            at = slice(side * LANES, (side + 1) * LANES)
            shift, total = wide(peak, g), mass[g]
            for c in range(0, tile, CHUNK):
                value = masked[pl.ds(pl.multiple_of(t * tile + c, CHUNK), CHUNK), at]
                p = jnp.exp2((value - shift) * (scale * LOG2E))
                total = total + fold(p, jnp.sum)
                out[c : c + CHUNK, at] = p.astype(BF16)
            mass[g] = total

    def pool(t, weights):
        block = docs[pl.ds(pl.multiple_of(t * tile, tile), tile), :]
        acc[met_rows(t), :] += lax.dot_general(weights[...], block, TN, preferred_element_type=F32)

    weigh(0, p_a)

    def second_step(k, carry):
        t = 2 * k + 1
        pool(t - 1, p_a)
        weigh(t, p_b)
        pool(t, p_b)
        weigh(t + 1, p_a)
        return carry

    lax.fori_loop(0, tiles // 2 - 1, second_step, 0)
    pool(tiles - 2, p_a)
    weigh(tiles - 1, p_b)
    pool(tiles - 1, p_b)

    def line(parts):
        return jnp.concatenate(parts, axis=1)

    return (
        line(tops) * scale,
        line([jnp.sum(mass[g], axis=0, keepdims=True) for g in groups]),
        line([jnp.sum(score_sum[g], axis=0, keepdims=True) for g in groups]) * scale,
    )


def stats_lines(stats):
    lines = [part for value in stats for part in split_float(value)]
    lines.append(jnp.zeros((META - len(lines), stats[0].shape[1]), F32))
    return jnp.concatenate(lines, axis=0).astype(BF16)


def bound_lines(meta, shift, n_docs):
    meta = meta.astype(F32)

    def bound(k):
        value = meta[2 * k : 2 * k + 1, :] * 256.0 + meta[2 * k + 1 : 2 * k + 2, :]
        return jnp.clip(value.astype(jnp.int32) - shift, 0, n_docs)

    lows = [bound(w) for w in range(2)]
    return lows, [jnp.maximum(bound(2 + w) - low, 0) for w, low in enumerate(lows)]


def own_kernel(shift, message, docs, out, *scratch):
    rows_q = scratch[0]
    queries = message.shape[0] - META
    lows, lengths = bound_lines(message[queries:, 0:queries], shift[0], docs.shape[0])
    set_bounds(scratch, jnp.concatenate(lows, axis=1), jnp.concatenate(lengths, axis=1))
    for w in range(2):
        rows_q[w * queries : (w + 1) * queries, :] = message[0:queries, :]
    stats = attend_rows(docs, scratch, 0)
    out[0 : 2 * queries, :] = scratch[-1][...].astype(BF16)
    out[2 * queries :, :] = jnp.zeros((META, out.shape[1]), BF16)
    out[2 * queries :, 0 : 2 * queries] = stats_lines(stats)


def own(shift, message, corpus):
    docs, width = corpus.shape
    queries = message.shape[0] - META
    tile = min(DOC_TILE, docs // 2)
    return pl.pallas_call(
        own_kernel,
        out_shape=jax.ShapeDtypeStruct((2 * queries + META, width), BF16),
        in_specs=[SMEM, VMEM, VMEM],
        out_specs=VMEM,
        scratch_shapes=row_scratch(2 * queries, docs, width, tile),
        compiler_params=params(16),
        cost_estimate=pl.CostEstimate(
            flops=8 * queries * docs * width,
            bytes_accessed=docs * width * 2,
            transcendentals=2 * queries * docs,
        ),
        name="own_block",
    )(shift, message, corpus)


def neighbour_kernel(shifts, near, far_a, far_b, corpus, near_out, far_out, docs, arrived, both_q, pooled, *scratch):
    rows_q = scratch[0]
    start_copies(corpus, docs, arrived)
    queries = near.shape[0] - META
    n_docs = docs.shape[0]
    held = rows_q.shape[0]
    centre = held // 2
    both_q[0:queries, :] = near[0:queries, :]
    both_q[queries:, :] = far_a[0:queries, :] + far_b[0:queries, :]
    metas = (near[queries:, 0:queries], far_a[queries:, 0:queries] + far_b[queries:, 0:queries])
    lows, lengths = [], []
    for side, meta in enumerate(metas):
        low, length = bound_lines(meta, shifts[side], n_docs)
        lows += low
        lengths += length
    blocks = len(lows)
    rows = blocks * queries

    keys = [
        jnp.where(length > 0, jnp.where(low == 0, length, n_docs + low), 2 * n_docs)
        for low, length in zip(lows, lengths)
    ]
    parts = []
    for low, length, key in zip(lows, lengths, keys):
        lines = [*split_int(low), *split_int(length), *split_int(key), jnp.zeros((META - 6, queries), F32)]
        parts.append(jnp.concatenate(lines, axis=0).astype(BF16))
    unit = identity(queries)
    lane = lax.broadcasted_iota(jnp.int32, (1, queries), 1)
    line = lax.broadcasted_iota(jnp.int32, (queries, 1), 0)
    ordered = [keys[b] * rows + (lane + b * queries) for b in range(blocks)]
    ranks = [jnp.zeros((1, queries), F32)] * blocks
    for a in range(blocks):
        columns = lax.dot_general(unit, parts[a], NT, preferred_element_type=F32)
        key = (columns[:, 4:5] * 256.0 + columns[:, 5:6]).astype(jnp.int32)
        key = jnp.broadcast_to(key * rows + (line + a * queries), (queries, queries))
        for b in range(blocks):
            ranks[b] = ranks[b] + jnp.sum((key < ordered[b]).astype(F32), axis=0, keepdims=True)
    opened = jnp.zeros((1, 1), F32)
    for low, length in zip(lows, lengths):
        opened = opened + jnp.sum(((length > 0) & (low == 0)).astype(F32), axis=1, keepdims=True)
    places, misfits = [], jnp.zeros((1, 1), F32)
    half = n_docs // 2
    for low, length, rank in zip(lows, lengths, ranks):
        place = (rank + (centre - opened)).astype(jnp.int32)
        bad = (place < 0) | (place >= held)
        bad = bad | ((place < LANES) & (low + length > half)) | ((place >= 2 * LANES) & (low < half))
        misfits = misfits + jnp.sum(((length > 0) & bad).astype(F32), axis=1, keepdims=True)
        places.append(jnp.where(length > 0, place, -1))
    fits = jnp.max(misfits) == 0.0
    passes = jnp.where(fits, 1, 2)
    step = jnp.where(fits, held // LANES - 2, 0)

    near_out[...] = jnp.zeros(near_out.shape, BF16)
    far_out[...] = jnp.zeros(far_out.shape, BF16)

    def work(turn, carry):
        row = lax.broadcasted_iota(jnp.int32, (held, queries), 0)
        pick = []
        for b in range(blocks):
            plain = jnp.where(turn == b // 2, lane + (b % 2) * queries, -1)
            place = jnp.where(fits, places[b], plain)
            pick.append((row == place).astype(F32).astype(BF16))
        of_query = jnp.concatenate([pick[0] + pick[1], pick[2] + pick[3]], axis=1)
        rows_q[...] = jnp.dot(of_query, both_q[...], preferred_element_type=F32).astype(BF16)
        lines = sum(
            lax.dot_general(part, chosen, NT, preferred_element_type=F32) for part, chosen in zip(parts, pick)
        )
        set_bounds(
            scratch,
            (lines[0:1, :] * 256.0 + lines[1:2, :]).astype(jnp.int32),
            (lines[2:3, :] * 256.0 + lines[3:4, :]).astype(jnp.int32),
        )
        stats = stats_lines(attend_rows(docs, scratch, step, corpus, arrived))
        pooled[...] = scratch[-1][...].astype(BF16)
        for b, chosen in enumerate(pick):
            out = (near_out, far_out)[b // 2]
            at = slice((b % 2) * queries, (b % 2 + 1) * queries)
            out[at, :] += lax.dot_general(chosen, pooled[...], TN, preferred_element_type=F32).astype(BF16)
            out[2 * queries :, at] += jnp.dot(stats, chosen, preferred_element_type=F32).astype(BF16)

        @pl.when(turn + 1 < passes)
        def _():
            start_copies(corpus, docs, arrived)

        return carry

    lax.fori_loop(0, passes, work, 0)


def neighbours(shifts, near, far_a, far_b, corpus):
    docs, width = corpus.shape
    queries = near.shape[0] - META
    held = 3 * LANES
    tile = min(DOC_TILE, docs // 2)
    result = jax.ShapeDtypeStruct((2 * queries + META, width), BF16)
    return pl.pallas_call(
        neighbour_kernel,
        out_shape=(result, result),
        in_specs=[SMEM, VMEM, VMEM, VMEM, HBM],
        out_specs=(VMEM, VMEM),
        scratch_shapes=[
            pltpu.VMEM((docs, width), BF16),
            pltpu.SemaphoreType.DMA((docs // tile,)),
            pltpu.VMEM((2 * queries, width), BF16),
            pltpu.VMEM((held, width), BF16),
        ]
        + row_scratch(held, docs, width, tile),
        compiler_params=params(30),
        cost_estimate=pl.CostEstimate(
            flops=8 * queries * docs * width,
            bytes_accessed=docs * width * 2,
            transcendentals=2 * queries * docs,
        ),
        name="neighbour_blocks",
    )(shifts, near, far_a, far_b, corpus)


def pack_kernel(base, queries, starts, ends, out):
    rows, width = queries.shape
    out[0:rows, :] = queries[...]
    out[rows:, :] = jnp.zeros((META, width), BF16)
    parts = [split_int(lines[...] - base[0]) for lines in (starts, ends)]
    lines = [part[w : w + 1, :] for pair in parts for w in range(2) for part in pair]
    lines.append(jnp.zeros((META - 8, rows), F32))
    out[rows:, 0:rows] = jnp.concatenate(lines, axis=0).astype(BF16)


def pack(base, queries, starts, ends):
    rows, width = queries.shape
    return pl.pallas_call(
        pack_kernel,
        out_shape=jax.ShapeDtypeStruct((rows + META, width), BF16),
        in_specs=[SMEM, VMEM, VMEM, VMEM],
        out_specs=VMEM,
        compiler_params=params(4),
        name="pack",
    )(base, queries, starts, ends)


def columns_of(state, unit, w):
    queries = unit.shape[0]
    lines = state[2 * queries :, w * queries : (w + 1) * queries]
    columns = lax.dot_general(unit, lines, NT, preferred_element_type=F32)
    top, total, score_sum = (
        columns[:, 3 * k : 3 * k + 1] + columns[:, 3 * k + 1 : 3 * k + 2] + columns[:, 3 * k + 2 : 3 * k + 3]
        for k in range(3)
    )
    return jnp.where(total > 0, top, NEG), total, score_sum


def weigh_states(tops):
    best = functools.reduce(jnp.maximum, tops)
    return best, [jnp.exp(top - best) for top in tops]


def stats_matrix(stats):
    rows = stats[0].shape[0]
    lane = lax.broadcasted_iota(jnp.int32, (rows, META), 1)
    matrix = jnp.zeros((rows, META), F32)
    for k, value in enumerate(stats):
        for j, part in enumerate(split_float(value)):
            matrix = jnp.where(lane == 3 * k + j, part, matrix)
    return matrix.astype(BF16)


def merge_kernel(first, second, out):
    queries = (first.shape[0] - META) // 2
    unit = identity(queries)
    out[2 * queries :, :] = jnp.zeros((META, out.shape[1]), BF16)
    for w in range(2):
        at = slice(w * queries, (w + 1) * queries)
        states = [columns_of(state, unit, w) for state in (first, second)]
        best, factors = weigh_states([state[0] for state in states])
        total = functools.reduce(jnp.add, [f * state[1] for f, state in zip(factors, states)])
        score_sum = states[0][2] + states[1][2]
        out[at, :] = (
            factors[0] * first[at, :].astype(F32) + factors[1] * second[at, :].astype(F32)
        ).astype(BF16)
        stats = stats_matrix((best, total, score_sum))
        out[2 * queries :, at] = lax.dot_general(
            stats, unit, TN, preferred_element_type=F32
        ).astype(BF16)


def merge(first, second):
    return pl.pallas_call(
        merge_kernel,
        out_shape=jax.ShapeDtypeStruct(first.shape, BF16),
        in_specs=[VMEM, VMEM],
        out_specs=VMEM,
        compiler_params=params(8),
        name="merge",
    )(first, second)


def finish_kernel(window_start, window_end, first, second, third, pooled, log_mass, mean_score):
    queries = window_start.shape[1]
    unit = identity(queries)
    members = (first, second, third)
    for w in range(2):
        at = slice(w * queries, (w + 1) * queries)
        states = [columns_of(member, unit, w) for member in members]
        _, factors = weigh_states([state[0] for state in states])
        total = functools.reduce(jnp.add, [f * state[1] for f, state in zip(factors, states)])
        weighted = functools.reduce(
            jnp.add, [f * member[at, :].astype(F32) for f, member in zip(factors, members)]
        )
        pooled[:, w, :] = (weighted / total).astype(BF16)

        lines = [member[2 * queries :, at].astype(F32) for member in members]
        tops, totals, sums = (
            [line[3 * k : 3 * k + 1, :] + line[3 * k + 1 : 3 * k + 2, :] + line[3 * k + 2 : 3 * k + 3, :] for line in lines]
            for k in range(3)
        )
        best, factors = weigh_states([jnp.where(t > 0, top, NEG) for top, t in zip(tops, totals)])
        total = functools.reduce(jnp.add, [f * t for f, t in zip(factors, totals)])
        log_mass[w : w + 1, :] = best + jnp.log(total)
        count = (window_end[w : w + 1, :] - window_start[w : w + 1, :]).astype(F32)
        mean_score[w : w + 1, :] = functools.reduce(jnp.add, sums) / count


def finish(window_start, window_end, *members):
    queries = window_start.shape[1]
    width = members[0].shape[1]
    line = jax.ShapeDtypeStruct((2, queries), F32)
    return pl.pallas_call(
        finish_kernel,
        out_shape=(jax.ShapeDtypeStruct((queries, 2, width), BF16), line, line),
        in_specs=[VMEM] * 5,
        out_specs=(VMEM, VMEM, VMEM),
        compiler_params=params(8),
        name="finish",
    )(window_start, window_end, *members)


def local(queries, corpus, window_start, window_end):
    docs = corpus.shape[0]
    size = lax.axis_size(AXES)
    position = lax.axis_index(AXES)
    across = [(i, i ^ 1) for i in range(size)]
    between = [(i, i + 1) for i in range(3, size - 1, 4)] + [(i + 1, i) for i in range(3, size - 1, 4)]
    relay = [(i, i + 2) for i in range(0, size, 4)] + [(i + 3, i + 1) for i in range(0, size, 4)]
    relay_back = [(target, source) for source, target in relay]
    odd = position % 2

    starts, ends = window_start.T, window_end.T
    base = jnp.full((1,), (position - 1) * docs, jnp.int32)
    message = pack(base, queries, starts, ends)
    near = lax.ppermute(message, AXES, across)
    far_a = lax.ppermute(message, AXES, between)
    far_b = lax.ppermute(near, AXES, relay)
    shifts = jnp.stack([2 * docs * odd, 2 * docs * (1 - odd)]).astype(jnp.int32)
    near_part, far_part = neighbours(shifts, near, far_a, far_b, corpus)
    far_back = lax.ppermute(far_part, AXES, between)
    relayed = lax.ppermute(far_part, AXES, relay_back)
    near_back = lax.ppermute(merge(near_part, relayed), AXES, across)
    message, _ = lax.optimization_barrier((message, far_part))
    own_part = own(jnp.full((1,), docs, jnp.int32), message, corpus)
    pooled, log_mass, mean_score = finish(starts, ends, own_part, near_back, far_back)
    return pooled, log_mass.T, mean_score.T


def solution(mesh):
    placed = P(AXES, None)
    return jax.shard_map(
        local,
        mesh=mesh,
        in_specs=(placed,) * 4,
        out_specs=(P(AXES, None, None), placed, placed),
        check_vma=False,
    )
```

```python
import functools
import math

import jax
import jax.numpy as jnp
from jax import lax
from jax.experimental import pallas as pl
from jax.experimental.pallas import tpu as pltpu
from jax.sharding import PartitionSpec as P

SCORE_SCALE = 3.0
NEG = -1e30
LOG2E = math.log2(math.e)
AXES = ("tm", "pb")
BF16 = jnp.bfloat16
F32 = jnp.float32
NT = (((1,), (1,)), ((), ()))
TN = (((0,), (0,)), ((), ()))
META = 16
LANES = 128
DOC_TILE = 1024
SUBLANES = 8
CHUNK = 32

VMEM = pl.BlockSpec(memory_space=pltpu.VMEM)
SMEM = pl.BlockSpec(memory_space=pltpu.SMEM)


def params(mebibytes):
    return pltpu.CompilerParams(vmem_limit_bytes=mebibytes * 2**20)


def identity(n):
    rows = lax.broadcasted_iota(jnp.int32, (n, n), 0)
    return (rows == lax.broadcasted_iota(jnp.int32, (n, n), 1)).astype(BF16)


def split_int(value):
    return (value >> 8).astype(F32), (value & 255).astype(F32)


def split_float(value):
    high = value.astype(BF16).astype(F32)
    rest = value - high
    middle = rest.astype(BF16).astype(F32)
    return high, middle, rest - middle


def row_scratch(rows, docs, width, tile):
    groups = rows // LANES
    return [
        pltpu.VMEM((rows, width), BF16),
        pltpu.VMEM((groups, SUBLANES, LANES), jnp.int32),
        pltpu.VMEM((groups, SUBLANES, LANES), jnp.int32),
        pltpu.VMEM((groups, SUBLANES, LANES), F32),
        pltpu.VMEM((groups, SUBLANES, LANES), F32),
        pltpu.VMEM((groups, SUBLANES, LANES), F32),
        pltpu.VMEM((tile, 2 * LANES), F32),
        pltpu.VMEM((tile, 2 * LANES), F32),
        pltpu.VMEM((docs, 2 * LANES), F32),
        pltpu.VMEM((tile, 2 * LANES), BF16),
        pltpu.VMEM((tile, 2 * LANES), BF16),
        pltpu.VMEM((rows, width), F32),
    ]


def fold(values, op):
    return op(values.reshape(values.shape[0] // SUBLANES, SUBLANES, values.shape[1]), axis=0)


def set_bounds(scratch, low, length):
    lows, lengths = scratch[1:3]
    for g in range(lows.shape[0]):
        at = slice(g * LANES, (g + 1) * LANES)
        lows[g] = jnp.broadcast_to(low[:, at], (SUBLANES, LANES))
        lengths[g] = jnp.broadcast_to(length[:, at], (SUBLANES, LANES))


def attend_rows(docs, scratch, step):
    rows_q, lows, lengths, peak, score_sum, mass, s_a, s_b, masked, p_a, p_b, acc = scratch
    n_docs, width = docs.shape
    tile = s_a.shape[0]
    tiles = n_docs // tile
    scale = SCORE_SCALE / math.sqrt(width)

    def first_group(t):
        if isinstance(t, int):
            return step if t >= tiles // 2 else 0
        return jnp.where(t >= tiles // 2, step, 0)

    def met_rows(t):
        first = first_group(t)
        if isinstance(first, int):
            return slice(first * LANES, (first + 2) * LANES)
        return pl.ds(pl.multiple_of(first * LANES, LANES), 2 * LANES)

    def wide(ref, g):
        return jnp.broadcast_to(ref[g][0:1, :], (CHUNK, LANES))

    def score(t):
        (s_a, s_b)[t % 2][...] = lax.dot_general(
            docs[t * tile : (t + 1) * tile, :], rows_q[met_rows(t), :], NT, preferred_element_type=F32
        )

    def scan(t):
        scores = (s_a, s_b)[t % 2]
        down = lax.broadcasted_iota(jnp.int32, (CHUNK, LANES), 0)
        for side in range(2):
            g = first_group(t) + side
            at = slice(side * LANES, (side + 1) * LANES)
            offset = down - wide(lows, g)
            length = wide(lengths, g).astype(jnp.uint32)
            top, total = peak[g], score_sum[g]
            for c in range(0, tile, CHUNK):
                value = scores[c : c + CHUNK, at]
                inside = (offset + (t * tile + c)).astype(jnp.uint32) < length
                kept = jnp.where(inside, value, NEG)
                top = jnp.maximum(top, fold(kept, jnp.max))
                total = total + fold(jnp.where(inside, value, 0.0), jnp.sum)
                masked[t * tile + c : t * tile + c + CHUNK, at] = kept
            peak[g] = top
            score_sum[g] = total

    peak[...] = jnp.full(peak.shape, NEG, F32)
    score_sum[...] = jnp.zeros(score_sum.shape, F32)
    mass[...] = jnp.zeros(mass.shape, F32)
    acc[...] = jnp.zeros(acc.shape, F32)
    score(0)
    for t in range(tiles):
        if t + 1 < tiles:
            score(t + 1)
        scan(t)
    groups = range(peak.shape[0])
    tops = [jnp.max(peak[g], axis=0, keepdims=True) for g in groups]
    for g in groups:
        peak[g] = jnp.broadcast_to(jnp.maximum(tops[g], 0.5 * NEG), (SUBLANES, LANES))

    def weigh(t, out):
        for side in range(2):
            g = first_group(t) + side
            at = slice(side * LANES, (side + 1) * LANES)
            shift, total = wide(peak, g), mass[g]
            for c in range(0, tile, CHUNK):
                value = masked[pl.ds(pl.multiple_of(t * tile + c, CHUNK), CHUNK), at]
                p = jnp.exp2((value - shift) * (scale * LOG2E))
                total = total + fold(p, jnp.sum)
                out[c : c + CHUNK, at] = p.astype(BF16)
            mass[g] = total

    def pool(t, weights):
        block = docs[pl.ds(pl.multiple_of(t * tile, tile), tile), :]
        acc[met_rows(t), :] += lax.dot_general(weights[...], block, TN, preferred_element_type=F32)

    weigh(0, p_a)

    def second_step(k, carry):
        t = 2 * k + 1
        pool(t - 1, p_a)
        weigh(t, p_b)
        pool(t, p_b)
        weigh(t + 1, p_a)
        return carry

    lax.fori_loop(0, tiles // 2 - 1, second_step, 0)
    pool(tiles - 2, p_a)
    weigh(tiles - 1, p_b)
    pool(tiles - 1, p_b)

    def line(parts):
        return jnp.concatenate(parts, axis=1)

    return (
        line(tops) * scale,
        line([jnp.sum(mass[g], axis=0, keepdims=True) for g in groups]),
        line([jnp.sum(score_sum[g], axis=0, keepdims=True) for g in groups]) * scale,
    )


def stats_lines(stats):
    lines = [part for value in stats for part in split_float(value)]
    lines.append(jnp.zeros((META - len(lines), stats[0].shape[1]), F32))
    return jnp.concatenate(lines, axis=0).astype(BF16)


def bound_lines(meta, shift, n_docs):
    meta = meta.astype(F32)

    def bound(k):
        value = meta[2 * k : 2 * k + 1, :] * 256.0 + meta[2 * k + 1 : 2 * k + 2, :]
        return jnp.clip(value.astype(jnp.int32) - shift, 0, n_docs)

    lows = [bound(w) for w in range(2)]
    return lows, [jnp.maximum(bound(2 + w) - low, 0) for w, low in enumerate(lows)]


def own_kernel(shift, message, docs, out, *scratch):
    rows_q = scratch[0]
    queries = message.shape[0] - META
    lows, lengths = bound_lines(message[queries:, 0:queries], shift[0], docs.shape[0])
    set_bounds(scratch, jnp.concatenate(lows, axis=1), jnp.concatenate(lengths, axis=1))
    for w in range(2):
        rows_q[w * queries : (w + 1) * queries, :] = message[0:queries, :]
    stats = attend_rows(docs, scratch, 0)
    out[0 : 2 * queries, :] = scratch[-1][...].astype(BF16)
    out[2 * queries :, :] = jnp.zeros((META, out.shape[1]), BF16)
    out[2 * queries :, 0 : 2 * queries] = stats_lines(stats)


def own(shift, message, corpus):
    docs, width = corpus.shape
    queries = message.shape[0] - META
    tile = min(DOC_TILE, docs // 2)
    return pl.pallas_call(
        own_kernel,
        out_shape=jax.ShapeDtypeStruct((2 * queries + META, width), BF16),
        in_specs=[SMEM, VMEM, VMEM],
        out_specs=VMEM,
        scratch_shapes=row_scratch(2 * queries, docs, width, tile),
        compiler_params=params(16),
        cost_estimate=pl.CostEstimate(
            flops=8 * queries * docs * width,
            bytes_accessed=docs * width * 2,
            transcendentals=2 * queries * docs,
        ),
        name="own_block",
    )(shift, message, corpus)


def neighbour_kernel(shifts, near, far_a, far_b, docs, near_out, far_out, both_q, pooled, *scratch):
    rows_q = scratch[0]
    queries = near.shape[0] - META
    n_docs = docs.shape[0]
    held = rows_q.shape[0]
    centre = held // 2
    both_q[0:queries, :] = near[0:queries, :]
    both_q[queries:, :] = far_a[0:queries, :] + far_b[0:queries, :]
    metas = (near[queries:, 0:queries], far_a[queries:, 0:queries] + far_b[queries:, 0:queries])
    lows, lengths = [], []
    for side, meta in enumerate(metas):
        low, length = bound_lines(meta, shifts[side], n_docs)
        lows += low
        lengths += length
    blocks = len(lows)
    rows = blocks * queries

    keys = [
        jnp.where(length > 0, jnp.where(low == 0, length, n_docs + low), 2 * n_docs)
        for low, length in zip(lows, lengths)
    ]
    parts = []
    for low, length, key in zip(lows, lengths, keys):
        lines = [*split_int(low), *split_int(length), *split_int(key), jnp.zeros((META - 6, queries), F32)]
        parts.append(jnp.concatenate(lines, axis=0).astype(BF16))
    unit = identity(queries)
    lane = lax.broadcasted_iota(jnp.int32, (1, queries), 1)
    line = lax.broadcasted_iota(jnp.int32, (queries, 1), 0)
    ordered = [keys[b] * rows + (lane + b * queries) for b in range(blocks)]
    ranks = [jnp.zeros((1, queries), F32)] * blocks
    for a in range(blocks):
        columns = lax.dot_general(unit, parts[a], NT, preferred_element_type=F32)
        key = (columns[:, 4:5] * 256.0 + columns[:, 5:6]).astype(jnp.int32)
        key = jnp.broadcast_to(key * rows + (line + a * queries), (queries, queries))
        for b in range(blocks):
            ranks[b] = ranks[b] + jnp.sum((key < ordered[b]).astype(F32), axis=0, keepdims=True)
    opened = jnp.zeros((1, 1), F32)
    for low, length in zip(lows, lengths):
        opened = opened + jnp.sum(((length > 0) & (low == 0)).astype(F32), axis=1, keepdims=True)
    places, misfits = [], jnp.zeros((1, 1), F32)
    half = n_docs // 2
    for low, length, rank in zip(lows, lengths, ranks):
        place = (rank + (centre - opened)).astype(jnp.int32)
        bad = (place < 0) | (place >= held)
        bad = bad | ((place < LANES) & (low + length > half)) | ((place >= 2 * LANES) & (low < half))
        misfits = misfits + jnp.sum(((length > 0) & bad).astype(F32), axis=1, keepdims=True)
        places.append(jnp.where(length > 0, place, -1))
    fits = jnp.max(misfits) == 0.0
    passes = jnp.where(fits, 1, 2)
    step = jnp.where(fits, held // LANES - 2, 0)

    near_out[...] = jnp.zeros(near_out.shape, BF16)
    far_out[...] = jnp.zeros(far_out.shape, BF16)

    def work(turn, carry):
        row = lax.broadcasted_iota(jnp.int32, (held, queries), 0)
        pick = []
        for b in range(blocks):
            plain = jnp.where(turn == b // 2, lane + (b % 2) * queries, -1)
            place = jnp.where(fits, places[b], plain)
            pick.append((row == place).astype(F32).astype(BF16))
        of_query = jnp.concatenate([pick[0] + pick[1], pick[2] + pick[3]], axis=1)
        rows_q[...] = jnp.dot(of_query, both_q[...], preferred_element_type=F32).astype(BF16)
        lines = sum(
            lax.dot_general(part, chosen, NT, preferred_element_type=F32) for part, chosen in zip(parts, pick)
        )
        set_bounds(
            scratch,
            (lines[0:1, :] * 256.0 + lines[1:2, :]).astype(jnp.int32),
            (lines[2:3, :] * 256.0 + lines[3:4, :]).astype(jnp.int32),
        )
        stats = stats_lines(attend_rows(docs, scratch, step))
        pooled[...] = scratch[-1][...].astype(BF16)
        for b, chosen in enumerate(pick):
            out = (near_out, far_out)[b // 2]
            at = slice((b % 2) * queries, (b % 2 + 1) * queries)
            out[at, :] += lax.dot_general(chosen, pooled[...], TN, preferred_element_type=F32).astype(BF16)
            out[2 * queries :, at] += jnp.dot(stats, chosen, preferred_element_type=F32).astype(BF16)
        return carry

    lax.fori_loop(0, passes, work, 0)


def neighbours(shifts, near, far_a, far_b, corpus):
    docs, width = corpus.shape
    queries = near.shape[0] - META
    held = 3 * LANES
    tile = min(DOC_TILE, docs // 2)
    result = jax.ShapeDtypeStruct((2 * queries + META, width), BF16)
    return pl.pallas_call(
        neighbour_kernel,
        out_shape=(result, result),
        in_specs=[SMEM, VMEM, VMEM, VMEM, VMEM],
        out_specs=(VMEM, VMEM),
        scratch_shapes=[
            pltpu.VMEM((2 * queries, width), BF16),
            pltpu.VMEM((held, width), BF16),
        ]
        + row_scratch(held, docs, width, tile),
        compiler_params=params(18),
        cost_estimate=pl.CostEstimate(
            flops=8 * queries * docs * width,
            bytes_accessed=docs * width * 2,
            transcendentals=2 * queries * docs,
        ),
        name="neighbour_blocks",
    )(shifts, near, far_a, far_b, corpus)


def pack_kernel(base, queries, starts, ends, out):
    rows, width = queries.shape
    out[0:rows, :] = queries[...]
    out[rows:, :] = jnp.zeros((META, width), BF16)
    parts = [split_int(lines[...] - base[0]) for lines in (starts, ends)]
    lines = [part[w : w + 1, :] for pair in parts for w in range(2) for part in pair]
    lines.append(jnp.zeros((META - 8, rows), F32))
    out[rows:, 0:rows] = jnp.concatenate(lines, axis=0).astype(BF16)


def pack(base, queries, starts, ends, waiting):
    rows, width = queries.shape
    return pl.pallas_call(
        pack_kernel,
        out_shape=jax.ShapeDtypeStruct((rows + META, width), BF16),
        in_specs=[SMEM, VMEM, VMEM, VMEM],
        out_specs=VMEM,
        compiler_params=params(4),
        cost_estimate=pl.CostEstimate(flops=waiting, bytes_accessed=0, transcendentals=0),
        name="pack",
    )(base, queries, starts, ends)


def columns_of(state, unit, w):
    queries = unit.shape[0]
    lines = state[2 * queries :, w * queries : (w + 1) * queries]
    columns = lax.dot_general(unit, lines, NT, preferred_element_type=F32)
    top, total, score_sum = (
        columns[:, 3 * k : 3 * k + 1] + columns[:, 3 * k + 1 : 3 * k + 2] + columns[:, 3 * k + 2 : 3 * k + 3]
        for k in range(3)
    )
    return jnp.where(total > 0, top, NEG), total, score_sum


def weigh_states(tops):
    best = functools.reduce(jnp.maximum, tops)
    return best, [jnp.exp(top - best) for top in tops]


def stats_matrix(stats):
    rows = stats[0].shape[0]
    lane = lax.broadcasted_iota(jnp.int32, (rows, META), 1)
    matrix = jnp.zeros((rows, META), F32)
    for k, value in enumerate(stats):
        for j, part in enumerate(split_float(value)):
            matrix = jnp.where(lane == 3 * k + j, part, matrix)
    return matrix.astype(BF16)


def merge_kernel(first, second, out):
    queries = (first.shape[0] - META) // 2
    unit = identity(queries)
    out[2 * queries :, :] = jnp.zeros((META, out.shape[1]), BF16)
    for w in range(2):
        at = slice(w * queries, (w + 1) * queries)
        states = [columns_of(state, unit, w) for state in (first, second)]
        best, factors = weigh_states([state[0] for state in states])
        total = functools.reduce(jnp.add, [f * state[1] for f, state in zip(factors, states)])
        score_sum = states[0][2] + states[1][2]
        out[at, :] = (
            factors[0] * first[at, :].astype(F32) + factors[1] * second[at, :].astype(F32)
        ).astype(BF16)
        stats = stats_matrix((best, total, score_sum))
        out[2 * queries :, at] = lax.dot_general(
            stats, unit, TN, preferred_element_type=F32
        ).astype(BF16)


def merge(first, second):
    return pl.pallas_call(
        merge_kernel,
        out_shape=jax.ShapeDtypeStruct(first.shape, BF16),
        in_specs=[VMEM, VMEM],
        out_specs=VMEM,
        compiler_params=params(8),
        name="merge",
    )(first, second)


def finish_kernel(window_start, window_end, first, second, third, pooled, log_mass, mean_score):
    queries = window_start.shape[1]
    unit = identity(queries)
    members = (first, second, third)
    for w in range(2):
        at = slice(w * queries, (w + 1) * queries)
        states = [columns_of(member, unit, w) for member in members]
        _, factors = weigh_states([state[0] for state in states])
        total = functools.reduce(jnp.add, [f * state[1] for f, state in zip(factors, states)])
        weighted = functools.reduce(
            jnp.add, [f * member[at, :].astype(F32) for f, member in zip(factors, members)]
        )
        pooled[:, w, :] = (weighted / total).astype(BF16)

        lines = [member[2 * queries :, at].astype(F32) for member in members]
        tops, totals, sums = (
            [line[3 * k : 3 * k + 1, :] + line[3 * k + 1 : 3 * k + 2, :] + line[3 * k + 2 : 3 * k + 3, :] for line in lines]
            for k in range(3)
        )
        best, factors = weigh_states([jnp.where(t > 0, top, NEG) for top, t in zip(tops, totals)])
        total = functools.reduce(jnp.add, [f * t for f, t in zip(factors, totals)])
        log_mass[w : w + 1, :] = best + jnp.log(total)
        count = (window_end[w : w + 1, :] - window_start[w : w + 1, :]).astype(F32)
        mean_score[w : w + 1, :] = functools.reduce(jnp.add, sums) / count


def finish(window_start, window_end, *members):
    queries = window_start.shape[1]
    width = members[0].shape[1]
    line = jax.ShapeDtypeStruct((2, queries), F32)
    return pl.pallas_call(
        finish_kernel,
        out_shape=(jax.ShapeDtypeStruct((queries, 2, width), BF16), line, line),
        in_specs=[VMEM] * 5,
        out_specs=(VMEM, VMEM, VMEM),
        compiler_params=params(8),
        name="finish",
    )(window_start, window_end, *members)


def local(queries, corpus, window_start, window_end):
    rows, width = queries.shape
    docs = corpus.shape[0]
    size = lax.axis_size(AXES)
    position = lax.axis_index(AXES)
    across = [(i, i ^ 1) for i in range(size)]
    between = [(i, i + 1) for i in range(3, size - 1, 4)] + [(i + 1, i) for i in range(3, size - 1, 4)]
    relay = [(i, i + 2) for i in range(0, size, 4)] + [(i + 3, i + 1) for i in range(0, size, 4)]
    relay_back = [(target, source) for source, target in relay]
    odd = position % 2

    starts, ends = window_start.T, window_end.T
    base = jnp.full((1,), (position - 1) * docs, jnp.int32)
    message = pack(base, queries, starts, ends, 8 * rows * docs * width)
    near = lax.ppermute(message, AXES, across)
    far_a = lax.ppermute(message, AXES, between)
    far_b = lax.ppermute(near, AXES, relay)
    shifts = jnp.stack([2 * docs * odd, 2 * docs * (1 - odd)]).astype(jnp.int32)
    near_part, far_part = neighbours(shifts, near, far_a, far_b, corpus)
    far_back = lax.ppermute(far_part, AXES, between)
    relayed = lax.ppermute(far_part, AXES, relay_back)
    near_back = lax.ppermute(merge(near_part, relayed), AXES, across)
    message, _ = lax.optimization_barrier((message, far_part))
    own_part = own(jnp.full((1,), docs, jnp.int32), message, corpus)
    pooled, log_mass, mean_score = finish(starts, ends, own_part, near_back, far_back)
    return pooled, log_mass.T, mean_score.T


def solution(mesh):
    placed = P(AXES, None)
    return jax.shard_map(
        local,
        mesh=mesh,
        in_specs=(placed,) * 4,
        out_specs=(P(AXES, None, None), placed, placed),
        check_vma=False,
    )
```

```python
import functools
import math

import jax
import jax.numpy as jnp
from jax import lax
from jax.experimental import pallas as pl
from jax.experimental.pallas import tpu as pltpu
from jax.sharding import PartitionSpec as P

SCORE_SCALE = 3.0
NEG = -1e30
LOG2E = math.log2(math.e)
AXES = ("tm", "pb")
BF16 = jnp.bfloat16
F32 = jnp.float32
NT = (((1,), (1,)), ((), ()))
TN = (((0,), (0,)), ((), ()))
META = 16
LANES = 128
DOC_TILE = 1024
SUBLANES = 8
CHUNK = 32

VMEM = pl.BlockSpec(memory_space=pltpu.VMEM)
SMEM = pl.BlockSpec(memory_space=pltpu.SMEM)
HBM = pl.BlockSpec(memory_space=pltpu.HBM)


def params(mebibytes):
    return pltpu.CompilerParams(vmem_limit_bytes=mebibytes * 2**20)


def identity(n):
    rows = lax.broadcasted_iota(jnp.int32, (n, n), 0)
    return (rows == lax.broadcasted_iota(jnp.int32, (n, n), 1)).astype(BF16)


def split_int(value):
    return (value >> 8).astype(F32), (value & 255).astype(F32)


def split_float(value):
    high = value.astype(BF16).astype(F32)
    rest = value - high
    middle = rest.astype(BF16).astype(F32)
    return high, middle, rest - middle


def row_scratch(rows, docs, width, tile):
    groups = rows // LANES
    return [
        pltpu.VMEM((rows, width), BF16),
        pltpu.VMEM((groups, SUBLANES, LANES), jnp.int32),
        pltpu.VMEM((groups, SUBLANES, LANES), jnp.int32),
        pltpu.VMEM((groups, SUBLANES, LANES), F32),
        pltpu.VMEM((groups, SUBLANES, LANES), F32),
        pltpu.VMEM((groups, SUBLANES, LANES), F32),
        pltpu.VMEM((tile, 2 * LANES), F32),
        pltpu.VMEM((tile, 2 * LANES), F32),
        pltpu.VMEM((docs, 2 * LANES), F32),
        pltpu.VMEM((tile, 2 * LANES), BF16),
        pltpu.VMEM((tile, 2 * LANES), BF16),
        pltpu.VMEM((rows, width), F32),
    ]


def part_copies(corpus, docs, arrived, tile):
    tiles = docs.shape[0] // tile
    firsts = sorted({0, tiles // 4, tiles // 2})
    copies = {}
    for k, (first, end) in enumerate(zip(firsts, firsts[1:] + [tiles])):
        at = pl.ds(first * tile, (end - first) * tile)
        copies[first] = pltpu.make_async_copy(corpus.at[at], docs.at[at], arrived.at[k])
    return copies


def fold(values, op):
    return op(values.reshape(values.shape[0] // SUBLANES, SUBLANES, values.shape[1]), axis=0)


def set_bounds(scratch, low, length):
    lows, lengths = scratch[1:3]
    for g in range(lows.shape[0]):
        at = slice(g * LANES, (g + 1) * LANES)
        lows[g] = jnp.broadcast_to(low[:, at], (SUBLANES, LANES))
        lengths[g] = jnp.broadcast_to(length[:, at], (SUBLANES, LANES))


def attend_rows(docs, scratch, step, copies):
    rows_q, lows, lengths, peak, score_sum, mass, s_a, s_b, masked, p_a, p_b, acc = scratch
    n_docs, width = docs.shape
    tile = s_a.shape[0]
    tiles = n_docs // tile
    scale = SCORE_SCALE / math.sqrt(width)

    def first_group(t):
        if isinstance(t, int):
            return step if t >= tiles // 2 else 0
        return jnp.where(t >= tiles // 2, step, 0)

    def met_rows(t):
        first = first_group(t)
        if isinstance(first, int):
            return slice(first * LANES, (first + 2) * LANES)
        return pl.ds(pl.multiple_of(first * LANES, LANES), 2 * LANES)

    def wide(ref, g):
        return jnp.broadcast_to(ref[g][0:1, :], (CHUNK, LANES))

    def score(t):
        if t in copies:
            copies[t].wait()
        (s_a, s_b)[t % 2][...] = lax.dot_general(
            docs[t * tile : (t + 1) * tile, :], rows_q[met_rows(t), :], NT, preferred_element_type=F32
        )

    def scan(t):
        scores = (s_a, s_b)[t % 2]
        down = lax.broadcasted_iota(jnp.int32, (CHUNK, LANES), 0)
        for side in range(2):
            g = first_group(t) + side
            at = slice(side * LANES, (side + 1) * LANES)
            offset = down - wide(lows, g)
            length = wide(lengths, g).astype(jnp.uint32)
            top, total = peak[g], score_sum[g]
            for c in range(0, tile, CHUNK):
                value = scores[c : c + CHUNK, at]
                inside = (offset + (t * tile + c)).astype(jnp.uint32) < length
                kept = jnp.where(inside, value, NEG)
                top = jnp.maximum(top, fold(kept, jnp.max))
                total = total + fold(jnp.where(inside, value, 0.0), jnp.sum)
                masked[t * tile + c : t * tile + c + CHUNK, at] = kept
            peak[g] = top
            score_sum[g] = total

    peak[...] = jnp.full(peak.shape, NEG, F32)
    score_sum[...] = jnp.zeros(score_sum.shape, F32)
    mass[...] = jnp.zeros(mass.shape, F32)
    acc[...] = jnp.zeros(acc.shape, F32)
    score(0)
    for t in range(tiles):
        if t + 1 < tiles:
            score(t + 1)
        scan(t)
    groups = range(peak.shape[0])
    tops = [jnp.max(peak[g], axis=0, keepdims=True) for g in groups]
    for g in groups:
        peak[g] = jnp.broadcast_to(jnp.maximum(tops[g], 0.5 * NEG), (SUBLANES, LANES))

    def weigh(t, out):
        for side in range(2):
            g = first_group(t) + side
            at = slice(side * LANES, (side + 1) * LANES)
            shift, total = wide(peak, g), mass[g]
            for c in range(0, tile, CHUNK):
                value = masked[pl.ds(pl.multiple_of(t * tile + c, CHUNK), CHUNK), at]
                p = jnp.exp2((value - shift) * (scale * LOG2E))
                total = total + fold(p, jnp.sum)
                out[c : c + CHUNK, at] = p.astype(BF16)
            mass[g] = total

    def pool(t, weights):
        block = docs[pl.ds(pl.multiple_of(t * tile, tile), tile), :]
        acc[met_rows(t), :] += lax.dot_general(weights[...], block, TN, preferred_element_type=F32)

    weigh(0, p_a)

    def second_step(k, carry):
        t = 2 * k + 1
        pool(t - 1, p_a)
        weigh(t, p_b)
        pool(t, p_b)
        weigh(t + 1, p_a)
        return carry

    lax.fori_loop(0, tiles // 2 - 1, second_step, 0)
    pool(tiles - 2, p_a)
    weigh(tiles - 1, p_b)
    pool(tiles - 1, p_b)

    def line(parts):
        return jnp.concatenate(parts, axis=1)

    return (
        line(tops) * scale,
        line([jnp.sum(mass[g], axis=0, keepdims=True) for g in groups]),
        line([jnp.sum(score_sum[g], axis=0, keepdims=True) for g in groups]) * scale,
    )


def stats_lines(stats):
    lines = [part for value in stats for part in split_float(value)]
    lines.append(jnp.zeros((META - len(lines), stats[0].shape[1]), F32))
    return jnp.concatenate(lines, axis=0).astype(BF16)


def bound_lines(meta, shift, n_docs):
    meta = meta.astype(F32)

    def bound(k):
        value = meta[2 * k : 2 * k + 1, :] * 256.0 + meta[2 * k + 1 : 2 * k + 2, :]
        return jnp.clip(value.astype(jnp.int32) - shift, 0, n_docs)

    lows = [bound(w) for w in range(2)]
    return lows, [jnp.maximum(bound(2 + w) - low, 0) for w, low in enumerate(lows)]


def own_kernel(shift, message, corpus, out, docs, arrived, *scratch):
    rows_q = scratch[0]
    copies = part_copies(corpus, docs, arrived, scratch[6].shape[0])
    for copy in copies.values():
        copy.start()
    queries = message.shape[0] - META
    lows, lengths = bound_lines(message[queries:, 0:queries], shift[0], docs.shape[0])
    set_bounds(scratch, jnp.concatenate(lows, axis=1), jnp.concatenate(lengths, axis=1))
    for w in range(2):
        rows_q[w * queries : (w + 1) * queries, :] = message[0:queries, :]
    stats = attend_rows(docs, scratch, 0, copies)
    out[0 : 2 * queries, :] = scratch[-1][...].astype(BF16)
    out[2 * queries :, :] = jnp.zeros((META, out.shape[1]), BF16)
    out[2 * queries :, 0 : 2 * queries] = stats_lines(stats)


def own(shift, message, corpus):
    docs, width = corpus.shape
    queries = message.shape[0] - META
    tile = min(DOC_TILE, docs // 2)
    return pl.pallas_call(
        own_kernel,
        out_shape=jax.ShapeDtypeStruct((2 * queries + META, width), BF16),
        in_specs=[SMEM, VMEM, HBM],
        out_specs=VMEM,
        scratch_shapes=[pltpu.VMEM((docs, width), BF16), pltpu.SemaphoreType.DMA((3,))]
        + row_scratch(2 * queries, docs, width, tile),
        compiler_params=params(44),
        cost_estimate=pl.CostEstimate(
            flops=8 * queries * docs * width,
            bytes_accessed=docs * width * 2,
            transcendentals=2 * queries * docs,
        ),
        name="own_block",
    )(shift, message, corpus)


def neighbour_kernel(shifts, near, far, corpus, near_out, far_out, docs, arrived, both_q, pooled, *scratch):
    rows_q = scratch[0]
    copies = part_copies(corpus, docs, arrived, scratch[6].shape[0])
    for copy in copies.values():
        copy.start()
    queries = near.shape[0] - META
    n_docs = docs.shape[0]
    held = rows_q.shape[0]
    centre = held // 2
    both_q[0:queries, :] = near[0:queries, :]
    both_q[queries:, :] = far[0:queries, :]
    metas = (near[queries:, 0:queries], far[queries:, 0:queries])
    lows, lengths = [], []
    for side, meta in enumerate(metas):
        low, length = bound_lines(meta, shifts[side], n_docs)
        lows += low
        lengths += length
    blocks = len(lows)
    rows = blocks * queries

    keys = [
        jnp.where(length > 0, jnp.where(low == 0, length, n_docs + low), 2 * n_docs)
        for low, length in zip(lows, lengths)
    ]
    parts = []
    for low, length, key in zip(lows, lengths, keys):
        lines = [*split_int(low), *split_int(length), *split_int(key), jnp.zeros((META - 6, queries), F32)]
        parts.append(jnp.concatenate(lines, axis=0).astype(BF16))
    unit = identity(queries)
    lane = lax.broadcasted_iota(jnp.int32, (1, queries), 1)
    line = lax.broadcasted_iota(jnp.int32, (queries, 1), 0)
    ordered = [keys[b] * rows + (lane + b * queries) for b in range(blocks)]
    ranks = [jnp.zeros((1, queries), F32)] * blocks
    for a in range(blocks):
        columns = lax.dot_general(unit, parts[a], NT, preferred_element_type=F32)
        key = (columns[:, 4:5] * 256.0 + columns[:, 5:6]).astype(jnp.int32)
        key = jnp.broadcast_to(key * rows + (line + a * queries), (queries, queries))
        for b in range(blocks):
            ranks[b] = ranks[b] + jnp.sum((key < ordered[b]).astype(F32), axis=0, keepdims=True)
    opened = jnp.zeros((1, 1), F32)
    for low, length in zip(lows, lengths):
        opened = opened + jnp.sum(((length > 0) & (low == 0)).astype(F32), axis=1, keepdims=True)
    places, misfits = [], jnp.zeros((1, 1), F32)
    half = n_docs // 2
    for low, length, rank in zip(lows, lengths, ranks):
        place = (rank + (centre - opened)).astype(jnp.int32)
        bad = (place < 0) | (place >= held)
        bad = bad | ((place < LANES) & (low + length > half)) | ((place >= 2 * LANES) & (low < half))
        misfits = misfits + jnp.sum(((length > 0) & bad).astype(F32), axis=1, keepdims=True)
        places.append(jnp.where(length > 0, place, -1))
    fits = jnp.max(misfits) == 0.0
    passes = jnp.where(fits, 1, 2)
    step = jnp.where(fits, held // LANES - 2, 0)

    near_out[...] = jnp.zeros(near_out.shape, BF16)
    far_out[...] = jnp.zeros(far_out.shape, BF16)

    def work(turn, carry):
        row = lax.broadcasted_iota(jnp.int32, (held, queries), 0)
        pick = []
        for b in range(blocks):
            plain = jnp.where(turn == b // 2, lane + (b % 2) * queries, -1)
            place = jnp.where(fits, places[b], plain)
            pick.append((row == place).astype(F32).astype(BF16))
        of_query = jnp.concatenate([pick[0] + pick[1], pick[2] + pick[3]], axis=1)
        rows_q[...] = jnp.dot(of_query, both_q[...], preferred_element_type=F32).astype(BF16)
        lines = sum(
            lax.dot_general(part, chosen, NT, preferred_element_type=F32) for part, chosen in zip(parts, pick)
        )
        set_bounds(
            scratch,
            (lines[0:1, :] * 256.0 + lines[1:2, :]).astype(jnp.int32),
            (lines[2:3, :] * 256.0 + lines[3:4, :]).astype(jnp.int32),
        )
        stats = stats_lines(attend_rows(docs, scratch, step, copies))
        pooled[...] = scratch[-1][...].astype(BF16)
        for b, chosen in enumerate(pick):
            out = (near_out, far_out)[b // 2]
            at = slice((b % 2) * queries, (b % 2 + 1) * queries)
            out[at, :] += lax.dot_general(chosen, pooled[...], TN, preferred_element_type=F32).astype(BF16)
            out[2 * queries :, at] += jnp.dot(stats, chosen, preferred_element_type=F32).astype(BF16)

        @pl.when(turn + 1 < passes)
        def _():
            for copy in copies.values():
                copy.start()

        return carry

    lax.fori_loop(0, passes, work, 0)


def neighbours(shifts, near, far, corpus):
    docs, width = corpus.shape
    queries = near.shape[0] - META
    held = 3 * LANES
    tile = min(DOC_TILE, docs // 2)
    result = jax.ShapeDtypeStruct((2 * queries + META, width), BF16)
    return pl.pallas_call(
        neighbour_kernel,
        out_shape=(result, result),
        in_specs=[SMEM, VMEM, VMEM, HBM],
        out_specs=(VMEM, VMEM),
        scratch_shapes=[
            pltpu.VMEM((docs, width), BF16),
            pltpu.SemaphoreType.DMA((3,)),
            pltpu.VMEM((2 * queries, width), BF16),
            pltpu.VMEM((held, width), BF16),
        ]
        + row_scratch(held, docs, width, tile),
        compiler_params=params(44),
        cost_estimate=pl.CostEstimate(
            flops=8 * queries * docs * width,
            bytes_accessed=docs * width * 2,
            transcendentals=2 * queries * docs,
        ),
        name="neighbour_blocks",
    )(shifts, near, far, corpus)


def pack_kernel(base, queries, starts, ends, out):
    rows, width = queries.shape
    out[0:rows, :] = queries[...]
    out[rows:, :] = jnp.zeros((META, width), BF16)
    parts = [split_int(lines[...] - base[0]) for lines in (starts, ends)]
    lines = [part[w : w + 1, :] for pair in parts for w in range(2) for part in pair]
    lines.append(jnp.zeros((META - 8, rows), F32))
    out[rows:, 0:rows] = jnp.concatenate(lines, axis=0).astype(BF16)


def pack(base, queries, starts, ends):
    rows, width = queries.shape
    return pl.pallas_call(
        pack_kernel,
        out_shape=jax.ShapeDtypeStruct((rows + META, width), BF16),
        in_specs=[SMEM, VMEM, VMEM, VMEM],
        out_specs=VMEM,
        name="pack",
    )(base, queries, starts, ends)


def columns_of(state, unit, w):
    queries = unit.shape[0]
    lines = state[2 * queries :, w * queries : (w + 1) * queries]
    columns = lax.dot_general(unit, lines, NT, preferred_element_type=F32)
    top, total, score_sum = (
        columns[:, 3 * k : 3 * k + 1] + columns[:, 3 * k + 1 : 3 * k + 2] + columns[:, 3 * k + 2 : 3 * k + 3]
        for k in range(3)
    )
    return jnp.where(total > 0, top, NEG), total, score_sum


def weigh_states(tops):
    best = functools.reduce(jnp.maximum, tops)
    return best, [jnp.exp(top - best) for top in tops]


def stats_matrix(stats):
    rows = stats[0].shape[0]
    lane = lax.broadcasted_iota(jnp.int32, (rows, META), 1)
    matrix = jnp.zeros((rows, META), F32)
    for k, value in enumerate(stats):
        for j, part in enumerate(split_float(value)):
            matrix = jnp.where(lane == 3 * k + j, part, matrix)
    return matrix.astype(BF16)


def merge_kernel(first, second, out):
    queries = (first.shape[0] - META) // 2
    unit = identity(queries)
    out[2 * queries :, :] = jnp.zeros((META, out.shape[1]), BF16)
    for w in range(2):
        at = slice(w * queries, (w + 1) * queries)
        states = [columns_of(state, unit, w) for state in (first, second)]
        best, factors = weigh_states([state[0] for state in states])
        total = functools.reduce(jnp.add, [f * state[1] for f, state in zip(factors, states)])
        score_sum = states[0][2] + states[1][2]
        out[at, :] = (
            factors[0] * first[at, :].astype(F32) + factors[1] * second[at, :].astype(F32)
        ).astype(BF16)
        stats = stats_matrix((best, total, score_sum))
        out[2 * queries :, at] = lax.dot_general(
            stats, unit, TN, preferred_element_type=F32
        ).astype(BF16)


def merge(first, second):
    return pl.pallas_call(
        merge_kernel,
        out_shape=jax.ShapeDtypeStruct(first.shape, BF16),
        in_specs=[VMEM, VMEM],
        out_specs=VMEM,
        compiler_params=params(8),
        name="merge",
    )(first, second)


def finish_kernel(window_start, window_end, first, second, third, pooled, log_mass, mean_score):
    queries = window_start.shape[1]
    unit = identity(queries)
    members = (first, second, third)
    for w in range(2):
        at = slice(w * queries, (w + 1) * queries)
        states = [columns_of(member, unit, w) for member in members]
        _, factors = weigh_states([state[0] for state in states])
        total = functools.reduce(jnp.add, [f * state[1] for f, state in zip(factors, states)])
        weighted = functools.reduce(
            jnp.add, [f * member[at, :].astype(F32) for f, member in zip(factors, members)]
        )
        pooled[:, w, :] = (weighted / total).astype(BF16)

        lines = [member[2 * queries :, at].astype(F32) for member in members]
        tops, totals, sums = (
            [line[3 * k : 3 * k + 1, :] + line[3 * k + 1 : 3 * k + 2, :] + line[3 * k + 2 : 3 * k + 3, :] for line in lines]
            for k in range(3)
        )
        best, factors = weigh_states([jnp.where(t > 0, top, NEG) for top, t in zip(tops, totals)])
        total = functools.reduce(jnp.add, [f * t for f, t in zip(factors, totals)])
        log_mass[w : w + 1, :] = best + jnp.log(total)
        count = (window_end[w : w + 1, :] - window_start[w : w + 1, :]).astype(F32)
        mean_score[w : w + 1, :] = functools.reduce(jnp.add, sums) / count


def finish(window_start, window_end, *members):
    queries = window_start.shape[1]
    width = members[0].shape[1]
    line = jax.ShapeDtypeStruct((2, queries), F32)
    return pl.pallas_call(
        finish_kernel,
        out_shape=(jax.ShapeDtypeStruct((queries, 2, width), BF16), line, line),
        in_specs=[VMEM] * 5,
        out_specs=(VMEM, VMEM, VMEM),
        compiler_params=params(8),
        name="finish",
    )(window_start, window_end, *members)


def local(queries, corpus, window_start, window_end):
    docs = corpus.shape[0]
    size = lax.axis_size(AXES)
    position = lax.axis_index(AXES)
    across = [(i, i ^ 1) for i in range(size)]
    between = [(i, i + 1) for i in range(3, size - 1, 4)] + [(i + 1, i) for i in range(3, size - 1, 4)]
    past = [(i, i + 1) for i in range(1, size - 1, 2)] + [(i + 1, i) for i in range(1, size - 1, 2)]
    relay = [(i + 2, i) for i in range(0, size, 4)] + [(i + 1, i + 3) for i in range(0, size, 4)]
    odd = position % 2

    starts, ends = window_start.T, window_end.T
    base = jnp.full((1,), (position - 1) * docs, jnp.int32)
    message = pack(base, queries, starts, ends)
    near = lax.ppermute(message, AXES, across)
    far = lax.ppermute(message, AXES, past)
    shifts = jnp.stack([2 * docs * odd, 2 * docs * (1 - odd)]).astype(jnp.int32)
    near_part, far_part = neighbours(shifts, near, far, corpus)
    far_back = lax.ppermute(far_part, AXES, between)
    relayed = lax.ppermute(far_part, AXES, relay)
    near_back = lax.ppermute(merge(near_part, relayed), AXES, across)
    message, _ = lax.optimization_barrier((message, far_part))
    own_part = own(jnp.full((1,), docs, jnp.int32), message, corpus)
    pooled, log_mass, mean_score = finish(starts, ends, own_part, near_back, far_back)
    return pooled, log_mass.T, mean_score.T


def solution(mesh):
    placed = P(AXES, None)
    return jax.shard_map(
        local,
        mesh=mesh,
        in_specs=(placed,) * 4,
        out_specs=(P(AXES, None, None), placed, placed),
        check_vma=False,
    )
```

```python
import functools
import math

import jax
import jax.numpy as jnp
from jax import lax
from jax.experimental import pallas as pl
from jax.experimental.pallas import tpu as pltpu
from jax.sharding import PartitionSpec as P

SCORE_SCALE = 3.0
NEG = -1e30
LOG2E = math.log2(math.e)
AXES = ("tm", "pb")
BF16 = jnp.bfloat16
F32 = jnp.float32
NT = (((1,), (1,)), ((), ()))
TN = (((0,), (0,)), ((), ()))
META = 16
LANES = 128
DOC_TILE = 1024
SUBLANES = 8
CHUNK = 32

VMEM = pl.BlockSpec(memory_space=pltpu.VMEM)
SMEM = pl.BlockSpec(memory_space=pltpu.SMEM)
HBM = pl.BlockSpec(memory_space=pltpu.HBM)


def params(mebibytes):
    return pltpu.CompilerParams(vmem_limit_bytes=mebibytes * 2**20)


def identity(n):
    rows = lax.broadcasted_iota(jnp.int32, (n, n), 0)
    return (rows == lax.broadcasted_iota(jnp.int32, (n, n), 1)).astype(BF16)


def split_int(value):
    return (value >> 8).astype(F32), (value & 255).astype(F32)


def split_float(value):
    high = value.astype(BF16).astype(F32)
    rest = value - high
    middle = rest.astype(BF16).astype(F32)
    return high, middle, rest - middle


def row_scratch(rows, docs, width, tile):
    groups = rows // LANES
    return [
        pltpu.VMEM((rows, width), BF16),
        pltpu.VMEM((groups, SUBLANES, LANES), jnp.int32),
        pltpu.VMEM((groups, SUBLANES, LANES), jnp.int32),
        pltpu.VMEM((groups, SUBLANES, LANES), F32),
        pltpu.VMEM((groups, SUBLANES, LANES), F32),
        pltpu.VMEM((groups, SUBLANES, LANES), F32),
        pltpu.VMEM((tile, 2 * LANES), F32),
        pltpu.VMEM((tile, 2 * LANES), F32),
        pltpu.VMEM((docs, 2 * LANES), F32),
        pltpu.VMEM((tile, 2 * LANES), BF16),
        pltpu.VMEM((tile, 2 * LANES), BF16),
        pltpu.VMEM((rows, width), F32),
    ]


def part_copies(corpus, docs, arrived, tile):
    tiles = docs.shape[0] // tile
    firsts = sorted({0, tiles // 4, tiles // 2})
    copies = {}
    for k, (first, end) in enumerate(zip(firsts, firsts[1:] + [tiles])):
        at = pl.ds(first * tile, (end - first) * tile)
        copies[first] = pltpu.make_async_copy(corpus.at[at], docs.at[at], arrived.at[k])
    return copies


def fold(values, op):
    return op(values.reshape(values.shape[0] // SUBLANES, SUBLANES, values.shape[1]), axis=0)


def set_bounds(scratch, low, length):
    lows, lengths = scratch[1:3]
    for g in range(lows.shape[0]):
        at = slice(g * LANES, (g + 1) * LANES)
        lows[g] = jnp.broadcast_to(low[:, at], (SUBLANES, LANES))
        lengths[g] = jnp.broadcast_to(length[:, at], (SUBLANES, LANES))


def attend_rows(docs, scratch, step, copies):
    rows_q, lows, lengths, peak, score_sum, mass, s_a, s_b, masked, p_a, p_b, acc = scratch
    n_docs, width = docs.shape
    tile = s_a.shape[0]
    tiles = n_docs // tile
    scale = SCORE_SCALE / math.sqrt(width)

    def first_group(t):
        if isinstance(t, int):
            return step if t >= tiles // 2 else 0
        return jnp.where(t >= tiles // 2, step, 0)

    def met_rows(t):
        first = first_group(t)
        if isinstance(first, int):
            return slice(first * LANES, (first + 2) * LANES)
        return pl.ds(pl.multiple_of(first * LANES, LANES), 2 * LANES)

    def wide(ref, g):
        return jnp.broadcast_to(ref[g][0:1, :], (CHUNK, LANES))

    def score(t):
        if t in copies:
            copies[t].wait()
        (s_a, s_b)[t % 2][...] = lax.dot_general(
            docs[t * tile : (t + 1) * tile, :], rows_q[met_rows(t), :], NT, preferred_element_type=F32
        )

    def scan(t):
        scores = (s_a, s_b)[t % 2]
        down = lax.broadcasted_iota(jnp.int32, (CHUNK, LANES), 0)
        for side in range(2):
            g = first_group(t) + side
            at = slice(side * LANES, (side + 1) * LANES)
            offset = down - wide(lows, g)
            length = wide(lengths, g).astype(jnp.uint32)
            top, total = peak[g], score_sum[g]
            for c in range(0, tile, CHUNK):
                value = scores[c : c + CHUNK, at]
                inside = (offset + (t * tile + c)).astype(jnp.uint32) < length
                kept = jnp.where(inside, value, NEG)
                top = jnp.maximum(top, fold(kept, jnp.max))
                total = total + fold(jnp.where(inside, value, 0.0), jnp.sum)
                masked[t * tile + c : t * tile + c + CHUNK, at] = kept
            peak[g] = top
            score_sum[g] = total

    peak[...] = jnp.full(peak.shape, NEG, F32)
    score_sum[...] = jnp.zeros(score_sum.shape, F32)
    mass[...] = jnp.zeros(mass.shape, F32)
    acc[...] = jnp.zeros(acc.shape, F32)
    score(0)
    for t in range(tiles):
        if t + 1 < tiles:
            score(t + 1)
        scan(t)
    groups = range(peak.shape[0])
    tops = [jnp.max(peak[g], axis=0, keepdims=True) for g in groups]
    for g in groups:
        peak[g] = jnp.broadcast_to(jnp.maximum(tops[g], 0.5 * NEG), (SUBLANES, LANES))

    def weigh(t, out):
        for side in range(2):
            g = first_group(t) + side
            at = slice(side * LANES, (side + 1) * LANES)
            shift, total = wide(peak, g), mass[g]
            for c in range(0, tile, CHUNK):
                value = masked[pl.ds(pl.multiple_of(t * tile + c, CHUNK), CHUNK), at]
                p = jnp.exp2((value - shift) * (scale * LOG2E))
                total = total + fold(p, jnp.sum)
                out[c : c + CHUNK, at] = p.astype(BF16)
            mass[g] = total

    def pool(t, weights):
        block = docs[pl.ds(pl.multiple_of(t * tile, tile), tile), :]
        acc[met_rows(t), :] += lax.dot_general(weights[...], block, TN, preferred_element_type=F32)

    weigh(0, p_a)

    def second_step(k, carry):
        t = 2 * k + 1
        pool(t - 1, p_a)
        weigh(t, p_b)
        pool(t, p_b)
        weigh(t + 1, p_a)
        return carry

    lax.fori_loop(0, tiles // 2 - 1, second_step, 0)
    pool(tiles - 2, p_a)
    weigh(tiles - 1, p_b)
    pool(tiles - 1, p_b)

    def line(parts):
        return jnp.concatenate(parts, axis=1)

    return (
        line(tops) * scale,
        line([jnp.sum(mass[g], axis=0, keepdims=True) for g in groups]),
        line([jnp.sum(score_sum[g], axis=0, keepdims=True) for g in groups]) * scale,
    )


def stats_lines(stats):
    lines = [part for value in stats for part in split_float(value)]
    lines.append(jnp.zeros((META - len(lines), stats[0].shape[1]), F32))
    return jnp.concatenate(lines, axis=0).astype(BF16)


def bound_lines(meta, shift, n_docs):
    meta = meta.astype(F32)

    def bound(k):
        value = meta[2 * k : 2 * k + 1, :] * 256.0 + meta[2 * k + 1 : 2 * k + 2, :]
        return jnp.clip(value.astype(jnp.int32) - shift, 0, n_docs)

    lows = [bound(w) for w in range(2)]
    return lows, [jnp.maximum(bound(2 + w) - low, 0) for w, low in enumerate(lows)]


def own_kernel(shift, message, corpus, out, docs, arrived, *scratch):
    rows_q = scratch[0]
    copies = part_copies(corpus, docs, arrived, scratch[6].shape[0])
    for copy in copies.values():
        copy.start()
    queries = message.shape[0] - META
    lows, lengths = bound_lines(message[queries:, 0:queries], shift[0], docs.shape[0])
    set_bounds(scratch, jnp.concatenate(lows, axis=1), jnp.concatenate(lengths, axis=1))
    for w in range(2):
        rows_q[w * queries : (w + 1) * queries, :] = message[0:queries, :]
    stats = attend_rows(docs, scratch, 0, copies)
    out[0 : 2 * queries, :] = scratch[-1][...].astype(BF16)
    out[2 * queries :, :] = jnp.zeros((META, out.shape[1]), BF16)
    out[2 * queries :, 0 : 2 * queries] = stats_lines(stats)


def own(shift, message, corpus):
    docs, width = corpus.shape
    queries = message.shape[0] - META
    tile = min(DOC_TILE, docs // 2)
    return pl.pallas_call(
        own_kernel,
        out_shape=jax.ShapeDtypeStruct((2 * queries + META, width), BF16),
        in_specs=[SMEM, VMEM, HBM],
        out_specs=VMEM,
        scratch_shapes=[pltpu.VMEM((docs, width), BF16), pltpu.SemaphoreType.DMA((3,))]
        + row_scratch(2 * queries, docs, width, tile),
        compiler_params=params(44),
        cost_estimate=pl.CostEstimate(
            flops=8 * queries * docs * width,
            bytes_accessed=docs * width * 2,
            transcendentals=2 * queries * docs,
        ),
        name="own_block",
    )(shift, message, corpus)


def neighbour_kernel(shifts, near, far, corpus, near_out, far_out, docs, arrived, both_q, pooled, *scratch):
    rows_q = scratch[0]
    copies = part_copies(corpus, docs, arrived, scratch[6].shape[0])
    for copy in copies.values():
        copy.start()
    queries = near.shape[0] - META
    n_docs = docs.shape[0]
    held = rows_q.shape[0]
    centre = held // 2
    both_q[0:queries, :] = near[0:queries, :]
    both_q[queries:, :] = far[0:queries, :]
    metas = (near[queries:, 0:queries], far[queries:, 0:queries])
    lows, lengths = [], []
    for side, meta in enumerate(metas):
        low, length = bound_lines(meta, shifts[side], n_docs)
        lows += low
        lengths += length
    blocks = len(lows)
    rows = blocks * queries

    keys = [
        jnp.where(length > 0, jnp.where(low == 0, length, n_docs + low), 2 * n_docs)
        for low, length in zip(lows, lengths)
    ]
    parts = []
    for low, length, key in zip(lows, lengths, keys):
        lines = [*split_int(low), *split_int(length), *split_int(key), jnp.zeros((META - 6, queries), F32)]
        parts.append(jnp.concatenate(lines, axis=0).astype(BF16))
    unit = identity(queries)
    lane = lax.broadcasted_iota(jnp.int32, (1, queries), 1)
    line = lax.broadcasted_iota(jnp.int32, (queries, 1), 0)
    ordered = [keys[b] * rows + (lane + b * queries) for b in range(blocks)]
    ranks = [jnp.zeros((1, queries), F32)] * blocks
    for a in range(blocks):
        columns = lax.dot_general(unit, parts[a], NT, preferred_element_type=F32)
        key = (columns[:, 4:5] * 256.0 + columns[:, 5:6]).astype(jnp.int32)
        key = jnp.broadcast_to(key * rows + (line + a * queries), (queries, queries))
        for b in range(blocks):
            ranks[b] = ranks[b] + jnp.sum((key < ordered[b]).astype(F32), axis=0, keepdims=True)
    opened = jnp.zeros((1, 1), F32)
    for low, length in zip(lows, lengths):
        opened = opened + jnp.sum(((length > 0) & (low == 0)).astype(F32), axis=1, keepdims=True)
    places, misfits = [], jnp.zeros((1, 1), F32)
    half = n_docs // 2
    for low, length, rank in zip(lows, lengths, ranks):
        place = (rank + (centre - opened)).astype(jnp.int32)
        bad = (place < 0) | (place >= held)
        bad = bad | ((place < LANES) & (low + length > half)) | ((place >= 2 * LANES) & (low < half))
        misfits = misfits + jnp.sum(((length > 0) & bad).astype(F32), axis=1, keepdims=True)
        places.append(jnp.where(length > 0, place, -1))
    fits = jnp.max(misfits) == 0.0
    passes = jnp.where(fits, 1, 2)
    step = jnp.where(fits, held // LANES - 2, 0)

    near_out[...] = jnp.zeros(near_out.shape, BF16)
    far_out[...] = jnp.zeros(far_out.shape, BF16)

    def work(turn, carry):
        row = lax.broadcasted_iota(jnp.int32, (held, queries), 0)
        pick = []
        for b in range(blocks):
            plain = jnp.where(turn == b // 2, lane + (b % 2) * queries, -1)
            place = jnp.where(fits, places[b], plain)
            pick.append((row == place).astype(F32).astype(BF16))
        of_query = jnp.concatenate([pick[0] + pick[1], pick[2] + pick[3]], axis=1)
        rows_q[...] = jnp.dot(of_query, both_q[...], preferred_element_type=F32).astype(BF16)
        lines = sum(
            lax.dot_general(part, chosen, NT, preferred_element_type=F32) for part, chosen in zip(parts, pick)
        )
        set_bounds(
            scratch,
            (lines[0:1, :] * 256.0 + lines[1:2, :]).astype(jnp.int32),
            (lines[2:3, :] * 256.0 + lines[3:4, :]).astype(jnp.int32),
        )
        stats = stats_lines(attend_rows(docs, scratch, step, copies))
        pooled[...] = scratch[-1][...].astype(BF16)
        for b, chosen in enumerate(pick):
            out = (near_out, far_out)[b // 2]
            at = slice((b % 2) * queries, (b % 2 + 1) * queries)
            out[at, :] += lax.dot_general(chosen, pooled[...], TN, preferred_element_type=F32).astype(BF16)
            out[2 * queries :, at] += jnp.dot(stats, chosen, preferred_element_type=F32).astype(BF16)

        @pl.when(turn + 1 < passes)
        def _():
            for copy in copies.values():
                copy.start()

        return carry

    lax.fori_loop(0, passes, work, 0)


def neighbours(shifts, near, far, corpus):
    docs, width = corpus.shape
    queries = near.shape[0] - META
    held = 3 * LANES
    tile = min(DOC_TILE, docs // 2)
    result = jax.ShapeDtypeStruct((2 * queries + META, width), BF16)
    return pl.pallas_call(
        neighbour_kernel,
        out_shape=(result, result),
        in_specs=[SMEM, VMEM, VMEM, HBM],
        out_specs=(VMEM, VMEM),
        scratch_shapes=[
            pltpu.VMEM((docs, width), BF16),
            pltpu.SemaphoreType.DMA((3,)),
            pltpu.VMEM((2 * queries, width), BF16),
            pltpu.VMEM((held, width), BF16),
        ]
        + row_scratch(held, docs, width, tile),
        compiler_params=params(44),
        cost_estimate=pl.CostEstimate(
            flops=8 * queries * docs * width,
            bytes_accessed=docs * width * 2,
            transcendentals=2 * queries * docs,
        ),
        name="neighbour_blocks",
    )(shifts, near, far, corpus)


def pack_kernel(base, queries, starts, ends, out):
    rows, width = queries.shape
    out[0:rows, :] = queries[...]
    out[rows:, :] = jnp.zeros((META, width), BF16)
    parts = [split_int(lines[...] - base[0]) for lines in (starts, ends)]
    lines = [part[w : w + 1, :] for pair in parts for w in range(2) for part in pair]
    lines.append(jnp.zeros((META - 8, rows), F32))
    out[rows:, 0:rows] = jnp.concatenate(lines, axis=0).astype(BF16)


def pack(base, queries, starts, ends):
    rows, width = queries.shape
    return pl.pallas_call(
        pack_kernel,
        out_shape=jax.ShapeDtypeStruct((rows + META, width), BF16),
        in_specs=[SMEM, VMEM, VMEM, VMEM],
        out_specs=VMEM,
        name="pack",
    )(base, queries, starts, ends)


def columns_of(state, unit, w):
    queries = unit.shape[0]
    lines = state[2 * queries :, w * queries : (w + 1) * queries]
    columns = lax.dot_general(unit, lines, NT, preferred_element_type=F32)
    top, total, score_sum = (
        columns[:, 3 * k : 3 * k + 1] + columns[:, 3 * k + 1 : 3 * k + 2] + columns[:, 3 * k + 2 : 3 * k + 3]
        for k in range(3)
    )
    return jnp.where(total > 0, top, NEG), total, score_sum


def weigh_states(tops):
    best = functools.reduce(jnp.maximum, tops)
    return best, [jnp.exp(top - best) for top in tops]


def stats_matrix(stats):
    rows = stats[0].shape[0]
    lane = lax.broadcasted_iota(jnp.int32, (rows, META), 1)
    matrix = jnp.zeros((rows, META), F32)
    for k, value in enumerate(stats):
        for j, part in enumerate(split_float(value)):
            matrix = jnp.where(lane == 3 * k + j, part, matrix)
    return matrix.astype(BF16)


def merge_kernel(first, second, out):
    queries = (first.shape[0] - META) // 2
    unit = identity(queries)
    out[2 * queries :, :] = jnp.zeros((META, out.shape[1]), BF16)
    for w in range(2):
        at = slice(w * queries, (w + 1) * queries)
        states = [columns_of(state, unit, w) for state in (first, second)]
        best, factors = weigh_states([state[0] for state in states])
        total = functools.reduce(jnp.add, [f * state[1] for f, state in zip(factors, states)])
        score_sum = states[0][2] + states[1][2]
        out[at, :] = (
            factors[0] * first[at, :].astype(F32) + factors[1] * second[at, :].astype(F32)
        ).astype(BF16)
        stats = stats_matrix((best, total, score_sum))
        out[2 * queries :, at] = lax.dot_general(
            stats, unit, TN, preferred_element_type=F32
        ).astype(BF16)


def merge(first, second):
    return pl.pallas_call(
        merge_kernel,
        out_shape=jax.ShapeDtypeStruct(first.shape, BF16),
        in_specs=[VMEM, VMEM],
        out_specs=VMEM,
        compiler_params=params(8),
        name="merge",
    )(first, second)


def finish_kernel(window_start, window_end, first, second, third, pooled, log_mass, mean_score):
    queries = window_start.shape[1]
    unit = identity(queries)
    members = (first, second, third)
    means = []
    for w in range(2):
        at = slice(w * queries, (w + 1) * queries)
        states = [columns_of(member, unit, w) for member in members]
        _, factors = weigh_states([state[0] for state in states])
        total = functools.reduce(jnp.add, [f * state[1] for f, state in zip(factors, states)])
        weighted = functools.reduce(
            jnp.add, [f * member[at, :].astype(F32) for f, member in zip(factors, members)]
        )
        means.append(weighted / total)

        lines = [member[2 * queries :, at].astype(F32) for member in members]
        tops, totals, sums = (
            [line[3 * k : 3 * k + 1, :] + line[3 * k + 1 : 3 * k + 2, :] + line[3 * k + 2 : 3 * k + 3, :] for line in lines]
            for k in range(3)
        )
        best, factors = weigh_states([jnp.where(t > 0, top, NEG) for top, t in zip(tops, totals)])
        total = functools.reduce(jnp.add, [f * t for f, t in zip(factors, totals)])
        log_mass[w : w + 1, :] = best + jnp.log(total)
        count = (window_end[w : w + 1, :] - window_start[w : w + 1, :]).astype(F32)
        mean_score[w : w + 1, :] = functools.reduce(jnp.add, sums) / count
    pooled[...] = jnp.stack(means, axis=1).astype(BF16)


def finish(window_start, window_end, *members):
    queries = window_start.shape[1]
    width = members[0].shape[1]
    line = jax.ShapeDtypeStruct((2, queries), F32)
    return pl.pallas_call(
        finish_kernel,
        out_shape=(jax.ShapeDtypeStruct((queries, 2, width), BF16), line, line),
        in_specs=[VMEM] * 5,
        out_specs=(VMEM, VMEM, VMEM),
        compiler_params=params(8),
        name="finish",
    )(window_start, window_end, *members)


def local(queries, corpus, window_start, window_end):
    docs = corpus.shape[0]
    size = lax.axis_size(AXES)
    position = lax.axis_index(AXES)
    across = [(i, i ^ 1) for i in range(size)]
    between = [(i, i + 1) for i in range(3, size - 1, 4)] + [(i + 1, i) for i in range(3, size - 1, 4)]
    past = [(i, i + 1) for i in range(1, size - 1, 2)] + [(i + 1, i) for i in range(1, size - 1, 2)]
    relay = [(i + 2, i) for i in range(0, size, 4)] + [(i + 1, i + 3) for i in range(0, size, 4)]
    odd = position % 2

    starts, ends = window_start.T, window_end.T
    base = jnp.full((1,), (position - 1) * docs, jnp.int32)
    message = pack(base, queries, starts, ends)
    near = lax.ppermute(message, AXES, across)
    far = lax.ppermute(message, AXES, past)
    shifts = jnp.stack([2 * docs * odd, 2 * docs * (1 - odd)]).astype(jnp.int32)
    near_part, far_part = neighbours(shifts, near, far, corpus)
    far_back = lax.ppermute(far_part, AXES, between)
    relayed = lax.ppermute(far_part, AXES, relay)
    near_back = lax.ppermute(merge(near_part, relayed), AXES, across)
    message, _ = lax.optimization_barrier((message, far_part))
    own_part = own(jnp.full((1,), docs, jnp.int32), message, corpus)
    pooled, log_mass, mean_score = finish(starts, ends, own_part, near_back, far_back)
    return pooled, log_mass.T, mean_score.T


def solution(mesh):
    placed = P(AXES, None)
    return jax.shard_map(
        local,
        mesh=mesh,
        in_specs=(placed,) * 4,
        out_specs=(P(AXES, None, None), placed, placed),
        check_vma=False,
    )
```
